32 devices in a mesh: groups: 2 (over y), leaf: 4 (over z), level: 2 (over x), sub: 2 (over core).
Axes of the slice: x: 2, y: 2, z: 4, core: 2. Of those that a mesh axis runs over, the one named last changes fastest.
Arguments:
- rhs: float32 [64, 262144], P(('level', 'sub'), ('groups', 'leaf')), parts along dimension 1, may hold values from -6 to 6
- points: float32 [3, 262144], P(None, ('groups', 'leaf')), parts along dimension 1, may hold values from 0 to 2
- basis: float32 [32, 262144], P(None, ('groups', 'leaf')), parts along dimension 1, may hold values from -0.75 to 0.75
- transfer: float32 [32, 261632], P(None, ('groups', 'leaf')), parts along dimension 1, may hold values from -0.875 to 0.875
- leaf_proxies: float32 [3, 131072], P(None, ('groups', 'leaf')), parts along dimension 1, may hold values from 0 to 2
- root_proxies: float32 [3, 256], P(None, 'groups'), parts along dimension 1, may hold values from 0 to 2
- near_src: int32 [4096, 8], P(('groups', 'leaf')), parts along dimension 0, may hold values from 0 to 2047, as said below
- near_count: int32 [4096], P(('groups', 'leaf')), parts along dimension 0, may hold values from 1 to 8, as said below
- far_src: int32 [4096, 16], P(('groups', 'leaf')), parts along dimension 0, may hold values from 0 to 2047, as said below
Outputs:
- product: float32 [64, 262144], P(('level', 'sub'), ('groups', 'leaf')), parts along dimension 1
The draws below stay inside these ranges and needn't reach their ends.
There are 2 independent parts, one for each index of `groups`. The reference program is written for one: setup_inputs(seed, part) draws one part's arguments, and reference() takes and returns one part's arrays. A program takes and returns all parts, laid end to end along the dimension named above; each array names one. Nothing has to cross between parts.
Inputs may be any that keep to these rules, and one draw needn't show every extreme that they name: `near_src`: each entry of row t lies within 512 of t; in every draw some row names t + 512 and some row t - 512; entries may repeat. Entries 0 to near_count[t] - 1 of row t of near_src are live, the rest are ignored; some leaf has 8. `far_src`: each entry of row t lies within 512 of t; in every draw some row names t + 512 and some row t - 512; entries may repeat.
All inputs are finite; a program needn't handle non-finite values.
Results may differ from the reference program's by a relative error of at most 0.00017.
Values sent between devices are 32-bit elements; how exact they have to be, the bound alone decides.
No kernel may reach another device: no remote copies, remote signals or barrier semaphores. Data moves between devices by JAX's collectives and lax.ppermute only.
A program may use at most 192 MiB of HBM per device.

```python
import jax
import jax.numpy as jnp
from jax import lax

LEAVES_DEV = 512
RHS = 64
RANK = 32
LEAF_PTS = 64
NEAR_MAX = 8
FAR_MAX = 16
LEAVES = 2048
NPTS = 131072
CHILD = 1022
N_LEAF = 4


def reach_table(key, columns):
    first_key, second_key = jax.random.split(key)
    reach = LEAVES_DEV
    leaf_ids = jnp.arange(LEAVES, dtype=jnp.int32)[:, None]
    offset = jax.random.randint(first_key, (LEAVES, columns), -reach, reach + 1, dtype=jnp.int32)
    table = jnp.clip(leaf_ids + offset, 0, LEAVES - 1)
    span = LEAVES - 2 * reach
    upper = reach + jax.random.randint(second_key, (), 0, span, dtype=jnp.int32)
    lower = reach + (upper - reach + 1) % span
    table = table.at[upper, 0].set(upper + reach)
    table = table.at[lower, 0].set(lower - reach)
    return table.astype(jnp.int32)


def draw_near_src(key, part):
    key = jax.random.fold_in(key, 11)
    return reach_table(key, NEAR_MAX)


def draw_far_src(key, part):
    key = jax.random.fold_in(key, 12)
    return reach_table(key, FAR_MAX)


def draw_near_count(key, part):
    key = jax.random.fold_in(key, 13)
    cap_key, count_key, pick_key = jax.random.split(key, 3)
    owners = LEAVES // LEAVES_DEV
    caps = jax.random.randint(cap_key, (owners,), 1, NEAR_MAX + 1, dtype=jnp.int32)
    per_leaf = jnp.repeat(caps, LEAVES_DEV)
    counts = jax.random.randint(count_key, (LEAVES,), 1, per_leaf + 1, dtype=jnp.int32)
    chosen = jax.random.randint(pick_key, (), 0, LEAVES, dtype=jnp.int32)
    return counts.at[chosen].set(NEAR_MAX).astype(jnp.int32)


def block_scale(own_key, shape, pieces, least, largest):
    gain, own = 1.0, jax.random.fold_in(own_key, 6)
    for axis_at, blocks in pieces:
        heights = jnp.exp(jax.random.uniform(jax.random.fold_in(own, axis_at), (blocks,), jnp.float32, least / len(pieces), largest / len(pieces)))
        gain = gain * jnp.repeat(heights, shape[axis_at] // blocks).reshape([-1 if axis == axis_at else 1 for axis in range(len(shape))])
    return gain


def gaussian(rng, extent, deviation, bound, shards=(), held_as=jnp.bfloat16):
    drawn = jax.random.normal(rng, extent, jnp.float32) * deviation
    if len(shards) > 0:
        drawn = block_scale(rng, extent, shards, -0.22, 0.18) * drawn
    return jnp.clip(drawn, min=-bound, max=bound).astype(held_as)


def setup_inputs(seed: int = 0, part: int = 0) -> dict:
    key_of = jax.random.split(jax.random.key(seed), 10)
    own_keys = jax.random.split(jax.random.fold_in(key_of[9], part), 10)
    return {
        "rhs": gaussian(own_keys[0], (RHS, NPTS), 1.0, 6.0, ((0, 4), (1, 4)), jnp.float32),
        "points": jnp.clip(2.0 * jax.random.uniform(own_keys[1], (3, NPTS), jnp.float32) ** block_scale(own_keys[1], (3, NPTS), ((1, 4),), -0.2, 0.2), 0.0, 2.0),
        "basis": gaussian(own_keys[2], (RANK, NPTS), LEAF_PTS ** -0.5, 0.75, ((1, 4),), jnp.float32),
        "transfer": gaussian(own_keys[3], (RANK, RANK * CHILD * N_LEAF), (RANK * 3 // 2) ** -0.5, 0.875, ((1, 4),), jnp.float32),
        "leaf_proxies": jnp.clip(2.0 * jax.random.uniform(own_keys[4], (3, LEAVES * RANK), jnp.float32) ** block_scale(own_keys[4], (3, LEAVES * RANK), ((1, 4),), -0.2, 0.2), 0.0, 2.0),
        "root_proxies": jnp.clip(jax.random.uniform(own_keys[5], (3, N_LEAF * RANK), jnp.float32, 0.0, 2.0), 0.0, 2.0),
        "near_src": draw_near_src(jax.random.fold_in(jax.random.fold_in(key_of[9], part), 71), part),
        "near_count": draw_near_count(jax.random.fold_in(jax.random.fold_in(key_of[9], part), 71), part),
        "far_src": draw_far_src(jax.random.fold_in(jax.random.fold_in(key_of[9], part), 71), part),
    }


spread_sq = 0.5


def pair_rows(src_x, src_c, tgt_c, src_idx, live):
    rows = src_x.shape[0]
    count = tgt_c.shape[1]
    width = tgt_c.shape[2]
    listed = src_idx.shape[1]
    step = min(16, count)
    blocks = count // step
    tgt_blocks = jnp.moveaxis(tgt_c.reshape(3, blocks, step, width), 1, 0)
    idx_blocks = src_idx.reshape(blocks, step, listed)
    live_blocks = live.reshape(blocks, step, listed)

    def one_block(packed):
        tgt_here, idx_here, live_here = packed
        src_here = src_c[:, idx_here].reshape(3, step, listed * width)
        dist = (tgt_here[0][:, :, None] - src_here[0][:, None, :]) ** 2
        dist = dist + (tgt_here[1][:, :, None] - src_here[1][:, None, :]) ** 2
        dist = dist + (tgt_here[2][:, :, None] - src_here[2][:, None, :]) ** 2
        weight = jnp.repeat(live_here, width, axis=1)[:, None, :]
        kernel = jnp.exp(-dist / spread_sq) * weight
        values = src_x[:, idx_here].reshape(rows, step, listed * width)
        return jnp.einsum("bij,rbj->rbi", kernel, values, precision=lax.Precision.HIGHEST)

    result = lax.map(one_block, (tgt_blocks, idx_blocks, live_blocks))
    return jnp.moveaxis(result, 0, 1).reshape(rows, count * width)


def reference(rhs, points, basis, transfer, leaf_proxies, root_proxies, near_src, near_count, far_src):
    highest = lax.Precision.HIGHEST
    owners = LEAVES // LEAVES_DEV
    levels = LEAVES_DEV.bit_length() - 1
    rhs3 = rhs.reshape(RHS, LEAVES, LEAF_PTS)
    coords3 = points.reshape(3, LEAVES, LEAF_PTS)
    basis3 = basis.reshape(RANK, LEAVES, LEAF_PTS)
    live = (jnp.arange(NEAR_MAX, dtype=jnp.int32)[None, :] < near_count[:, None]).astype(jnp.float32)
    near = pair_rows(rhs3, coords3, coords3, near_src, live)
    coef = jnp.einsum("rlp,alp->rla", rhs3, basis3, precision=highest)
    proxy3 = leaf_proxies.reshape(3, LEAVES, RANK)
    all_live = jnp.ones((LEAVES, FAR_MAX), jnp.float32)
    couple = pair_rows(coef, proxy3, proxy3, far_src, all_live).reshape(RHS, LEAVES, RANK)
    blocks = transfer.reshape(RANK, owners, CHILD, RANK)
    mats = []
    current = coef
    for level in range(levels):
        here = LEAVES_DEV >> level
        offset = 2 * LEAVES_DEV - 2 * here
        mat = blocks[:, :, offset:offset + here, :].reshape(RANK, owners * here, RANK)
        mats.append(mat)
        lifted = jnp.einsum("rca,acb->rcb", current, mat, precision=highest)
        current = lifted.reshape(RHS, owners * here // 2, 2, RANK).sum(axis=2)
    roots = current.reshape(RHS, owners * RANK)
    dist = (root_proxies[0][:, None] - root_proxies[0][None, :]) ** 2
    dist = dist + (root_proxies[1][:, None] - root_proxies[1][None, :]) ** 2
    dist = dist + (root_proxies[2][:, None] - root_proxies[2][None, :]) ** 2
    owner_of = jnp.arange(owners * RANK, dtype=jnp.int32) // RANK
    far_mask = (jnp.abs(owner_of[:, None] - owner_of[None, :]) >= 2).astype(jnp.float32)
    kernel = jnp.exp(-dist / spread_sq) * far_mask
    down = jnp.einsum("ij,rj->ri", kernel, roots, precision=highest).reshape(RHS, owners, RANK)
    for level in reversed(range(levels)):
        down = jnp.einsum("rcb,acb->rca", jnp.repeat(down, 2, axis=1), mats[level], precision=highest)
    down = down + couple
    far = jnp.einsum("rla,alp->rlp", down, basis3, precision=highest).reshape(RHS, NPTS)
    return near + far
```

```python
import functools
import math

import jax
import jax.numpy as jnp
import numpy as np
from jax import lax
from jax.experimental import pallas as pl
from jax.experimental.pallas import tpu as pltpu
from jax.sharding import PartitionSpec as P

spread_sq = 0.5
LANES = 128
FEATS = 16
UNROLL = 32
WIDE = 2
VMEM_LIMIT = 58 * 1024 * 1024
f32, bf16, i32 = jnp.float32, jnp.bfloat16, jnp.int32

NN = (((1,), (0,)), ((), ()))
NT = (((1,), (1,)), ((), ()))


def dot(a, b, dims=NN):
    return lax.dot_general(a, b, dims, preferred_element_type=f32)


def halves(x):
    hi = x.astype(bf16).astype(f32)
    return hi, x - hi


def stacked(x):
    hi, lo = halves(x)
    return jnp.concatenate([hi, lo], axis=0).astype(bf16)


def two_term(x, terms, dims):
    rows = x.shape[0]
    xs = stacked(x)
    high = dot(xs, terms[0], dims)
    low = dot(xs, terms[1], dims)
    return (high[:rows] + high[rows:]) + (low[:rows] + low[rows:])


def in_chunks(count, most, run):
    size = min(count, most)
    if count == size:
        run(0, size)
    else:

        def step(i, carry):
            run(i * size, size)
            return carry

        lax.fori_loop(0, count // size, step, 0)


def at(i, size):
    first = i * size
    return pl.ds(first if isinstance(first, int) else pl.multiple_of(first, size), size)


def span_of(first, n):
    start = first * LANES
    return pl.ds(start if isinstance(start, int) else pl.multiple_of(start, LANES), n * LANES)


def group_mask(shape, row_width, col_width):
    row = lax.broadcasted_iota(i32, shape, 0) // row_width
    col = lax.broadcasted_iota(i32, shape, 1) // col_width
    return row == col


def spread_rows(mat, copies, mask):
    zero = jnp.zeros((), bf16)
    parts = [part.astype(bf16) for part in halves(mat)]
    return [jnp.where(mask, jnp.concatenate([part] * copies, axis=0), zero) for part in parts]


def whole(n):
    return [pl.BlockSpec(memory_space=pltpu.VMEM)] * n


def call(body, out_shape, n_in, scratch=(), flops=0, nbytes=0, prefetch=False):
    specs = ([pl.BlockSpec(memory_space=pltpu.SMEM)] if prefetch else []) + whole(n_in)
    return pl.pallas_call(
        body,
        out_shape=out_shape,
        in_specs=specs,
        out_specs=pl.BlockSpec(memory_space=pltpu.VMEM),
        scratch_shapes=list(scratch),
        compiler_params=pltpu.CompilerParams(vmem_limit_bytes=VMEM_LIMIT),
        cost_estimate=pl.CostEstimate(flops=flops, bytes_accessed=nbytes, transcendentals=0),
    )


def leaf_coefs(rhs, basis, leaf_pts):
    rows, width = rhs.shape
    rank = basis.shape[0]
    per = LANES // rank
    span = per * leaf_pts

    def body(x_ref, b_ref, o_ref):
        mask = group_mask((per * rank, span), rank, leaf_pts)

        def run(first, n):
            ids = [first + j for j in range(n)]
            ins = [(x_ref[:, at(i, span)], b_ref[:, at(i, span)]) for i in ids]
            outs = [two_term(x, spread_rows(m, per, mask), NT) for x, m in ins]
            for i, out in zip(ids, outs):
                o_ref[:, at(i, LANES)] = out

        in_chunks(width // span, 8, run)

    out = jax.ShapeDtypeStruct((rows, width // leaf_pts * rank), f32)
    return call(body, out, 2, flops=10**9, nbytes=4 * width * (rows + rank))(rhs, basis)


def leaf_product(down, couple, basis, near, leaf_pts):
    rows, width = near.shape
    rank = basis.shape[0]
    per = LANES // rank
    span = per * leaf_pts

    def body(d_ref, c_ref, b_ref, n_ref, o_ref):
        mask = group_mask((per * rank, span), rank, leaf_pts)

        def run(first, n):
            ids = [first + j for j in range(n)]
            ins = [
                (d_ref[:, at(i, LANES)] + c_ref[:, at(i, LANES)], b_ref[:, at(i, span)]) for i in ids
            ]
            outs = [two_term(x, spread_rows(m, per, mask), NN) for x, m in ins]
            for i, out in zip(ids, outs):
                o_ref[:, at(i, span)] = n_ref[:, at(i, span)] + out

        in_chunks(width // span, 8, run)

    out = jax.ShapeDtypeStruct((rows, width), f32)
    return call(body, out, 4, flops=10**9, nbytes=4 * width * (3 * rows + rank))(
        down, couple, basis, near
    )


def tree_up(coef, transfer, leaves):
    rows, width = coef.shape
    rank = transfer.shape[0]
    levels = leaves.bit_length() - 1

    def body(c_ref, e_ref, o_ref, buf):
        for level in range(levels):
            here = leaves >> level
            offset = (2 * leaves - 2 * here) * rank
            share = 1 if level == 0 else 2
            out_span = min(LANES, here * rank)
            groups = out_span // rank * share
            span = groups * rank
            mask = group_mask((span, out_span), share * rank, rank)
            src = c_ref if level == 0 else buf.at[(level - 1) % 2]
            dst = buf.at[level % 2]

            def run(first, n):
                ids = [first + j for j in range(n)]
                base = offset // out_span
                ins = [(src[:, at(i, span)], e_ref[:, at(base + i, out_span)]) for i in ids]
                outs = [two_term(x, spread_rows(m, groups, mask), NN) for x, m in ins]
                for i, out in zip(ids, outs):
                    dst[:, at(i, out_span)] = out

            in_chunks(here * rank // out_span, 8, run)
        last = buf[(levels - 1) % 2, :, : 2 * rank]
        o_ref[...] = last[:, :rank] + last[:, rank:]

    return call(
        body,
        jax.ShapeDtypeStruct((rows, rank), f32),
        2,
        [pltpu.VMEM((2, rows, width), f32)],
        flops=10**9,
        nbytes=4 * width * (rows + 2 * rank),
    )(coef, transfer)


def tree_down(root, transfer, leaves):
    rows = root.shape[0]
    rank = transfer.shape[0]
    levels = leaves.bit_length() - 1
    width = leaves * rank

    def body(r_ref, e_ref, o_ref, buf):
        top = r_ref[...]
        buf[levels % 2, :, : 2 * rank] = jnp.concatenate([top, top], axis=1)
        for level in reversed(range(levels)):
            here = leaves >> level
            offset = (2 * leaves - 2 * here) * rank
            share = 1 if level == 0 else 2
            in_span = min(LANES, here * rank)
            groups = in_span // rank * share
            span = groups * rank
            mask = group_mask((span, in_span), share * rank, rank)
            src = buf.at[(level + 1) % 2]
            dst = o_ref if level == 0 else buf.at[level % 2]

            def run(first, n):
                ids = [first + j for j in range(n)]
                base = offset // in_span
                ins = [(src[:, at(i, in_span)], e_ref[:, at(base + i, in_span)]) for i in ids]
                outs = [two_term(x, spread_rows(m, groups, mask), NT) for x, m in ins]
                for i, out in zip(ids, outs):
                    dst[:, at(i, span)] = out

            in_chunks(here * rank // in_span, 8, run)

    return call(
        body,
        jax.ShapeDtypeStruct((rows, width), f32),
        2,
        [pltpu.VMEM((2, rows, width), f32)],
        flops=10**9,
        nbytes=4 * width * (rows + 2 * rank),
    )(root, transfer)


LOG2E = math.log2(math.e)


def selections():
    source, target = np.zeros((FEATS, FEATS), np.float32), np.zeros((FEATS, FEATS), np.float32)
    for d in range(3):
        for row, (p, q) in enumerate(((0, 0), (0, 1), (1, 0), (1, 1))):
            target[3 * row + d, 8 * p + d] = 1.0
            source[3 * row + d, 8 * q + d] = 1.0
    for row, term in ((12, 3), (13, 11)):
        source[row, term] = 1.0
        target[row, 4] = 1.0
        target[row + 2, term] = 1.0
        source[row + 2, 4] = 1.0
    return source, target


def features(coords, selection, scale):
    c = coords - 1.0
    row = lax.broadcasted_iota(i32, c.shape, 0)
    square = (-LOG2E / spread_sq) * jnp.sum(c * c, axis=0, keepdims=True)
    terms = jnp.where(row == 3, square, jnp.where(row == 4, 1.0, c * scale))
    return dot(selection, stacked(terms))


def eight_rows(coords):
    return jnp.pad(coords, ((0, 5), (0, 0)), constant_values=1.0)


def work_list(idx, live, group, dummy):
    count, listed = idx.shape
    items = count * (listed // group)
    livei = live.astype(i32)
    rank = jnp.sum(
        livei[:, None, :] * (jnp.arange(listed)[None, None, :] < jnp.arange(listed)[None, :, None]),
        axis=2,
    )
    slot = jnp.arange(listed, dtype=i32)
    hit = live[:, :, None] & (rank[:, :, None] == slot[None, None, :])
    total = jnp.sum(livei, axis=1)
    packed = jnp.sum(jnp.where(hit, idx[:, :, None], 0), axis=1)
    packed = jnp.where(slot[None, :] < total[:, None], packed, dummy)
    need = (total + group - 1) // group
    upto = jnp.arange(count)
    start = jnp.sum(jnp.where(upto[None, :] < upto[:, None], need[None, :], 0), axis=1)
    end = start + need
    k = jnp.arange(items, dtype=i32)
    one_hot = (start[None, :] <= k[:, None]) & (k[:, None] < end[None, :])
    target = jnp.sum(jnp.where(one_hot, upto[None, :].astype(i32), 0), axis=1)
    within = jnp.sum(jnp.where(one_hot, k[:, None] - start[None, :], 0), axis=1)
    rows = jnp.einsum(
        "kt,tm->km", one_hot.astype(f32), packed.astype(f32), precision=lax.Precision.HIGHEST
    )
    rows = jnp.round(rows).astype(i32).reshape(items, listed // group, group)
    pick = within[:, None, None] == jnp.arange(listed // group)[None, :, None]
    sources = jnp.sum(jnp.where(pick, rows, 0), axis=1)
    used = jnp.sum(need)
    sources = jnp.where((k < used)[:, None], sources, dummy)
    steps = (used + UNROLL - 1) // UNROLL
    return jnp.concatenate([target, sources.T.reshape(-1), steps[None]]), items


def pair_sums(listing, items, place, coords, sources, before, leaves, pts):
    rows = sources[0].shape[0]
    width = leaves * pts
    per = LANES // pts
    pieces = len(sources)
    held = pieces * leaves
    group = WIDE * per
    narrow = per > 2
    pick_source, pick_target = selections()
    eye = np.eye(LANES, dtype=np.float32)
    consts = [jnp.asarray(m, bf16) for m in (pick_source, pick_target, eye)]

    def body(list_ref, pick_s_ref, pick_t_ref, eye_ref, place_ref, *refs):
        coord_refs = refs[:pieces]
        x_refs = refs[pieces : 2 * pieces]
        more = refs[2 * pieces :]
        base_ref = more[0] if before is not None else None
        o_ref, tab, targets_tab, acc = more[-4:]
        lane = lax.broadcasted_iota(i32, (1, LANES), 1) // pts

        def fill_targets(first, n):
            here = span_of(first, n)
            feats = features(place_ref[:, here], pick_t_ref[...], 2.0 * LOG2E / spread_sq).astype(bf16)
            outs = [
                dot(eye_ref[...], feats[:, j * LANES : (j + 1) * LANES], NT).astype(bf16)
                for j in range(n)
            ]
            for j, out in enumerate(outs):
                for g in range(per):
                    targets_tab[(first + j) * per + g] = out[g * pts : (g + 1) * pts]

        in_chunks(width // LANES, 32, fill_targets)

        for piece in range(pieces):

            def fill(first, n):
                here = span_of(first, n)
                feats = features(coord_refs[piece][:, here], pick_s_ref[...], 1.0)
                hi, lo = halves(x_refs[piece][:, here])
                whole_rec = jnp.concatenate([feats, hi, lo], axis=0)
                outs = []
                for c in range(n):
                    rec = whole_rec[:, c * LANES : (c + 1) * LANES]
                    turned = [rec] + [pltpu.roll(rec, pts * j, 1) for j in range(1, per)]
                    for j in range(per):
                        out = turned[(per - j) % per]
                        for g in range(1, per):
                            out = jnp.where(lane == g, turned[(g - j) % per], out)
                        outs.append(out.astype(bf16))
                for j, out in enumerate(outs):
                    tab[piece * leaves + first * per + j] = out

            in_chunks(width // LANES, 16, fill)
        tab[held] = jnp.zeros(tab.shape[1:], bf16)

        def clear(first, n):
            for j in range(n):
                acc[first + j] = jnp.zeros(acc.shape[1:], f32)

        in_chunks(leaves, 32, clear)

        masks = [
            lax.broadcasted_iota(i32, (FEATS + 2 * rows, LANES), 1) >= g * pts
            for g in range(1, per)
        ]

        def step(n, carry):
            ks = [n * UNROLL + u for u in range(UNROLL)]
            targets = [list_ref[k] for k in ks]
            recs = []
            for k in ks:
                blocks = []
                for w in range(WIDE):
                    rec = tab[list_ref[(w * per + 1) * items + k]]
                    for g in range(1, per):
                        other = tab[list_ref[(w * per + g + 1) * items + k]]
                        rec = jnp.where(masks[g - 1], other, rec)
                    blocks.append(rec)
                recs.append(jnp.concatenate(blocks, axis=1))
            logs = [dot(targets_tab[t], rec[:FEATS]) for t, rec in zip(targets, recs)]
            kernels = [jnp.exp2(e) for e in logs]
            his = [k.astype(bf16) for k in kernels]
            los = [(k - h.astype(f32)).astype(bf16) for k, h in zip(kernels, his)]
            outs = []
            for rec, hi, lo in zip(recs, his, los):
                both = jnp.concatenate([hi, lo], axis=0)
                if narrow:
                    out = dot(both, rec[FEATS:], NT)
                    outs.append(out[:pts] + out[pts:])
                else:
                    out = dot(rec[FEATS:], both, NT)
                    outs.append(out[:rows] + out[rows:])
            for t, out in zip(targets, outs):
                acc[t] += out
            return carry

        lax.fori_loop(0, list_ref[(group + 1) * items], step, 0)

        def lay(start, n):
            outs = []
            for c in range(n):
                first = (start + c) * per
                if narrow:
                    out = jnp.concatenate([acc[first + j] for j in range(per)], axis=0).T
                    outs.append(out[:rows] + out[rows:])
                else:
                    for j in range(per):
                        one = acc[first + j]
                        one = one + pltpu.roll(one, pts, 1)
                        out = one if j == 0 else jnp.where(lane == j, one, out)
                    outs.append(out)
            for c, out in enumerate(outs):
                here = at(start + c, LANES)
                o_ref[:, here] = out if base_ref is None else out + base_ref[:, here]

        in_chunks(width // LANES, 16, lay)

    scratch = [
        pltpu.VMEM((held + 1, FEATS + 2 * rows, LANES), bf16),
        pltpu.VMEM((leaves, pts, FEATS), bf16),
        pltpu.VMEM((leaves, pts, 2 * rows) if narrow else (leaves, rows, LANES), f32),
    ]
    args = [listing, *consts, place, *coords, *sources] + ([before] if before is not None else [])
    return call(
        body,
        jax.ShapeDtypeStruct((rows, width), f32),
        len(args) - 1,
        scratch,
        flops=4 * 10**9,
        nbytes=3 * 10**7,
        prefetch=True,
    )(*args)


def local(rhs, points, basis, transfer, leaf_proxies, root_proxies, near_src, near_count, far_src):
    highest = lax.Precision.HIGHEST
    rows, width = rhs.shape
    leaves = near_src.shape[0]
    leaf_pts = width // leaves
    rank = basis.shape[0]
    near_max = near_src.shape[1]
    owner = lax.axis_index("leaf")
    size = lax.axis_size("leaf")
    up = [(i, (i + 1) % size) for i in range(size - 1)]
    down_pairs = [(j, i) for i, j in up]
    both_ways = lambda x: (lax.ppermute(x, "leaf", up), lax.ppermute(x, "leaf", down_pairs))

    shares = lax.axis_size("level") * lax.axis_size("sub")
    mine = lax.axis_index("level") * lax.axis_size("sub") + lax.axis_index("sub")
    near_share, far_share = width // shares, leaves * rank // shares
    share = jnp.concatenate(
        [
            lax.dynamic_slice_in_dim(points, mine * near_share, near_share, 1),
            lax.dynamic_slice_in_dim(leaf_proxies, mine * far_share, far_share, 1),
        ],
        axis=1,
    )
    share = jnp.stack(both_ways(share))
    coords = lax.all_gather(share, ("level", "sub"), axis=0)
    coords = jnp.moveaxis(coords, 0, 2)
    halo_points = coords[..., :near_share].reshape(2, 3, width)
    halo_proxies = coords[..., near_share:].reshape(2, 3, leaves * rank)

    coef = leaf_coefs(rhs, basis, leaf_pts)
    halo_rhs = both_ways(rhs)
    halo_coef = both_ways(coef)

    anchor = owner * leaves

    def lists(src, live, group):
        place = src - anchor
        own = (place >= 0) & (place < leaves)
        inside = work_list(place, live & own, group, leaves)
        outside = jnp.where(place < 0, place + leaves, place)
        return inside, work_list(outside, live & ~own, group, 2 * leaves)

    live = jnp.arange(near_max, dtype=i32)[None, :] < near_count[:, None]
    near_in, near_out = lists(near_src, live, WIDE * LANES // leaf_pts)
    far_in, far_out = lists(far_src, jnp.ones(far_src.shape, bool), WIDE * LANES // rank)

    own_points, own_proxies = eight_rows(points), eight_rows(leaf_proxies)
    near = pair_sums(*near_in, own_points, [own_points], [rhs], None, leaves, leaf_pts)
    couple = pair_sums(*far_in, own_proxies, [own_proxies], [coef], None, leaves, rank)

    root = tree_up(coef, transfer, leaves)
    own_proxy = lax.dynamic_slice_in_dim(root_proxies, owner * rank, rank, 1)
    piece = lax.all_gather(root, "leaf", axis=1, tiled=True)
    dist = (own_proxy[0][:, None] - root_proxies[0][None, :]) ** 2
    dist = dist + (own_proxy[1][:, None] - root_proxies[1][None, :]) ** 2
    dist = dist + (own_proxy[2][:, None] - root_proxies[2][None, :]) ** 2
    source_owner = jnp.arange(piece.shape[1], dtype=i32) // rank
    far_mask = (jnp.abs(source_owner - owner) >= 2).astype(f32)
    kernel = jnp.exp(-dist / spread_sq) * far_mask[None, :]
    top = jnp.einsum("aj,rj->ra", kernel, piece, precision=highest)
    down = tree_down(top, transfer, leaves)

    halo_points = [eight_rows(halo_points[i]) for i in range(2)]
    halo_proxies = [eight_rows(halo_proxies[i]) for i in range(2)]
    near = pair_sums(*near_out, own_points, halo_points, list(halo_rhs), near, leaves, leaf_pts)
    couple = pair_sums(
        *far_out, own_proxies, halo_proxies, list(halo_coef), couple, leaves, rank
    )
    return leaf_product(down, couple, basis, near, leaf_pts)


def solution(mesh):
    in_specs = (
        P(("level", "sub"), ("groups", "leaf")),
        P(None, ("groups", "leaf")),
        P(None, ("groups", "leaf")),
        P(None, ("groups", "leaf")),
        P(None, ("groups", "leaf")),
        P(None, "groups"),
        P(("groups", "leaf"), None),
        P(("groups", "leaf")),
        P(("groups", "leaf"), None),
    )
    out_specs = P(("level", "sub"), ("groups", "leaf"))
    return jax.shard_map(local, mesh=mesh, in_specs=in_specs, out_specs=out_specs, check_vma=False)
```

```python
import functools
import math

import jax
import jax.numpy as jnp
import numpy as np
from jax import lax
from jax.experimental import pallas as pl
from jax.experimental.pallas import tpu as pltpu
from jax.sharding import PartitionSpec as P

spread_sq = 0.5
LANES = 128
FEATS = 16
UNROLL = 32
WIDE = 2
VMEM_LIMIT = 58 * 1024 * 1024
f32, bf16, i32 = jnp.float32, jnp.bfloat16, jnp.int32

NN = (((1,), (0,)), ((), ()))
NT = (((1,), (1,)), ((), ()))


def dot(a, b, dims=NN):
    return lax.dot_general(a, b, dims, preferred_element_type=f32)


def halves(x):
    hi = x.astype(bf16).astype(f32)
    return hi, x - hi


def stacked(x):
    hi, lo = halves(x)
    return jnp.concatenate([hi, lo], axis=0).astype(bf16)


def two_term(x, terms, dims):
    rows = x.shape[0]
    xs = stacked(x)
    high = dot(xs, terms[0], dims)
    low = dot(xs, terms[1], dims)
    return (high[:rows] + high[rows:]) + (low[:rows] + low[rows:])


def in_chunks(count, most, run):
    size = min(count, most)
    if count == size:
        run(0, size)
    else:

        def step(i, carry):
            run(i * size, size)
            return carry

        lax.fori_loop(0, count // size, step, 0)


def at(i, size):
    first = i * size
    return pl.ds(first if isinstance(first, int) else pl.multiple_of(first, size), size)


def span_of(first, n):
    start = first * LANES
    return pl.ds(start if isinstance(start, int) else pl.multiple_of(start, LANES), n * LANES)


def group_mask(shape, row_width, col_width):
    row = lax.broadcasted_iota(i32, shape, 0) // row_width
    col = lax.broadcasted_iota(i32, shape, 1) // col_width
    return row == col


def spread_rows(mat, copies, mask):
    zero = jnp.zeros((), bf16)
    parts = [part.astype(bf16) for part in halves(mat)]
    return [jnp.where(mask, jnp.concatenate([part] * copies, axis=0), zero) for part in parts]


def whole(n):
    return [pl.BlockSpec(memory_space=pltpu.VMEM)] * n


def call(body, out_shape, n_in, scratch=(), nbytes=0, prefetch=False):
    specs = ([pl.BlockSpec(memory_space=pltpu.SMEM)] if prefetch else []) + whole(n_in)
    return pl.pallas_call(
        body,
        out_shape=out_shape,
        in_specs=specs,
        out_specs=pl.BlockSpec(memory_space=pltpu.VMEM),
        scratch_shapes=list(scratch),
        compiler_params=pltpu.CompilerParams(vmem_limit_bytes=VMEM_LIMIT),
        cost_estimate=pl.CostEstimate(flops=0, bytes_accessed=nbytes, transcendentals=0),
    )


def leaf_coefs(rhs, basis, leaf_pts):
    rows, width = rhs.shape
    rank = basis.shape[0]
    per = LANES // rank
    span = per * leaf_pts

    def body(x_ref, b_ref, o_ref):
        mask = group_mask((per * rank, span), rank, leaf_pts)

        def run(first, n):
            ids = [first + j for j in range(n)]
            ins = [(x_ref[:, at(i, span)], b_ref[:, at(i, span)]) for i in ids]
            outs = [two_term(x, spread_rows(m, per, mask), NT) for x, m in ins]
            for i, out in zip(ids, outs):
                o_ref[:, at(i, LANES)] = out

        in_chunks(width // span, 8, run)

    out = jax.ShapeDtypeStruct((rows, width // leaf_pts * rank), f32)
    return call(body, out, 2, nbytes=4 * 10**7)(rhs, basis)


def leaf_product(down, couple, basis, near, leaf_pts):
    rows, width = near.shape
    rank = basis.shape[0]
    per = LANES // rank
    span = per * leaf_pts

    def body(d_ref, c_ref, b_ref, n_ref, o_ref):
        mask = group_mask((per * rank, span), rank, leaf_pts)

        def run(first, n):
            ids = [first + j for j in range(n)]
            ins = [
                (d_ref[:, at(i, LANES)] + c_ref[:, at(i, LANES)], b_ref[:, at(i, span)]) for i in ids
            ]
            outs = [two_term(x, spread_rows(m, per, mask), NN) for x, m in ins]
            for i, out in zip(ids, outs):
                o_ref[:, at(i, span)] = n_ref[:, at(i, span)] + out

        in_chunks(width // span, 8, run)

    out = jax.ShapeDtypeStruct((rows, width), f32)
    return call(body, out, 4, nbytes=4 * 10**7)(
        down, couple, basis, near
    )


def tree_up(coef, transfer, leaves):
    rows, width = coef.shape
    rank = transfer.shape[0]
    levels = leaves.bit_length() - 1

    def body(c_ref, e_ref, o_ref, buf):
        for level in range(levels):
            here = leaves >> level
            offset = (2 * leaves - 2 * here) * rank
            share = 1 if level == 0 else 2
            out_span = min(LANES, here * rank)
            groups = out_span // rank * share
            span = groups * rank
            mask = group_mask((span, out_span), share * rank, rank)
            src = c_ref if level == 0 else buf.at[(level - 1) % 2]
            dst = buf.at[level % 2]

            def run(first, n):
                ids = [first + j for j in range(n)]
                base = offset // out_span
                ins = [(src[:, at(i, span)], e_ref[:, at(base + i, out_span)]) for i in ids]
                outs = [two_term(x, spread_rows(m, groups, mask), NN) for x, m in ins]
                for i, out in zip(ids, outs):
                    dst[:, at(i, out_span)] = out

            in_chunks(here * rank // out_span, 8, run)
        last = buf[(levels - 1) % 2, :, : 2 * rank]
        o_ref[...] = last[:, :rank] + last[:, rank:]

    return call(
        body,
        jax.ShapeDtypeStruct((rows, rank), f32),
        2,
        [pltpu.VMEM((2, rows, width), f32)],
        nbytes=4 * 10**7,
    )(coef, transfer)


def tree_down(root, transfer, leaves):
    rows = root.shape[0]
    rank = transfer.shape[0]
    levels = leaves.bit_length() - 1
    width = leaves * rank

    def body(r_ref, e_ref, o_ref, buf):
        top = r_ref[...]
        buf[levels % 2, :, : 2 * rank] = jnp.concatenate([top, top], axis=1)
        for level in reversed(range(levels)):
            here = leaves >> level
            offset = (2 * leaves - 2 * here) * rank
            share = 1 if level == 0 else 2
            in_span = min(LANES, here * rank)
            groups = in_span // rank * share
            span = groups * rank
            mask = group_mask((span, in_span), share * rank, rank)
            src = buf.at[(level + 1) % 2]
            dst = o_ref if level == 0 else buf.at[level % 2]

            def run(first, n):
                ids = [first + j for j in range(n)]
                base = offset // in_span
                ins = [(src[:, at(i, in_span)], e_ref[:, at(base + i, in_span)]) for i in ids]
                outs = [two_term(x, spread_rows(m, groups, mask), NT) for x, m in ins]
                for i, out in zip(ids, outs):
                    dst[:, at(i, span)] = out

            in_chunks(here * rank // in_span, 8, run)

    return call(
        body,
        jax.ShapeDtypeStruct((rows, width), f32),
        2,
        [pltpu.VMEM((2, rows, width), f32)],
        nbytes=4 * 10**7,
    )(root, transfer)


LOG2E = math.log2(math.e)


def selections():
    source, target = np.zeros((FEATS, FEATS), np.float32), np.zeros((FEATS, FEATS), np.float32)
    for d in range(3):
        for row, (p, q) in enumerate(((0, 0), (0, 1), (1, 0), (1, 1))):
            target[3 * row + d, 8 * p + d] = 1.0
            source[3 * row + d, 8 * q + d] = 1.0
    for row, term in ((12, 3), (13, 11)):
        source[row, term] = 1.0
        target[row, 4] = 1.0
        target[row + 2, term] = 1.0
        source[row + 2, 4] = 1.0
    return source, target


def features(coords, selection, scale):
    c = coords - 1.0
    row = lax.broadcasted_iota(i32, c.shape, 0)
    square = (-LOG2E / spread_sq) * jnp.sum(c * c, axis=0, keepdims=True)
    terms = jnp.where(row == 3, square, jnp.where(row == 4, 1.0, c * scale))
    return dot(selection, stacked(terms))


def eight_rows(coords):
    return jnp.pad(coords, ((0, 5), (0, 0)), constant_values=1.0)


def work_list(idx, live, group, dummy):
    count, listed = idx.shape
    items = count * (listed // group)
    livei = live.astype(i32)
    rank = jnp.sum(
        livei[:, None, :] * (jnp.arange(listed)[None, None, :] < jnp.arange(listed)[None, :, None]),
        axis=2,
    )
    slot = jnp.arange(listed, dtype=i32)
    hit = live[:, :, None] & (rank[:, :, None] == slot[None, None, :])
    total = jnp.sum(livei, axis=1)
    packed = jnp.sum(jnp.where(hit, idx[:, :, None], 0), axis=1)
    packed = jnp.where(slot[None, :] < total[:, None], packed, dummy)
    need = (total + group - 1) // group
    upto = jnp.arange(count)
    start = jnp.sum(jnp.where(upto[None, :] < upto[:, None], need[None, :], 0), axis=1)
    end = start + need
    k = jnp.arange(items, dtype=i32)
    one_hot = (start[None, :] <= k[:, None]) & (k[:, None] < end[None, :])
    target = jnp.sum(jnp.where(one_hot, upto[None, :].astype(i32), 0), axis=1)
    within = jnp.sum(jnp.where(one_hot, k[:, None] - start[None, :], 0), axis=1)
    rows = jnp.einsum(
        "kt,tm->km", one_hot.astype(f32), packed.astype(f32), precision=lax.Precision.HIGHEST
    )
    rows = jnp.round(rows).astype(i32).reshape(items, listed // group, group)
    pick = within[:, None, None] == jnp.arange(listed // group)[None, :, None]
    sources = jnp.sum(jnp.where(pick, rows, 0), axis=1)
    used = jnp.sum(need)
    sources = jnp.where((k < used)[:, None], sources, dummy)
    steps = (used + UNROLL - 1) // UNROLL
    return jnp.concatenate([target, sources.T.reshape(-1), steps[None]]), items


def pair_sums(listing, items, place, coords, sources, leaves, pts):
    rows = sources[0].shape[0]
    width = leaves * pts
    per = LANES // pts
    pieces = len(sources)
    held = pieces * leaves
    group = WIDE * per
    narrow = per > 2
    pick_source, pick_target = selections()
    eye = np.eye(LANES, dtype=np.float32)
    consts = [jnp.asarray(m, bf16) for m in (pick_source, pick_target, eye)]

    def body(list_ref, pick_s_ref, pick_t_ref, eye_ref, place_ref, *refs):
        coord_refs = refs[:pieces]
        x_refs = refs[pieces : 2 * pieces]
        o_ref, tab, targets_tab, acc = refs[2 * pieces :]
        lane = lax.broadcasted_iota(i32, (1, LANES), 1) // pts

        def fill_targets(first, n):
            here = span_of(first, n)
            feats = features(place_ref[:, here], pick_t_ref[...], 2.0 * LOG2E / spread_sq).astype(bf16)
            outs = [
                dot(eye_ref[...], feats[:, j * LANES : (j + 1) * LANES], NT).astype(bf16)
                for j in range(n)
            ]
            for j, out in enumerate(outs):
                for g in range(per):
                    targets_tab[(first + j) * per + g] = out[g * pts : (g + 1) * pts]

        in_chunks(width // LANES, 32, fill_targets)

        for piece in range(pieces):

            def fill(first, n):
                here = span_of(first, n)
                feats = features(coord_refs[piece][:, here], pick_s_ref[...], 1.0)
                hi, lo = halves(x_refs[piece][:, here])
                whole_rec = jnp.concatenate([feats, hi, lo], axis=0)
                outs = []
                for c in range(n):
                    rec = whole_rec[:, c * LANES : (c + 1) * LANES]
                    turned = [rec] + [pltpu.roll(rec, pts * j, 1) for j in range(1, per)]
                    for j in range(per):
                        out = turned[(per - j) % per]
                        for g in range(1, per):
                            out = jnp.where(lane == g, turned[(g - j) % per], out)
                        outs.append(out.astype(bf16))
                for j, out in enumerate(outs):
                    tab[piece * leaves + first * per + j] = out

            in_chunks(width // LANES, 16, fill)
        tab[held] = jnp.zeros(tab.shape[1:], bf16)

        def clear(first, n):
            for j in range(n):
                acc[first + j] = jnp.zeros(acc.shape[1:], f32)

        in_chunks(leaves, 32, clear)

        masks = [
            lax.broadcasted_iota(i32, (FEATS + 2 * rows, LANES), 1) >= g * pts
            for g in range(1, per)
        ]

        def step(n, carry):
            ks = [n * UNROLL + u for u in range(UNROLL)]
            targets = [list_ref[k] for k in ks]
            recs = []
            for k in ks:
                blocks = []
                for w in range(WIDE):
                    rec = tab[list_ref[(w * per + 1) * items + k]]
                    for g in range(1, per):
                        other = tab[list_ref[(w * per + g + 1) * items + k]]
                        rec = jnp.where(masks[g - 1], other, rec)
                    blocks.append(rec)
                recs.append(jnp.concatenate(blocks, axis=1))
            logs = [dot(targets_tab[t], rec[:FEATS]) for t, rec in zip(targets, recs)]
            kernels = [jnp.exp2(e) for e in logs]
            his = [k.astype(bf16) for k in kernels]
            los = [(k - h.astype(f32)).astype(bf16) for k, h in zip(kernels, his)]
            outs = []
            for rec, hi, lo in zip(recs, his, los):
                both = jnp.concatenate([hi, lo], axis=0)
                if narrow:
                    out = dot(both, rec[FEATS:], NT)
                    outs.append(out[:pts] + out[pts:])
                else:
                    out = dot(rec[FEATS:], both, NT)
                    outs.append(out[:rows] + out[rows:])
            for t, out in zip(targets, outs):
                acc[t] += out
            return carry

        lax.fori_loop(0, list_ref[(group + 1) * items], step, 0)

        def lay(start, n):
            outs = []
            for c in range(n):
                first = (start + c) * per
                if narrow:
                    out = jnp.concatenate([acc[first + j] for j in range(per)], axis=0).T
                    outs.append(out[:rows] + out[rows:])
                else:
                    for j in range(per):
                        one = acc[first + j]
                        one = one + pltpu.roll(one, pts, 1)
                        out = one if j == 0 else jnp.where(lane == j, one, out)
                    outs.append(out)
            for c, out in enumerate(outs):
                o_ref[:, at(start + c, LANES)] = out

        in_chunks(width // LANES, 16, lay)

    scratch = [
        pltpu.VMEM((held + 1, FEATS + 2 * rows, LANES), bf16),
        pltpu.VMEM((leaves, pts, FEATS), bf16),
        pltpu.VMEM((leaves, pts, 2 * rows) if narrow else (leaves, rows, LANES), f32),
    ]
    args = [listing, *consts, place, *coords, *sources]
    return call(
        body,
        jax.ShapeDtypeStruct((rows, width), f32),
        len(args) - 1,
        scratch,
        nbytes=15 * 10**7,
        prefetch=True,
    )(*args)


def local(rhs, points, basis, transfer, leaf_proxies, root_proxies, near_src, near_count, far_src):
    highest = lax.Precision.HIGHEST
    rows, width = rhs.shape
    leaves = near_src.shape[0]
    leaf_pts = width // leaves
    rank = basis.shape[0]
    near_max = near_src.shape[1]
    owner = lax.axis_index("leaf")
    size = lax.axis_size("leaf")
    up = [(i, (i + 1) % size) for i in range(size - 1)]
    down_pairs = [(j, i) for i, j in up]
    both_ways = lambda x: (lax.ppermute(x, "leaf", up), lax.ppermute(x, "leaf", down_pairs))

    shares = lax.axis_size("level") * lax.axis_size("sub")
    mine = lax.axis_index("level") * lax.axis_size("sub") + lax.axis_index("sub")
    near_share, far_share = width // shares, leaves * rank // shares
    share = jnp.concatenate(
        [
            lax.dynamic_slice_in_dim(points, mine * near_share, near_share, 1),
            lax.dynamic_slice_in_dim(leaf_proxies, mine * far_share, far_share, 1),
        ],
        axis=1,
    )
    share = jnp.stack(both_ways(share))
    coords = lax.all_gather(share, ("level", "sub"), axis=0)
    coords = jnp.moveaxis(coords, 0, 2)
    halo_points = coords[..., :near_share].reshape(2, 3, width)
    halo_proxies = coords[..., near_share:].reshape(2, 3, leaves * rank)

    coef = leaf_coefs(rhs, basis, leaf_pts)
    halo_rhs = both_ways(rhs)
    halo_coef = both_ways(coef)

    anchor = (owner - 1) * leaves
    live = jnp.arange(near_max, dtype=i32)[None, :] < near_count[:, None]
    near_list = work_list(near_src - anchor, live, WIDE * LANES // leaf_pts, 3 * leaves)
    far_live = jnp.ones(far_src.shape, bool)
    far_list = work_list(far_src - anchor, far_live, WIDE * LANES // rank, 3 * leaves)

    root = tree_up(coef, transfer, leaves)
    parts, origins = [], []
    for s in range(2, size):
        rise, fall = [(i, i + s) for i in range(size - s)], [(i + s, i) for i in range(size - s)]
        if 2 * s >= size:
            parts.append(lax.ppermute(root, "leaf", rise + fall))
            origins.append(jnp.where(owner >= s, owner - s, owner + s))
        else:
            parts += [lax.ppermute(root, "leaf", rise), lax.ppermute(root, "leaf", fall)]
            origins += [owner - s, owner + s]

    own_points, own_proxies = eight_rows(points), eight_rows(leaf_proxies)
    near = pair_sums(
        *near_list,
        own_points,
        [eight_rows(halo_points[0]), own_points, eight_rows(halo_points[1])],
        [halo_rhs[0], rhs, halo_rhs[1]],
        leaves,
        leaf_pts,
    )

    parts, near = lax.optimization_barrier((parts, near))
    own_proxy = lax.dynamic_slice_in_dim(root_proxies, owner * rank, rank, 1)
    top = jnp.zeros((rows, rank), f32)
    for part, origin in zip(parts, origins):
        there = (origin >= 0) & (origin < size)
        start = jnp.clip(origin, 0, size - 1) * rank
        proxy = lax.dynamic_slice_in_dim(root_proxies, start, rank, 1)
        dist = jnp.sum((own_proxy[:, :, None] - proxy[:, None, :]) ** 2, axis=0)
        kernel = jnp.where(there, jnp.exp(-dist / spread_sq), 0.0)
        top = top + jnp.einsum("aj,rj->ra", kernel, part, precision=highest)
    down = tree_down(top, transfer, leaves)

    couple = pair_sums(
        *far_list,
        own_proxies,
        [eight_rows(halo_proxies[0]), own_proxies, eight_rows(halo_proxies[1])],
        [halo_coef[0], coef, halo_coef[1]],
        leaves,
        rank,
    )
    return leaf_product(down, couple, basis, near, leaf_pts)


def solution(mesh):
    in_specs = (
        P(("level", "sub"), ("groups", "leaf")),
        P(None, ("groups", "leaf")),
        P(None, ("groups", "leaf")),
        P(None, ("groups", "leaf")),
        P(None, ("groups", "leaf")),
        P(None, "groups"),
        P(("groups", "leaf"), None),
        P(("groups", "leaf")),
        P(("groups", "leaf"), None),
    )
    out_specs = P(("level", "sub"), ("groups", "leaf"))
    return jax.shard_map(local, mesh=mesh, in_specs=in_specs, out_specs=out_specs, check_vma=False)
```

```python
import functools
import math

import jax
import jax.numpy as jnp
import numpy as np
from jax import lax
from jax.experimental import pallas as pl
from jax.experimental.pallas import tpu as pltpu
from jax.sharding import PartitionSpec as P

spread_sq = 0.5
LANES = 128
FEATS = 16
UNROLL = 32
WIDE = 2
STEPS = 8
VMEM_LIMIT = 58 * 1024 * 1024
f32, bf16, i32 = jnp.float32, jnp.bfloat16, jnp.int32

NN = (((1,), (0,)), ((), ()))
NT = (((1,), (1,)), ((), ()))


def dot(a, b, dims=NN):
    return lax.dot_general(a, b, dims, preferred_element_type=f32)


def halves(x):
    hi = x.astype(bf16).astype(f32)
    return hi, x - hi


def stacked(x):
    hi, lo = halves(x)
    return jnp.concatenate([hi, lo], axis=0).astype(bf16)


def two_term(x, terms, dims):
    rows = x.shape[0]
    xs = stacked(x)
    high = dot(xs, terms[0], dims)
    low = dot(xs, terms[1], dims)
    return (high[:rows] + high[rows:]) + (low[:rows] + low[rows:])


def in_chunks(count, most, run):
    size = min(count, most)
    if count == size:
        run(0, size)
    else:

        def step(i, carry):
            run(i * size, size)
            return carry

        lax.fori_loop(0, count // size, step, 0)


def at(i, size):
    first = i * size
    return pl.ds(first if isinstance(first, int) else pl.multiple_of(first, size), size)


def span_of(first, n):
    start = first * LANES
    return pl.ds(start if isinstance(start, int) else pl.multiple_of(start, LANES), n * LANES)


def group_mask(shape, row_width, col_width):
    row = lax.broadcasted_iota(i32, shape, 0) // row_width
    col = lax.broadcasted_iota(i32, shape, 1) // col_width
    return row == col


def spread_rows(mat, copies, mask):
    zero = jnp.zeros((), bf16)
    parts = [part.astype(bf16) for part in halves(mat)]
    return [jnp.where(mask, jnp.concatenate([part] * copies, axis=0), zero) for part in parts]


def whole(n):
    return [pl.BlockSpec(memory_space=pltpu.VMEM)] * n


def call_blocks(body, out_shape, widths, rows, steps, nbytes):
    block = lambda r, w: pl.BlockSpec((r, w // steps), lambda i: (0, i))
    return pl.pallas_call(
        body,
        out_shape=out_shape,
        grid=(steps,),
        in_specs=[block(r, w) for r, w in zip(rows, widths)],
        out_specs=block(*out_shape.shape),
        compiler_params=pltpu.CompilerParams(vmem_limit_bytes=VMEM_LIMIT),
        cost_estimate=pl.CostEstimate(flops=0, bytes_accessed=nbytes, transcendentals=0),
    )


def call(body, out_shape, n_in, scratch=(), nbytes=0, prefetch=False):
    specs = ([pl.BlockSpec(memory_space=pltpu.SMEM)] if prefetch else []) + whole(n_in)
    return pl.pallas_call(
        body,
        out_shape=out_shape,
        in_specs=specs,
        out_specs=pl.BlockSpec(memory_space=pltpu.VMEM),
        scratch_shapes=list(scratch),
        compiler_params=pltpu.CompilerParams(vmem_limit_bytes=VMEM_LIMIT),
        cost_estimate=pl.CostEstimate(flops=0, bytes_accessed=nbytes, transcendentals=0),
    )


def leaf_coefs(rhs, basis, leaf_pts):
    rows, width = rhs.shape
    rank = basis.shape[0]
    per = LANES // rank
    span = per * leaf_pts

    def body(x_ref, b_ref, o_ref):
        mask = group_mask((per * rank, span), rank, leaf_pts)

        def run(first, n):
            ids = [first + j for j in range(n)]
            ins = [(x_ref[:, at(i, span)], b_ref[:, at(i, span)]) for i in ids]
            outs = [two_term(x, spread_rows(m, per, mask), NT) for x, m in ins]
            for i, out in zip(ids, outs):
                o_ref[:, at(i, LANES)] = out

        in_chunks(width // span // STEPS, 8, run)

    out = jax.ShapeDtypeStruct((rows, width // leaf_pts * rank), f32)
    return call_blocks(body, out, (width, width), (rows, rank), STEPS, 4 * 10**7)(rhs, basis)


def leaf_product(down, couple, basis, near, leaf_pts):
    rows, width = near.shape
    rank = basis.shape[0]
    per = LANES // rank
    span = per * leaf_pts

    def body(d_ref, c_ref, b_ref, n_ref, o_ref):
        mask = group_mask((per * rank, span), rank, leaf_pts)

        def run(first, n):
            ids = [first + j for j in range(n)]
            ins = [
                (d_ref[:, at(i, LANES)] + c_ref[:, at(i, LANES)], b_ref[:, at(i, span)]) for i in ids
            ]
            outs = [two_term(x, spread_rows(m, per, mask), NN) for x, m in ins]
            for i, out in zip(ids, outs):
                o_ref[:, at(i, span)] = n_ref[:, at(i, span)] + out

        in_chunks(width // span // STEPS, 8, run)

    out = jax.ShapeDtypeStruct((rows, width), f32)
    far = down.shape[1]
    sizes = (far, far, width, width), (rows, rows, rank, rows)
    return call_blocks(body, out, *sizes, STEPS, 4 * 10**7)(down, couple, basis, near)


def tree_up(coef, transfer, leaves):
    rows, width = coef.shape
    rank = transfer.shape[0]
    levels = leaves.bit_length() - 1

    def body(c_ref, e_ref, o_ref, buf):
        for level in range(levels):
            here = leaves >> level
            offset = (2 * leaves - 2 * here) * rank
            share = 1 if level == 0 else 2
            out_span = min(LANES, here * rank)
            groups = out_span // rank * share
            span = groups * rank
            mask = group_mask((span, out_span), share * rank, rank)
            src = c_ref if level == 0 else buf.at[(level - 1) % 2]
            dst = buf.at[level % 2]

            def run(first, n):
                ids = [first + j for j in range(n)]
                base = offset // out_span
                ins = [(src[:, at(i, span)], e_ref[:, at(base + i, out_span)]) for i in ids]
                outs = [two_term(x, spread_rows(m, groups, mask), NN) for x, m in ins]
                for i, out in zip(ids, outs):
                    dst[:, at(i, out_span)] = out

            in_chunks(here * rank // out_span, 8, run)
        last = buf[(levels - 1) % 2, :, : 2 * rank]
        o_ref[...] = last[:, :rank] + last[:, rank:]

    return call(
        body,
        jax.ShapeDtypeStruct((rows, rank), f32),
        2,
        [pltpu.VMEM((2, rows, width), f32)],
        nbytes=4 * 10**7,
    )(coef, transfer)


def tree_down(root, transfer, leaves):
    rows = root.shape[0]
    rank = transfer.shape[0]
    levels = leaves.bit_length() - 1
    width = leaves * rank

    def body(r_ref, e_ref, o_ref, buf):
        top = r_ref[...]
        buf[levels % 2, :, : 2 * rank] = jnp.concatenate([top, top], axis=1)
        for level in reversed(range(levels)):
            here = leaves >> level
            offset = (2 * leaves - 2 * here) * rank
            share = 1 if level == 0 else 2
            in_span = min(LANES, here * rank)
            groups = in_span // rank * share
            span = groups * rank
            mask = group_mask((span, in_span), share * rank, rank)
            src = buf.at[(level + 1) % 2]
            dst = o_ref if level == 0 else buf.at[level % 2]

            def run(first, n):
                ids = [first + j for j in range(n)]
                base = offset // in_span
                ins = [(src[:, at(i, in_span)], e_ref[:, at(base + i, in_span)]) for i in ids]
                outs = [two_term(x, spread_rows(m, groups, mask), NT) for x, m in ins]
                for i, out in zip(ids, outs):
                    dst[:, at(i, span)] = out

            in_chunks(here * rank // in_span, 8, run)

    return call(
        body,
        jax.ShapeDtypeStruct((rows, width), f32),
        2,
        [pltpu.VMEM((2, rows, width), f32)],
        nbytes=4 * 10**7,
    )(root, transfer)


LOG2E = math.log2(math.e)


def selections():
    source, target = np.zeros((FEATS, FEATS), np.float32), np.zeros((FEATS, FEATS), np.float32)
    for d in range(3):
        for row, (p, q) in enumerate(((0, 0), (0, 1), (1, 0), (1, 1))):
            target[3 * row + d, 8 * p + d] = 1.0
            source[3 * row + d, 8 * q + d] = 1.0
    for row, term in ((12, 3), (13, 11)):
        source[row, term] = 1.0
        target[row, 4] = 1.0
        target[row + 2, term] = 1.0
        source[row + 2, 4] = 1.0
    return source, target


def features(coords, selection, scale):
    c = jnp.concatenate([coords - 1.0, jnp.zeros((5, coords.shape[1]), f32)], axis=0)
    row = lax.broadcasted_iota(i32, c.shape, 0)
    square = (-LOG2E / spread_sq) * jnp.sum(c * c, axis=0, keepdims=True)
    terms = jnp.where(row == 3, square, jnp.where(row == 4, 1.0, c * scale))
    return dot(selection, stacked(terms))


def work_list(idx, live, group, dummy):
    count, listed = idx.shape
    items = count * (listed // group)
    livei = live.astype(i32)
    rank = jnp.sum(
        livei[:, None, :] * (jnp.arange(listed)[None, None, :] < jnp.arange(listed)[None, :, None]),
        axis=2,
    )
    slot = jnp.arange(listed, dtype=i32)
    hit = live[:, :, None] & (rank[:, :, None] == slot[None, None, :])
    total = jnp.sum(livei, axis=1)
    packed = jnp.sum(jnp.where(hit, idx[:, :, None], 0), axis=1)
    packed = jnp.where(slot[None, :] < total[:, None], packed, dummy)
    need = (total + group - 1) // group
    upto = jnp.arange(count)
    start = jnp.sum(jnp.where(upto[None, :] < upto[:, None], need[None, :], 0), axis=1)
    end = start + need
    k = jnp.arange(items, dtype=i32)
    one_hot = (start[None, :] <= k[:, None]) & (k[:, None] < end[None, :])
    target = jnp.sum(jnp.where(one_hot, upto[None, :].astype(i32), 0), axis=1)
    within = jnp.sum(jnp.where(one_hot, k[:, None] - start[None, :], 0), axis=1)
    rows = jnp.einsum(
        "kt,tm->km", one_hot.astype(f32), packed.astype(f32), precision=lax.Precision.HIGHEST
    )
    rows = jnp.round(rows).astype(i32).reshape(items, listed // group, group)
    pick = within[:, None, None] == jnp.arange(listed // group)[None, :, None]
    sources = jnp.sum(jnp.where(pick, rows, 0), axis=1)
    used = jnp.sum(need)
    sources = jnp.where((k < used)[:, None], sources, dummy)
    steps = (used + UNROLL - 1) // UNROLL
    return jnp.concatenate([target, sources.T.reshape(-1), steps[None]]), items


def pair_sums(listing, items, coords, offset, sources, leaves, pts):
    rows = sources[0].shape[0]
    width = leaves * pts
    per = LANES // pts
    pieces = len(sources)
    held = pieces * leaves
    group = WIDE * per
    narrow = per > 2
    pick_source, pick_target = selections()
    eye = np.eye(LANES, dtype=np.float32)
    consts = [jnp.asarray(m, bf16) for m in (pick_source, pick_target, eye)]

    def body(list_ref, pick_s_ref, pick_t_ref, eye_ref, *refs):
        coord_refs = refs[:pieces]
        x_refs = refs[pieces : 2 * pieces]
        o_ref, tab, targets_tab, acc = refs[2 * pieces : 2 * pieces + 4]
        flat = refs[-1]
        lane = lax.broadcasted_iota(i32, (1, LANES), 1) // pts

        def fill_targets(first, n):
            here = span_of(first + offset // LANES, n)
            feats = features(coord_refs[pieces // 2][:, here], pick_t_ref[...], 2.0 * LOG2E / spread_sq).astype(bf16)
            outs = [
                dot(eye_ref[...], feats[:, j * LANES : (j + 1) * LANES], NT).astype(bf16)
                for j in range(n)
            ]
            for j, out in enumerate(outs):
                for g in range(per):
                    targets_tab[(first + j) * per + g] = out[g * pts : (g + 1) * pts]

        in_chunks(width // LANES, 32, fill_targets)

        def repeated(rec):
            turned = [rec] + [pltpu.roll(rec, pts * j, 1) for j in range(1, per)]
            outs = []
            for j in range(per):
                out = turned[(per - j) % per]
                for g in range(1, per):
                    out = jnp.where(lane == g, turned[(g - j) % per], out)
                outs.append(out.astype(bf16))
            return outs

        def fill_narrow(piece, first, n, feats):
            outs, upright = [], []
            for c in range(n):
                outs += repeated(feats[:, c * LANES : (c + 1) * LANES])
                x = stacked(x_refs[piece][:, at(first + c, LANES)])
                upright.append(dot(eye_ref[...], x, NT).astype(bf16))
            for j, out in enumerate(outs):
                tab[piece * leaves + first * per + j] = out
            for c, out in enumerate(upright):
                for j in range(per):
                    flat[piece * leaves + (first + c) * per + j] = out[j * pts : (j + 1) * pts]

        for piece in range(pieces):

            def fill(first, n):
                feats = features(
                    coord_refs[piece][:, span_of(first + offset // LANES, n)], pick_s_ref[...], 1.0
                )
                if narrow:
                    fill_narrow(piece, first, n, feats)
                    return
                hi, lo = halves(x_refs[piece][:, span_of(first, n)])
                whole_rec = jnp.concatenate([feats, hi, lo], axis=0)
                outs = []
                for c in range(n):
                    outs += repeated(whole_rec[:, c * LANES : (c + 1) * LANES])
                for j, out in enumerate(outs):
                    tab[piece * leaves + first * per + j] = out

            in_chunks(width // LANES, 16, fill)
        tab[held] = jnp.zeros(tab.shape[1:], bf16)
        if narrow:
            flat[held] = jnp.zeros(flat.shape[1:], bf16)

        def clear(first, n):
            for j in range(n):
                acc[first + j] = jnp.zeros(acc.shape[1:], f32)

        in_chunks(leaves, 32, clear)

        masks = [
            lax.broadcasted_iota(i32, (tab.shape[1], LANES), 1) >= g * pts
            for g in range(1, per)
        ]

        def step(n, carry):
            ks = [n * UNROLL + u for u in range(UNROLL)]
            targets = [list_ref[k] for k in ks]
            recs, values = [], []
            for k in ks:
                picks = [list_ref[(g + 1) * items + k] for g in range(group)]
                blocks = []
                for w in range(WIDE):
                    rec = tab[picks[w * per]]
                    for g in range(1, per):
                        rec = jnp.where(masks[g - 1], tab[picks[w * per + g]], rec)
                    blocks.append(rec)
                recs.append(jnp.concatenate(blocks, axis=1))
                if narrow:
                    values.append(jnp.concatenate([flat[pick] for pick in picks], axis=0))
                else:
                    values.append(recs[-1][FEATS:])
            logs = [dot(targets_tab[t], rec[:FEATS]) for t, rec in zip(targets, recs)]
            kernels = [jnp.exp2(e) for e in logs]
            his = [k.astype(bf16) for k in kernels]
            los = [(k - h.astype(f32)).astype(bf16) for k, h in zip(kernels, his)]
            outs = []
            for value, hi, lo in zip(values, his, los):
                both = jnp.concatenate([hi, lo], axis=0)
                if narrow:
                    out = dot(both, value, NN)
                    outs.append(out[:pts] + out[pts:])
                else:
                    out = dot(value, both, NT)
                    outs.append(out[:rows] + out[rows:])
            for t, out in zip(targets, outs):
                acc[t] += out
            return carry

        lax.fori_loop(0, list_ref[(group + 1) * items], step, 0)

        def lay(start, n):
            outs = []
            for c in range(n):
                first = (start + c) * per
                if narrow:
                    out = jnp.concatenate([acc[first + j] for j in range(per)], axis=0).T
                    outs.append(out[:rows] + out[rows:])
                else:
                    for j in range(per):
                        one = acc[first + j]
                        one = one + pltpu.roll(one, pts, 1)
                        out = one if j == 0 else jnp.where(lane == j, one, out)
                    outs.append(out)
            for c, out in enumerate(outs):
                o_ref[:, at(start + c, LANES)] = out

        in_chunks(width // LANES, 16, lay)

    scratch = [
        pltpu.VMEM((held + 1, FEATS + (0 if narrow else 2 * rows), LANES), bf16),
        pltpu.VMEM((leaves, pts, FEATS), bf16),
        pltpu.VMEM((leaves, pts, 2 * rows) if narrow else (leaves, rows, LANES), f32),
    ]
    if narrow:
        scratch.append(pltpu.VMEM((held + 1, pts, 2 * rows), bf16))
    args = [listing, *consts, *coords, *sources]
    return call(
        body,
        jax.ShapeDtypeStruct((rows, width), f32),
        len(args) - 1,
        scratch,
        nbytes=15 * 10**7,
        prefetch=True,
    )(*args)


def local(rhs, points, basis, transfer, leaf_proxies, root_proxies, near_src, near_count, far_src):
    highest = lax.Precision.HIGHEST
    rows, width = rhs.shape
    leaves = near_src.shape[0]
    leaf_pts = width // leaves
    rank = basis.shape[0]
    near_max = near_src.shape[1]
    owner = lax.axis_index("leaf")
    size = lax.axis_size("leaf")
    up = [(i, (i + 1) % size) for i in range(size - 1)]
    down_pairs = [(j, i) for i, j in up]
    both_ways = lambda x: (lax.ppermute(x, "leaf", up), lax.ppermute(x, "leaf", down_pairs))

    coords = jnp.concatenate([points, leaf_proxies], axis=1)
    halo_coords = both_ways(coords)
    coords = [halo_coords[0], coords, halo_coords[1]]
    coef = leaf_coefs(rhs, basis, leaf_pts)
    halo_rhs = both_ways(rhs)
    halo_coef = both_ways(coef)

    anchor = (owner - 1) * leaves
    live = jnp.arange(near_max, dtype=i32)[None, :] < near_count[:, None]
    near_list = work_list(near_src - anchor, live, WIDE * LANES // leaf_pts, 3 * leaves)
    far_live = jnp.ones(far_src.shape, bool)
    far_list = work_list(far_src - anchor, far_live, WIDE * LANES // rank, 3 * leaves)

    root = tree_up(coef, transfer, leaves)
    parts, origins = [], []
    for s in range(2, size):
        rise, fall = [(i, i + s) for i in range(size - s)], [(i + s, i) for i in range(size - s)]
        if 2 * s >= size:
            parts.append(lax.ppermute(root, "leaf", rise + fall))
            origins.append(jnp.where(owner >= s, owner - s, owner + s))
        else:
            parts += [lax.ppermute(root, "leaf", rise), lax.ppermute(root, "leaf", fall)]
            origins += [owner - s, owner + s]

    near = pair_sums(
        *near_list, coords, 0, [halo_rhs[0], rhs, halo_rhs[1]], leaves, leaf_pts
    )

    parts, near = lax.optimization_barrier((parts, near))
    own_proxy = lax.dynamic_slice_in_dim(root_proxies, owner * rank, rank, 1)
    top = jnp.zeros((rows, rank), f32)
    for part, origin in zip(parts, origins):
        there = (origin >= 0) & (origin < size)
        start = jnp.clip(origin, 0, size - 1) * rank
        proxy = lax.dynamic_slice_in_dim(root_proxies, start, rank, 1)
        dist = jnp.sum((own_proxy[:, :, None] - proxy[:, None, :]) ** 2, axis=0)
        kernel = jnp.where(there, jnp.exp(-dist / spread_sq), 0.0)
        top = top + jnp.einsum("aj,rj->ra", kernel, part, precision=highest)
    down = tree_down(top, transfer, leaves)

    couple = pair_sums(
        *far_list, coords, width, [halo_coef[0], coef, halo_coef[1]], leaves, rank
    )
    return leaf_product(down, couple, basis, near, leaf_pts)


def solution(mesh):
    in_specs = (
        P(("level", "sub"), ("groups", "leaf")),
        P(None, ("groups", "leaf")),
        P(None, ("groups", "leaf")),
        P(None, ("groups", "leaf")),
        P(None, ("groups", "leaf")),
        P(None, "groups"),
        P(("groups", "leaf"), None),
        P(("groups", "leaf")),
        P(("groups", "leaf"), None),
    )
    out_specs = P(("level", "sub"), ("groups", "leaf"))
    return jax.shard_map(local, mesh=mesh, in_specs=in_specs, out_specs=out_specs, check_vma=False)
```

```python
import functools
import math

import jax
import jax.numpy as jnp
import numpy as np
from jax import lax
from jax.experimental import pallas as pl
from jax.experimental.pallas import tpu as pltpu
from jax.sharding import PartitionSpec as P

spread_sq = 0.5
LANES = 128
FEATS = 16
UNROLL = 64
WIDE = 2
STEPS = 8
VMEM_LIMIT = 58 * 1024 * 1024
f32, bf16, i32 = jnp.float32, jnp.bfloat16, jnp.int32

NN = (((1,), (0,)), ((), ()))
NT = (((1,), (1,)), ((), ()))


def dot(a, b, dims=NN):
    return lax.dot_general(a, b, dims, preferred_element_type=f32)


def halves(x):
    hi = x.astype(bf16).astype(f32)
    return hi, x - hi


def stacked(x):
    hi, lo = halves(x)
    return jnp.concatenate([hi, lo], axis=0).astype(bf16)


def two_term(x, terms, dims):
    rows = x.shape[0]
    xs = stacked(x)
    high = dot(xs, terms[0], dims)
    low = dot(xs, terms[1], dims)
    return (high[:rows] + high[rows:]) + (low[:rows] + low[rows:])


def in_chunks(count, most, run):
    size = min(count, most)
    if count == size:
        run(0, size)
    else:

        def step(i, carry):
            run(i * size, size)
            return carry

        lax.fori_loop(0, count // size, step, 0)


def at(i, size):
    first = i * size
    return pl.ds(first if isinstance(first, int) else pl.multiple_of(first, size), size)


def span_of(first, n):
    start = first * LANES
    return pl.ds(start if isinstance(start, int) else pl.multiple_of(start, LANES), n * LANES)


def group_mask(shape, row_width, col_width):
    row = lax.broadcasted_iota(i32, shape, 0) // row_width
    col = lax.broadcasted_iota(i32, shape, 1) // col_width
    return row == col


def spread_rows(mat, copies, mask):
    zero = jnp.zeros((), bf16)
    parts = [part.astype(bf16) for part in halves(mat)]
    return [jnp.where(mask, jnp.concatenate([part] * copies, axis=0), zero) for part in parts]


def whole(n):
    return [pl.BlockSpec(memory_space=pltpu.VMEM)] * n


def call_blocks(body, out_shape, widths, rows, steps, nbytes):
    block = lambda r, w: pl.BlockSpec((r, w // steps), lambda i: (0, i))
    return pl.pallas_call(
        body,
        out_shape=out_shape,
        grid=(steps,),
        in_specs=[block(r, w) for r, w in zip(rows, widths)],
        out_specs=block(*out_shape.shape),
        compiler_params=pltpu.CompilerParams(vmem_limit_bytes=VMEM_LIMIT),
        cost_estimate=pl.CostEstimate(flops=0, bytes_accessed=nbytes, transcendentals=0),
    )


def call(body, out_shape, n_in, scratch=(), nbytes=0, prefetch=False):
    specs = ([pl.BlockSpec(memory_space=pltpu.SMEM)] if prefetch else []) + whole(n_in)
    return pl.pallas_call(
        body,
        out_shape=out_shape,
        in_specs=specs,
        out_specs=pl.BlockSpec(memory_space=pltpu.VMEM),
        scratch_shapes=list(scratch),
        compiler_params=pltpu.CompilerParams(vmem_limit_bytes=VMEM_LIMIT),
        cost_estimate=pl.CostEstimate(flops=0, bytes_accessed=nbytes, transcendentals=0),
    )


def leaf_coefs(rhs, basis, leaf_pts):
    rows, width = rhs.shape
    rank = basis.shape[0]
    per = LANES // rank
    span = per * leaf_pts

    def body(x_ref, b_ref, o_ref):
        mask = group_mask((per * rank, span), rank, leaf_pts)

        def run(first, n):
            ids = [first + j for j in range(n)]
            ins = [(x_ref[:, at(i, span)], b_ref[:, at(i, span)]) for i in ids]
            outs = [two_term(x, spread_rows(m, per, mask), NT) for x, m in ins]
            for i, out in zip(ids, outs):
                o_ref[:, at(i, LANES)] = out

        in_chunks(width // span // STEPS, 8, run)

    out = jax.ShapeDtypeStruct((rows, width // leaf_pts * rank), f32)
    return call_blocks(body, out, (width, width), (rows, rank), STEPS, 4 * 10**7)(rhs, basis)


def leaf_product(down, couple, basis, near, leaf_pts):
    rows, width = near.shape
    rank = basis.shape[0]
    per = LANES // rank
    span = per * leaf_pts

    def body(d_ref, c_ref, b_ref, n_ref, o_ref):
        mask = group_mask((per * rank, span), rank, leaf_pts)

        def run(first, n):
            ids = [first + j for j in range(n)]
            ins = [
                (d_ref[:, at(i, LANES)] + c_ref[:, at(i, LANES)], b_ref[:, at(i, span)]) for i in ids
            ]
            outs = [two_term(x, spread_rows(m, per, mask), NN) for x, m in ins]
            for i, out in zip(ids, outs):
                o_ref[:, at(i, span)] = n_ref[:, at(i, span)] + out

        in_chunks(width // span // STEPS, 8, run)

    out = jax.ShapeDtypeStruct((rows, width), f32)
    far = down.shape[1]
    sizes = (far, far, width, width), (rows, rows, rank, rows)
    return call_blocks(body, out, *sizes, STEPS, 4 * 10**7)(down, couple, basis, near)


def tree_up(coef, transfer, leaves):
    rows, width = coef.shape
    rank = transfer.shape[0]
    levels = leaves.bit_length() - 1

    def body(c_ref, e_ref, o_ref, buf):
        for level in range(levels):
            here = leaves >> level
            offset = (2 * leaves - 2 * here) * rank
            share = 1 if level == 0 else 2
            out_span = min(LANES, here * rank)
            groups = out_span // rank * share
            span = groups * rank
            mask = group_mask((span, out_span), share * rank, rank)
            src = c_ref if level == 0 else buf.at[(level - 1) % 2]
            dst = buf.at[level % 2]

            def run(first, n):
                ids = [first + j for j in range(n)]
                base = offset // out_span
                ins = [(src[:, at(i, span)], e_ref[:, at(base + i, out_span)]) for i in ids]
                outs = [two_term(x, spread_rows(m, groups, mask), NN) for x, m in ins]
                for i, out in zip(ids, outs):
                    dst[:, at(i, out_span)] = out

            in_chunks(here * rank // out_span, 8, run)
        last = buf[(levels - 1) % 2, :, : 2 * rank]
        o_ref[...] = last[:, :rank] + last[:, rank:]

    return call(
        body,
        jax.ShapeDtypeStruct((rows, rank), f32),
        2,
        [pltpu.VMEM((2, rows, width), f32)],
        nbytes=4 * 10**7,
    )(coef, transfer)


def tree_down(root, transfer, leaves):
    rows = root.shape[0]
    rank = transfer.shape[0]
    levels = leaves.bit_length() - 1
    width = leaves * rank

    def body(r_ref, e_ref, o_ref, buf):
        top = r_ref[...]
        buf[levels % 2, :, : 2 * rank] = jnp.concatenate([top, top], axis=1)
        for level in reversed(range(levels)):
            here = leaves >> level
            offset = (2 * leaves - 2 * here) * rank
            share = 1 if level == 0 else 2
            in_span = min(LANES, here * rank)
            groups = in_span // rank * share
            span = groups * rank
            mask = group_mask((span, in_span), share * rank, rank)
            src = buf.at[(level + 1) % 2]
            dst = o_ref if level == 0 else buf.at[level % 2]

            def run(first, n):
                ids = [first + j for j in range(n)]
                base = offset // in_span
                ins = [(src[:, at(i, in_span)], e_ref[:, at(base + i, in_span)]) for i in ids]
                outs = [two_term(x, spread_rows(m, groups, mask), NT) for x, m in ins]
                for i, out in zip(ids, outs):
                    dst[:, at(i, span)] = out

            in_chunks(here * rank // in_span, 8, run)

    return call(
        body,
        jax.ShapeDtypeStruct((rows, width), f32),
        2,
        [pltpu.VMEM((2, rows, width), f32)],
        nbytes=4 * 10**7,
    )(root, transfer)


LOG2E = math.log2(math.e)


def selections():
    source, target = np.zeros((FEATS, FEATS), np.float32), np.zeros((FEATS, FEATS), np.float32)
    for d in range(3):
        for row, (p, q) in enumerate(((0, 0), (0, 1), (1, 0), (1, 1))):
            target[3 * row + d, 8 * p + d] = 1.0
            source[3 * row + d, 8 * q + d] = 1.0
    for row, term in ((12, 3), (13, 11)):
        source[row, term] = 1.0
        target[row, 4] = 1.0
        target[row + 2, term] = 1.0
        source[row + 2, 4] = 1.0
    return source, target


def features(coords, selection, scale):
    c = jnp.concatenate([coords - 1.0, jnp.zeros((5, coords.shape[1]), f32)], axis=0)
    row = lax.broadcasted_iota(i32, c.shape, 0)
    square = (-LOG2E / spread_sq) * jnp.sum(c * c, axis=0, keepdims=True)
    terms = jnp.where(row == 3, square, jnp.where(row == 4, 1.0, c * scale))
    return dot(selection, stacked(terms))


def work_list(idx, live, group, dummy):
    count, listed = idx.shape
    items = count * (listed // group)
    livei = live.astype(i32)
    rank = jnp.sum(
        livei[:, None, :] * (jnp.arange(listed)[None, None, :] < jnp.arange(listed)[None, :, None]),
        axis=2,
    )
    slot = jnp.arange(listed, dtype=i32)
    hit = live[:, :, None] & (rank[:, :, None] == slot[None, None, :])
    total = jnp.sum(livei, axis=1)
    packed = jnp.sum(jnp.where(hit, idx[:, :, None], 0), axis=1)
    packed = jnp.where(slot[None, :] < total[:, None], packed, dummy)
    need = (total + group - 1) // group
    upto = jnp.arange(count)
    start = jnp.sum(jnp.where(upto[None, :] < upto[:, None], need[None, :], 0), axis=1)
    end = start + need
    k = jnp.arange(items, dtype=i32)
    one_hot = (start[None, :] <= k[:, None]) & (k[:, None] < end[None, :])
    target = jnp.sum(jnp.where(one_hot, upto[None, :].astype(i32), 0), axis=1)
    within = jnp.sum(jnp.where(one_hot, k[:, None] - start[None, :], 0), axis=1)
    rows = jnp.einsum(
        "kt,tm->km", one_hot.astype(f32), packed.astype(f32), precision=lax.Precision.HIGHEST
    )
    rows = jnp.round(rows).astype(i32).reshape(items, listed // group, group)
    pick = within[:, None, None] == jnp.arange(listed // group)[None, :, None]
    sources = jnp.sum(jnp.where(pick, rows, 0), axis=1)
    used = jnp.sum(need)
    sources = jnp.where((k < used)[:, None], sources, dummy)
    steps = (used + UNROLL - 1) // UNROLL
    return jnp.concatenate([target, sources.T.reshape(-1), steps[None]]), items


def pair_sums(listing, items, coords, offset, sources, leaves, pts):
    rows = sources[0].shape[0]
    width = leaves * pts
    per = LANES // pts
    pieces = len(sources)
    held = pieces * leaves
    group = WIDE * per
    narrow = per > 2
    pick_source, pick_target = selections()
    eye = np.eye(LANES, dtype=np.float32)
    consts = [jnp.asarray(m, bf16) for m in (pick_source, pick_target, eye)]

    def body(list_ref, pick_s_ref, pick_t_ref, eye_ref, *refs):
        coord_refs = refs[:pieces]
        x_refs = refs[pieces : 2 * pieces]
        o_ref, tab, targets_tab, acc = refs[2 * pieces : 2 * pieces + 4]
        flat = refs[-1]
        lane = lax.broadcasted_iota(i32, (1, LANES), 1) // pts

        def fill_targets(first, n):
            here = span_of(first + offset // LANES, n)
            feats = features(coord_refs[pieces // 2][:, here], pick_t_ref[...], 2.0 * LOG2E / spread_sq).astype(bf16)
            outs = [
                dot(eye_ref[...], feats[:, j * LANES : (j + 1) * LANES], NT).astype(bf16)
                for j in range(n)
            ]
            for j, out in enumerate(outs):
                for g in range(per):
                    targets_tab[(first + j) * per + g] = out[g * pts : (g + 1) * pts]

        in_chunks(width // LANES, 32, fill_targets)

        def repeated(rec):
            turned = [rec] + [pltpu.roll(rec, pts * j, 1) for j in range(1, per)]
            outs = []
            for j in range(per):
                out = turned[(per - j) % per]
                for g in range(1, per):
                    out = jnp.where(lane == g, turned[(g - j) % per], out)
                outs.append(out.astype(bf16))
            return outs

        def fill_narrow(piece, first, n, feats):
            outs, upright = [], []
            for c in range(n):
                outs += repeated(feats[:, c * LANES : (c + 1) * LANES])
                x = stacked(x_refs[piece][:, at(first + c, LANES)])
                upright.append(dot(eye_ref[...], x, NT).astype(bf16))
            for j, out in enumerate(outs):
                tab[piece * leaves + first * per + j] = out
            for c, out in enumerate(upright):
                for j in range(per):
                    flat[piece * leaves + (first + c) * per + j] = out[j * pts : (j + 1) * pts]

        for piece in range(pieces):

            def fill(first, n):
                feats = features(
                    coord_refs[piece][:, span_of(first + offset // LANES, n)], pick_s_ref[...], 1.0
                )
                if narrow:
                    fill_narrow(piece, first, n, feats)
                    return
                hi, lo = halves(x_refs[piece][:, span_of(first, n)])
                whole_rec = jnp.concatenate([feats, hi, lo], axis=0)
                outs = []
                for c in range(n):
                    outs += repeated(whole_rec[:, c * LANES : (c + 1) * LANES])
                for j, out in enumerate(outs):
                    tab[piece * leaves + first * per + j] = out

            in_chunks(width // LANES, 16, fill)
        tab[held] = jnp.zeros(tab.shape[1:], bf16)
        if narrow:
            flat[held] = jnp.zeros(flat.shape[1:], bf16)

        def clear(first, n):
            for j in range(n):
                acc[first + j] = jnp.zeros(acc.shape[1:], f32)

        in_chunks(leaves, 32, clear)

        masks = [
            lax.broadcasted_iota(i32, (tab.shape[1], LANES), 1) >= g * pts
            for g in range(1, per)
        ]

        def step(n, carry):
            ks = [n * UNROLL + u for u in range(UNROLL)]
            targets = [list_ref[k] for k in ks]
            recs, values = [], []
            for k in ks:
                picks = [list_ref[(g + 1) * items + k] for g in range(group)]
                blocks = []
                for w in range(WIDE):
                    rec = tab[picks[w * per]]
                    for g in range(1, per):
                        rec = jnp.where(masks[g - 1], tab[picks[w * per + g]], rec)
                    blocks.append(rec)
                recs.append(jnp.concatenate(blocks, axis=1))
                if narrow:
                    values.append(jnp.concatenate([flat[pick] for pick in picks], axis=0))
                else:
                    values.append(recs[-1][FEATS:])
            logs = [dot(targets_tab[t], rec[:FEATS]) for t, rec in zip(targets, recs)]
            kernels = [jnp.exp2(e) for e in logs]
            his = [k.astype(bf16) for k in kernels]
            los = [(k - h.astype(f32)).astype(bf16) for k, h in zip(kernels, his)]
            outs = []
            for value, hi, lo in zip(values, his, los):
                both = jnp.concatenate([hi, lo], axis=0)
                if narrow:
                    out = dot(both, value, NN)
                    outs.append(out[:pts] + out[pts:])
                else:
                    out = dot(value, both, NT)
                    outs.append(out[:rows] + out[rows:])
            for t, out in zip(targets, outs):
                acc[t] += out
            return carry

        lax.fori_loop(0, list_ref[(group + 1) * items], step, 0)

        def lay(start, n):
            outs = []
            for c in range(n):
                first = (start + c) * per
                if narrow:
                    out = jnp.concatenate([acc[first + j] for j in range(per)], axis=0).T
                    outs.append(out[:rows] + out[rows:])
                else:
                    for j in range(per):
                        one = acc[first + j]
                        one = one + pltpu.roll(one, pts, 1)
                        out = one if j == 0 else jnp.where(lane == j, one, out)
                    outs.append(out)
            for c, out in enumerate(outs):
                o_ref[:, at(start + c, LANES)] = out

        in_chunks(width // LANES, 16, lay)

    scratch = [
        pltpu.VMEM((held + 1, FEATS + (0 if narrow else 2 * rows), LANES), bf16),
        pltpu.VMEM((leaves, pts, FEATS), bf16),
        pltpu.VMEM((leaves, pts, 2 * rows) if narrow else (leaves, rows, LANES), f32),
    ]
    if narrow:
        scratch.append(pltpu.VMEM((held + 1, pts, 2 * rows), bf16))
    args = [listing, *consts, *coords, *sources]
    return call(
        body,
        jax.ShapeDtypeStruct((rows, width), f32),
        len(args) - 1,
        scratch,
        nbytes=15 * 10**7,
        prefetch=True,
    )(*args)


def local(rhs, points, basis, transfer, leaf_proxies, root_proxies, near_src, near_count, far_src):
    highest = lax.Precision.HIGHEST
    rows, width = rhs.shape
    leaves = near_src.shape[0]
    leaf_pts = width // leaves
    rank = basis.shape[0]
    near_max = near_src.shape[1]
    owner = lax.axis_index("leaf")
    size = lax.axis_size("leaf")
    up = [(i, (i + 1) % size) for i in range(size - 1)]
    down_pairs = [(j, i) for i, j in up]
    both_ways = lambda x: (lax.ppermute(x, "leaf", up), lax.ppermute(x, "leaf", down_pairs))

    coords = jnp.concatenate([points, leaf_proxies], axis=1)
    halo_coords = both_ways(coords)
    coef = leaf_coefs(rhs, basis, leaf_pts)

    anchor = (owner - 1) * leaves
    live = jnp.arange(near_max, dtype=i32)[None, :] < near_count[:, None]
    near_list = work_list(near_src - anchor, live, WIDE * LANES // leaf_pts, 3 * leaves)
    far_live = jnp.ones(far_src.shape, bool)
    far_list = work_list(far_src - anchor, far_live, WIDE * LANES // rank, 3 * leaves)

    root = tree_up(coef, transfer, leaves)
    halo_coords, coef, root = lax.optimization_barrier((halo_coords, coef, root))
    coords = [halo_coords[0], coords, halo_coords[1]]
    halo_coef = both_ways(coef)
    parts, origins = [], []
    for s in range(2, size):
        rise, fall = [(i, i + s) for i in range(size - s)], [(i + s, i) for i in range(size - s)]
        if 2 * s >= size:
            parts.append(lax.ppermute(root, "leaf", rise + fall))
            origins.append(jnp.where(owner >= s, owner - s, owner + s))
        else:
            parts += [lax.ppermute(root, "leaf", rise), lax.ppermute(root, "leaf", fall)]
            origins += [owner - s, owner + s]

    own_proxy = lax.dynamic_slice_in_dim(root_proxies, owner * rank, rank, 1)
    top = jnp.zeros((rows, rank), f32)
    for part, origin in zip(parts, origins):
        there = (origin >= 0) & (origin < size)
        start = jnp.clip(origin, 0, size - 1) * rank
        proxy = lax.dynamic_slice_in_dim(root_proxies, start, rank, 1)
        dist = jnp.sum((own_proxy[:, :, None] - proxy[:, None, :]) ** 2, axis=0)
        kernel = jnp.where(there, jnp.exp(-dist / spread_sq), 0.0)
        top = top + jnp.einsum("aj,rj->ra", kernel, part, precision=highest)
    down = tree_down(top, transfer, leaves)

    halo_coef, down, sent = lax.optimization_barrier((halo_coef, down, rhs))
    halo_rhs = both_ways(sent)
    couple = pair_sums(
        *far_list, coords, width, [halo_coef[0], coef, halo_coef[1]], leaves, rank
    )
    halo_rhs, couple = lax.optimization_barrier((halo_rhs, couple))
    near = pair_sums(
        *near_list, coords, 0, [halo_rhs[0], rhs, halo_rhs[1]], leaves, leaf_pts
    )
    return leaf_product(down, couple, basis, near, leaf_pts)


def solution(mesh):
    in_specs = (
        P(("level", "sub"), ("groups", "leaf")),
        P(None, ("groups", "leaf")),
        P(None, ("groups", "leaf")),
        P(None, ("groups", "leaf")),
        P(None, ("groups", "leaf")),
        P(None, "groups"),
        P(("groups", "leaf"), None),
        P(("groups", "leaf")),
        P(("groups", "leaf"), None),
    )
    out_specs = P(("level", "sub"), ("groups", "leaf"))
    return jax.shard_map(local, mesh=mesh, in_specs=in_specs, out_specs=out_specs, check_vma=False)
```

```python
import functools
import math

import jax
import jax.numpy as jnp
import numpy as np
from jax import lax
from jax.experimental import pallas as pl
from jax.experimental.pallas import tpu as pltpu
from jax.sharding import PartitionSpec as P

spread_sq = 0.5
LANES = 128
FEATS = 16
UNROLL = 64
WIDE = 2
STEPS = 4
VMEM_LIMIT = 58 * 1024 * 1024
f32, bf16, i32 = jnp.float32, jnp.bfloat16, jnp.int32

NN = (((1,), (0,)), ((), ()))
NT = (((1,), (1,)), ((), ()))


def dot(a, b, dims=NN):
    return lax.dot_general(a, b, dims, preferred_element_type=f32)


def halves(x):
    hi = x.astype(bf16).astype(f32)
    return hi, x - hi


def stacked(x):
    hi, lo = halves(x)
    return jnp.concatenate([hi, lo], axis=0).astype(bf16)


def two_term(x, terms, dims):
    rows = x.shape[0]
    xs = stacked(x)
    high = dot(xs, terms[0], dims)
    low = dot(xs, terms[1], dims)
    return (high[:rows] + high[rows:]) + (low[:rows] + low[rows:])


def in_chunks(count, most, run):
    size = min(count, most)
    if count == size:
        run(0, size)
    else:

        def step(i, carry):
            run(i * size, size)
            return carry

        lax.fori_loop(0, count // size, step, 0)


def at(i, size):
    first = i * size
    return pl.ds(first if isinstance(first, int) else pl.multiple_of(first, size), size)


def span_of(first, n):
    start = first * LANES
    return pl.ds(start if isinstance(start, int) else pl.multiple_of(start, LANES), n * LANES)


def group_mask(shape, row_width, col_width):
    row = lax.broadcasted_iota(i32, shape, 0) // row_width
    col = lax.broadcasted_iota(i32, shape, 1) // col_width
    return row == col


def spread_rows(mat, copies, mask):
    zero = jnp.zeros((), bf16)
    parts = [part.astype(bf16) for part in halves(mat)]
    return [jnp.where(mask, jnp.concatenate([part] * copies, axis=0), zero) for part in parts]


def whole(n):
    return [pl.BlockSpec(memory_space=pltpu.VMEM)] * n


def call_blocks(body, out_shape, widths, rows, steps, nbytes):
    block = lambda r, w: pl.BlockSpec((r, w // steps), lambda i: (0, i))
    return pl.pallas_call(
        body,
        out_shape=out_shape,
        grid=(steps,),
        in_specs=[block(r, w) for r, w in zip(rows, widths)],
        out_specs=block(*out_shape.shape),
        compiler_params=pltpu.CompilerParams(vmem_limit_bytes=VMEM_LIMIT),
        cost_estimate=pl.CostEstimate(flops=0, bytes_accessed=nbytes, transcendentals=0),
    )


def call(body, out_shape, n_in, scratch=(), nbytes=0, prefetch=False):
    specs = ([pl.BlockSpec(memory_space=pltpu.SMEM)] if prefetch else []) + whole(n_in)
    return pl.pallas_call(
        body,
        out_shape=out_shape,
        in_specs=specs,
        out_specs=pl.BlockSpec(memory_space=pltpu.VMEM),
        scratch_shapes=list(scratch),
        compiler_params=pltpu.CompilerParams(vmem_limit_bytes=VMEM_LIMIT),
        cost_estimate=pl.CostEstimate(flops=0, bytes_accessed=nbytes, transcendentals=0),
    )


def leaf_coefs(rhs, basis, leaf_pts):
    rows, width = rhs.shape
    rank = basis.shape[0]
    per = LANES // rank
    span = per * leaf_pts

    def body(x_ref, b_ref, o_ref):
        mask = group_mask((per * rank, span), rank, leaf_pts)

        def run(first, n):
            ids = [first + j for j in range(n)]
            ins = [(x_ref[:, at(i, span)], b_ref[:, at(i, span)]) for i in ids]
            outs = [two_term(x, spread_rows(m, per, mask), NT) for x, m in ins]
            for i, out in zip(ids, outs):
                o_ref[:, at(i, LANES)] = out

        in_chunks(width // span // STEPS, 32, run)

    out = jax.ShapeDtypeStruct((rows, width // leaf_pts * rank), f32)
    return call_blocks(body, out, (width, width), (rows, rank), STEPS, 4 * 10**7)(rhs, basis)


def leaf_product(down, couple, basis, near, leaf_pts):
    rows, width = near.shape
    rank = basis.shape[0]
    per = LANES // rank
    span = per * leaf_pts

    def body(d_ref, c_ref, b_ref, n_ref, o_ref):
        mask = group_mask((per * rank, span), rank, leaf_pts)

        def run(first, n):
            ids = [first + j for j in range(n)]
            ins = [
                (d_ref[:, at(i, LANES)] + c_ref[:, at(i, LANES)], b_ref[:, at(i, span)]) for i in ids
            ]
            outs = [two_term(x, spread_rows(m, per, mask), NN) for x, m in ins]
            for i, out in zip(ids, outs):
                o_ref[:, at(i, span)] = n_ref[:, at(i, span)] + out

        in_chunks(width // span // STEPS, 32, run)

    out = jax.ShapeDtypeStruct((rows, width), f32)
    far = down.shape[1]
    sizes = (far, far, width, width), (rows, rows, rank, rows)
    return call_blocks(body, out, *sizes, STEPS, 4 * 10**7)(down, couple, basis, near)


def tree_up(coef, transfer, leaves):
    rows, width = coef.shape
    rank = transfer.shape[0]
    levels = leaves.bit_length() - 1

    def body(c_ref, e_ref, o_ref, buf):
        for level in range(levels):
            here = leaves >> level
            offset = (2 * leaves - 2 * here) * rank
            share = 1 if level == 0 else 2
            out_span = min(LANES, here * rank)
            groups = out_span // rank * share
            span = groups * rank
            mask = group_mask((span, out_span), share * rank, rank)
            src = c_ref if level == 0 else buf.at[(level - 1) % 2]
            dst = buf.at[level % 2]

            def run(first, n):
                ids = [first + j for j in range(n)]
                base = offset // out_span
                ins = [(src[:, at(i, span)], e_ref[:, at(base + i, out_span)]) for i in ids]
                outs = [two_term(x, spread_rows(m, groups, mask), NN) for x, m in ins]
                for i, out in zip(ids, outs):
                    dst[:, at(i, out_span)] = out

            in_chunks(here * rank // out_span, 32, run)
        last = buf[(levels - 1) % 2, :, : 2 * rank]
        o_ref[...] = last[:, :rank] + last[:, rank:]

    return call(
        body,
        jax.ShapeDtypeStruct((rows, rank), f32),
        2,
        [pltpu.VMEM((2, rows, width), f32)],
        nbytes=4 * 10**7,
    )(coef, transfer)


def tree_down(root, transfer, leaves):
    rows = root.shape[0]
    rank = transfer.shape[0]
    levels = leaves.bit_length() - 1
    width = leaves * rank

    def body(r_ref, e_ref, o_ref, buf):
        top = r_ref[...]
        buf[levels % 2, :, : 2 * rank] = jnp.concatenate([top, top], axis=1)
        for level in reversed(range(levels)):
            here = leaves >> level
            offset = (2 * leaves - 2 * here) * rank
            share = 1 if level == 0 else 2
            in_span = min(LANES, here * rank)
            groups = in_span // rank * share
            span = groups * rank
            mask = group_mask((span, in_span), share * rank, rank)
            src = buf.at[(level + 1) % 2]
            dst = o_ref if level == 0 else buf.at[level % 2]

            def run(first, n):
                ids = [first + j for j in range(n)]
                base = offset // in_span
                ins = [(src[:, at(i, in_span)], e_ref[:, at(base + i, in_span)]) for i in ids]
                outs = [two_term(x, spread_rows(m, groups, mask), NT) for x, m in ins]
                for i, out in zip(ids, outs):
                    dst[:, at(i, span)] = out

            in_chunks(here * rank // in_span, 32, run)

    return call(
        body,
        jax.ShapeDtypeStruct((rows, width), f32),
        2,
        [pltpu.VMEM((2, rows, width), f32)],
        nbytes=4 * 10**7,
    )(root, transfer)


LOG2E = math.log2(math.e)


def selections():
    source, target = np.zeros((FEATS, FEATS), np.float32), np.zeros((FEATS, FEATS), np.float32)
    for d in range(3):
        for row, (p, q) in enumerate(((0, 0), (0, 1), (1, 0), (1, 1))):
            target[3 * row + d, 8 * p + d] = 1.0
            source[3 * row + d, 8 * q + d] = 1.0
    for row, term in ((12, 3), (13, 11)):
        source[row, term] = 1.0
        target[row, 4] = 1.0
        target[row + 2, term] = 1.0
        source[row + 2, 4] = 1.0
    return source, target


def features(coords, selection, scale):
    c = jnp.concatenate([coords - 1.0, jnp.zeros((5, coords.shape[1]), f32)], axis=0)
    row = lax.broadcasted_iota(i32, c.shape, 0)
    square = (-LOG2E / spread_sq) * jnp.sum(c * c, axis=0, keepdims=True)
    terms = jnp.where(row == 3, square, jnp.where(row == 4, 1.0, c * scale))
    return dot(selection, stacked(terms))


def work_list(idx, live, group, dummy):
    count, listed = idx.shape
    items = count * (listed // group)
    livei = live.astype(i32)
    rank = jnp.sum(
        livei[:, None, :] * (jnp.arange(listed)[None, None, :] < jnp.arange(listed)[None, :, None]),
        axis=2,
    )
    slot = jnp.arange(listed, dtype=i32)
    hit = live[:, :, None] & (rank[:, :, None] == slot[None, None, :])
    total = jnp.sum(livei, axis=1)
    packed = jnp.sum(jnp.where(hit, idx[:, :, None], 0), axis=1)
    packed = jnp.where(slot[None, :] < total[:, None], packed, dummy)
    need = (total + group - 1) // group
    upto = jnp.arange(count)
    start = jnp.sum(jnp.where(upto[None, :] < upto[:, None], need[None, :], 0), axis=1)
    end = start + need
    k = jnp.arange(items, dtype=i32)
    one_hot = (start[None, :] <= k[:, None]) & (k[:, None] < end[None, :])
    target = jnp.sum(jnp.where(one_hot, upto[None, :].astype(i32), 0), axis=1)
    within = jnp.sum(jnp.where(one_hot, k[:, None] - start[None, :], 0), axis=1)
    rows = jnp.einsum(
        "kt,tm->km", one_hot.astype(f32), packed.astype(f32), precision=lax.Precision.HIGHEST
    )
    rows = jnp.round(rows).astype(i32).reshape(items, listed // group, group)
    pick = within[:, None, None] == jnp.arange(listed // group)[None, :, None]
    sources = jnp.sum(jnp.where(pick, rows, 0), axis=1)
    used = jnp.sum(need)
    sources = jnp.where((k < used)[:, None], sources, dummy)
    steps = (used + UNROLL - 1) // UNROLL
    return jnp.concatenate([target, sources.T.reshape(-1), steps[None]]), items


def pair_sums(listing, items, coords, offset, sources, leaves, pts):
    rows = sources[0].shape[0]
    width = leaves * pts
    per = LANES // pts
    pieces = len(sources)
    held = pieces * leaves
    group = WIDE * per
    narrow = per > 2
    pick_source, pick_target = selections()
    eye = np.eye(LANES, dtype=np.float32)
    consts = [jnp.asarray(m, bf16) for m in (pick_source, pick_target, eye)]

    def body(list_ref, pick_s_ref, pick_t_ref, eye_ref, *refs):
        coord_refs = refs[:pieces]
        x_refs = refs[pieces : 2 * pieces]
        o_ref, tab, targets_tab, acc = refs[2 * pieces : 2 * pieces + 4]
        flat = refs[-1]
        lane = lax.broadcasted_iota(i32, (1, LANES), 1) // pts

        def fill_targets(first, n):
            here = span_of(first + offset // LANES, n)
            feats = features(coord_refs[pieces // 2][:, here], pick_t_ref[...], 2.0 * LOG2E / spread_sq).astype(bf16)
            outs = [
                dot(eye_ref[...], feats[:, j * LANES : (j + 1) * LANES], NT).astype(bf16)
                for j in range(n)
            ]
            for j, out in enumerate(outs):
                for g in range(per):
                    targets_tab[(first + j) * per + g] = out[g * pts : (g + 1) * pts]

        in_chunks(width // LANES, 32, fill_targets)

        def repeated(rec):
            turned = [rec] + [pltpu.roll(rec, pts * j, 1) for j in range(1, per)]
            outs = []
            for j in range(per):
                out = turned[(per - j) % per]
                for g in range(1, per):
                    out = jnp.where(lane == g, turned[(g - j) % per], out)
                outs.append(out.astype(bf16))
            return outs

        def fill_narrow(piece, first, n, feats):
            outs, upright = [], []
            for c in range(n):
                outs += repeated(feats[:, c * LANES : (c + 1) * LANES])
                x = stacked(x_refs[piece][:, at(first + c, LANES)])
                upright.append(dot(eye_ref[...], x, NT).astype(bf16))
            for j, out in enumerate(outs):
                tab[piece * leaves + first * per + j] = out
            for c, out in enumerate(upright):
                for j in range(per):
                    flat[piece * leaves + (first + c) * per + j] = out[j * pts : (j + 1) * pts]

        for piece in range(pieces):

            def fill(first, n):
                feats = features(
                    coord_refs[piece][:, span_of(first + offset // LANES, n)], pick_s_ref[...], 1.0
                )
                if narrow:
                    fill_narrow(piece, first, n, feats)
                    return
                hi, lo = halves(x_refs[piece][:, span_of(first, n)])
                whole_rec = jnp.concatenate([feats, hi, lo], axis=0)
                outs = []
                for c in range(n):
                    outs += repeated(whole_rec[:, c * LANES : (c + 1) * LANES])
                for j, out in enumerate(outs):
                    tab[piece * leaves + first * per + j] = out

            in_chunks(width // LANES, 64, fill)
        tab[held] = jnp.zeros(tab.shape[1:], bf16)
        if narrow:
            flat[held] = jnp.zeros(flat.shape[1:], bf16)

        def clear(first, n):
            for j in range(n):
                acc[first + j] = jnp.zeros(acc.shape[1:], f32)

        in_chunks(leaves, 32, clear)

        masks = [
            lax.broadcasted_iota(i32, (tab.shape[1], LANES), 1) >= g * pts
            for g in range(1, per)
        ]

        def step(n, carry):
            ks = [n * UNROLL + u for u in range(UNROLL)]
            targets = [list_ref[k] for k in ks]
            recs, values = [], []
            for k in ks:
                picks = [list_ref[(g + 1) * items + k] for g in range(group)]
                blocks = []
                for w in range(WIDE):
                    rec = tab[picks[w * per]]
                    for g in range(1, per):
                        rec = jnp.where(masks[g - 1], tab[picks[w * per + g]], rec)
                    blocks.append(rec)
                recs.append(jnp.concatenate(blocks, axis=1))
                if narrow:
                    values.append(jnp.concatenate([flat[pick] for pick in picks], axis=0))
                else:
                    values.append(recs[-1][FEATS:])
            logs = [dot(targets_tab[t], rec[:FEATS]) for t, rec in zip(targets, recs)]
            kernels = [jnp.exp2(e) for e in logs]
            his = [k.astype(bf16) for k in kernels]
            los = [(k - h.astype(f32)).astype(bf16) for k, h in zip(kernels, his)]
            outs = []
            for value, hi, lo in zip(values, his, los):
                both = jnp.concatenate([hi, lo], axis=0)
                if narrow:
                    out = dot(both, value, NN)
                    outs.append(out[:pts] + out[pts:])
                else:
                    out = dot(value, both, NT)
                    outs.append(out[:rows] + out[rows:])
            for t, out in zip(targets, outs):
                acc[t] += out
            return carry

        lax.fori_loop(0, list_ref[(group + 1) * items], step, 0)

        def lay(start, n):
            outs = []
            for c in range(n):
                first = (start + c) * per
                if narrow:
                    out = jnp.concatenate([acc[first + j] for j in range(per)], axis=0).T
                    outs.append(out[:rows] + out[rows:])
                else:
                    for j in range(per):
                        one = acc[first + j]
                        one = one + pltpu.roll(one, pts, 1)
                        out = one if j == 0 else jnp.where(lane == j, one, out)
                    outs.append(out)
            for c, out in enumerate(outs):
                o_ref[:, at(start + c, LANES)] = out

        in_chunks(width // LANES, 64, lay)

    scratch = [
        pltpu.VMEM((held + 1, FEATS + (0 if narrow else 2 * rows), LANES), bf16),
        pltpu.VMEM((leaves, pts, FEATS), bf16),
        pltpu.VMEM((leaves, pts, 2 * rows) if narrow else (leaves, rows, LANES), f32),
    ]
    if narrow:
        scratch.append(pltpu.VMEM((held + 1, pts, 2 * rows), bf16))
    args = [listing, *consts, *coords, *sources]
    return call(
        body,
        jax.ShapeDtypeStruct((rows, width), f32),
        len(args) - 1,
        scratch,
        nbytes=15 * 10**7,
        prefetch=True,
    )(*args)


def local(rhs, points, basis, transfer, leaf_proxies, root_proxies, near_src, near_count, far_src):
    highest = lax.Precision.HIGHEST
    rows, width = rhs.shape
    leaves = near_src.shape[0]
    leaf_pts = width // leaves
    rank = basis.shape[0]
    near_max = near_src.shape[1]
    owner = lax.axis_index("leaf")
    size = lax.axis_size("leaf")
    up = [(i, (i + 1) % size) for i in range(size - 1)]
    down_pairs = [(j, i) for i, j in up]
    both_ways = lambda x: (lax.ppermute(x, "leaf", up), lax.ppermute(x, "leaf", down_pairs))

    coords = jnp.concatenate([points, leaf_proxies], axis=1)
    halo_coords = both_ways(coords)
    coef = leaf_coefs(rhs, basis, leaf_pts)

    anchor = (owner - 1) * leaves
    live = jnp.arange(near_max, dtype=i32)[None, :] < near_count[:, None]
    near_list = work_list(near_src - anchor, live, WIDE * LANES // leaf_pts, 3 * leaves)
    far_live = jnp.ones(far_src.shape, bool)
    far_list = work_list(far_src - anchor, far_live, WIDE * LANES // rank, 3 * leaves)

    root = tree_up(coef, transfer, leaves)
    halo_coords, root = lax.optimization_barrier((halo_coords, root))
    halo_coef = both_ways(coef)
    parts, origins = [], []
    for s in range(2, size):
        rise, fall = [(i, i + s) for i in range(size - s)], [(i + s, i) for i in range(size - s)]
        if 2 * s >= size:
            parts.append(lax.ppermute(root, "leaf", rise + fall))
            origins.append(jnp.where(owner >= s, owner - s, owner + s))
        else:
            parts += [lax.ppermute(root, "leaf", rise), lax.ppermute(root, "leaf", fall)]
            origins += [owner - s, owner + s]

    halo_coef, halo_coords, sent = lax.optimization_barrier((halo_coef, halo_coords, rhs))
    halo_rhs = both_ways(sent)
    coords = [halo_coords[0], coords, halo_coords[1]]
    couple = pair_sums(
        *far_list, coords, width, [halo_coef[0], coef, halo_coef[1]], leaves, rank
    )
    parts, couple = lax.optimization_barrier((parts, couple))
    own_proxy = lax.dynamic_slice_in_dim(root_proxies, owner * rank, rank, 1)
    top = jnp.zeros((rows, rank), f32)
    for part, origin in zip(parts, origins):
        there = (origin >= 0) & (origin < size)
        start = jnp.clip(origin, 0, size - 1) * rank
        proxy = lax.dynamic_slice_in_dim(root_proxies, start, rank, 1)
        dist = jnp.sum((own_proxy[:, :, None] - proxy[:, None, :]) ** 2, axis=0)
        kernel = jnp.where(there, jnp.exp(-dist / spread_sq), 0.0)
        top = top + jnp.einsum("aj,rj->ra", kernel, part, precision=highest)
    down = tree_down(top, transfer, leaves)
    halo_rhs, down = lax.optimization_barrier((halo_rhs, down))
    near = pair_sums(
        *near_list, coords, 0, [halo_rhs[0], rhs, halo_rhs[1]], leaves, leaf_pts
    )
    return leaf_product(down, couple, basis, near, leaf_pts)


def solution(mesh):
    in_specs = (
        P(("level", "sub"), ("groups", "leaf")),
        P(None, ("groups", "leaf")),
        P(None, ("groups", "leaf")),
        P(None, ("groups", "leaf")),
        P(None, ("groups", "leaf")),
        P(None, "groups"),
        P(("groups", "leaf"), None),
        P(("groups", "leaf")),
        P(("groups", "leaf"), None),
    )
    out_specs = P(("level", "sub"), ("groups", "leaf"))
    return jax.shard_map(local, mesh=mesh, in_specs=in_specs, out_specs=out_specs, check_vma=False)
```

```python
import functools
import math

import jax
import jax.numpy as jnp
import numpy as np
from jax import lax
from jax.experimental import pallas as pl
from jax.experimental.pallas import tpu as pltpu
from jax.sharding import PartitionSpec as P

spread_sq = 0.5
LANES = 128
FEATS = 16
UNROLL = 64
WIDE = 2
STEPS = 4
VMEM_LIMIT = 58 * 1024 * 1024
f32, bf16, i32 = jnp.float32, jnp.bfloat16, jnp.int32

NN = (((1,), (0,)), ((), ()))
NT = (((1,), (1,)), ((), ()))


def dot(a, b, dims=NN):
    return lax.dot_general(a, b, dims, preferred_element_type=f32)


def halves(x):
    hi = x.astype(bf16).astype(f32)
    return hi, x - hi


def stacked(x):
    hi, lo = halves(x)
    return jnp.concatenate([hi, lo], axis=0).astype(bf16)


def two_term(x, terms, dims):
    rows = x.shape[0]
    xs = stacked(x)
    high = dot(xs, terms[0], dims)
    low = dot(xs, terms[1], dims)
    return (high[:rows] + high[rows:]) + (low[:rows] + low[rows:])


def in_chunks(count, most, run):
    size = min(count, most)
    if count == size:
        run(0, size)
    else:

        def step(i, carry):
            run(i * size, size)
            return carry

        lax.fori_loop(0, count // size, step, 0)


def at(i, size):
    first = i * size
    return pl.ds(first if isinstance(first, int) else pl.multiple_of(first, size), size)


def span_of(first, n):
    start = first * LANES
    return pl.ds(start if isinstance(start, int) else pl.multiple_of(start, LANES), n * LANES)


def group_mask(shape, row_width, col_width):
    row = lax.broadcasted_iota(i32, shape, 0) // row_width
    col = lax.broadcasted_iota(i32, shape, 1) // col_width
    return row == col


def spread_rows(mat, copies, mask):
    zero = jnp.zeros((), bf16)
    parts = [part.astype(bf16) for part in halves(mat)]
    return [jnp.where(mask, jnp.concatenate([part] * copies, axis=0), zero) for part in parts]


def whole(n):
    return [pl.BlockSpec(memory_space=pltpu.VMEM)] * n


def call_blocks(body, out_shape, widths, rows, steps, nbytes):
    block = lambda r, w: pl.BlockSpec((r, w // steps), lambda i: (0, i))
    return pl.pallas_call(
        body,
        out_shape=out_shape,
        grid=(steps,),
        in_specs=[block(r, w) for r, w in zip(rows, widths)],
        out_specs=block(*out_shape.shape),
        compiler_params=pltpu.CompilerParams(vmem_limit_bytes=VMEM_LIMIT),
        cost_estimate=pl.CostEstimate(flops=0, bytes_accessed=nbytes, transcendentals=0),
    )


def call(body, out_shape, n_in, scratch=(), nbytes=0, prefetch=False, n_any=0):
    specs = ([pl.BlockSpec(memory_space=pltpu.SMEM)] if prefetch else []) + whole(n_in)
    specs += [pl.BlockSpec(memory_space=pl.ANY)] * n_any
    return pl.pallas_call(
        body,
        out_shape=out_shape,
        in_specs=specs,
        out_specs=pl.BlockSpec(memory_space=pltpu.VMEM),
        scratch_shapes=list(scratch),
        compiler_params=pltpu.CompilerParams(vmem_limit_bytes=VMEM_LIMIT),
        cost_estimate=pl.CostEstimate(flops=0, bytes_accessed=nbytes, transcendentals=0),
    )


def leaf_coefs(rhs, basis, leaf_pts):
    rows, width = rhs.shape
    rank = basis.shape[0]
    per = LANES // rank
    span = per * leaf_pts

    def body(x_ref, b_ref, o_ref):
        mask = group_mask((per * rank, span), rank, leaf_pts)

        def run(first, n):
            ids = [first + j for j in range(n)]
            ins = [(x_ref[:, at(i, span)], b_ref[:, at(i, span)]) for i in ids]
            outs = [two_term(x, spread_rows(m, per, mask), NT) for x, m in ins]
            for i, out in zip(ids, outs):
                o_ref[:, at(i, LANES)] = out

        in_chunks(width // span // STEPS, 32, run)

    out = jax.ShapeDtypeStruct((rows, width // leaf_pts * rank), f32)
    return call_blocks(body, out, (width, width), (rows, rank), STEPS, 4 * 10**7)(rhs, basis)


def leaf_product(down, couple, basis, near, leaf_pts):
    rows, width = near.shape
    rank = basis.shape[0]
    per = LANES // rank
    span = per * leaf_pts

    def body(d_ref, c_ref, b_ref, n_ref, o_ref):
        mask = group_mask((per * rank, span), rank, leaf_pts)

        def run(first, n):
            ids = [first + j for j in range(n)]
            ins = [
                (d_ref[:, at(i, LANES)] + c_ref[:, at(i, LANES)], b_ref[:, at(i, span)]) for i in ids
            ]
            outs = [two_term(x, spread_rows(m, per, mask), NN) for x, m in ins]
            for i, out in zip(ids, outs):
                o_ref[:, at(i, span)] = n_ref[:, at(i, span)] + out

        in_chunks(width // span // STEPS, 32, run)

    out = jax.ShapeDtypeStruct((rows, width), f32)
    far = down.shape[1]
    sizes = (far, far, width, width), (rows, rows, rank, rows)
    return call_blocks(body, out, *sizes, STEPS, 4 * 10**7)(down, couple, basis, near)


def tree_up(coef, transfer, leaves):
    rows, width = coef.shape
    rank = transfer.shape[0]
    levels = leaves.bit_length() - 1

    def body(c_ref, e_ref, o_ref, buf):
        for level in range(levels):
            here = leaves >> level
            offset = (2 * leaves - 2 * here) * rank
            share = 1 if level == 0 else 2
            out_span = min(LANES, here * rank)
            groups = out_span // rank * share
            span = groups * rank
            mask = group_mask((span, out_span), share * rank, rank)
            src = c_ref if level == 0 else buf.at[(level - 1) % 2]
            dst = buf.at[level % 2]

            def run(first, n):
                ids = [first + j for j in range(n)]
                base = offset // out_span
                ins = [(src[:, at(i, span)], e_ref[:, at(base + i, out_span)]) for i in ids]
                outs = [two_term(x, spread_rows(m, groups, mask), NN) for x, m in ins]
                for i, out in zip(ids, outs):
                    dst[:, at(i, out_span)] = out

            in_chunks(here * rank // out_span, 32, run)
        last = buf[(levels - 1) % 2, :, : 2 * rank]
        o_ref[...] = last[:, :rank] + last[:, rank:]

    return call(
        body,
        jax.ShapeDtypeStruct((rows, rank), f32),
        2,
        [pltpu.VMEM((2, rows, width), f32)],
        nbytes=4 * 10**7,
    )(coef, transfer)


def tree_down(root, transfer, leaves):
    rows = root.shape[0]
    rank = transfer.shape[0]
    levels = leaves.bit_length() - 1
    width = leaves * rank

    def body(r_ref, e_ref, o_ref, buf):
        top = r_ref[...]
        buf[levels % 2, :, : 2 * rank] = jnp.concatenate([top, top], axis=1)
        for level in reversed(range(levels)):
            here = leaves >> level
            offset = (2 * leaves - 2 * here) * rank
            share = 1 if level == 0 else 2
            in_span = min(LANES, here * rank)
            groups = in_span // rank * share
            span = groups * rank
            mask = group_mask((span, in_span), share * rank, rank)
            src = buf.at[(level + 1) % 2]
            dst = o_ref if level == 0 else buf.at[level % 2]

            def run(first, n):
                ids = [first + j for j in range(n)]
                base = offset // in_span
                ins = [(src[:, at(i, in_span)], e_ref[:, at(base + i, in_span)]) for i in ids]
                outs = [two_term(x, spread_rows(m, groups, mask), NT) for x, m in ins]
                for i, out in zip(ids, outs):
                    dst[:, at(i, span)] = out

            in_chunks(here * rank // in_span, 32, run)

    return call(
        body,
        jax.ShapeDtypeStruct((rows, width), f32),
        2,
        [pltpu.VMEM((2, rows, width), f32)],
        nbytes=4 * 10**7,
    )(root, transfer)


LOG2E = math.log2(math.e)


def selections():
    source, target = np.zeros((FEATS, FEATS), np.float32), np.zeros((FEATS, FEATS), np.float32)
    for d in range(3):
        for row, (p, q) in enumerate(((0, 0), (0, 1), (1, 0), (1, 1))):
            target[3 * row + d, 8 * p + d] = 1.0
            source[3 * row + d, 8 * q + d] = 1.0
    for row, term in ((12, 3), (13, 11)):
        source[row, term] = 1.0
        target[row, 4] = 1.0
        target[row + 2, term] = 1.0
        source[row + 2, 4] = 1.0
    return source, target


def features(coords, selection, scale):
    c = jnp.concatenate([coords - 1.0, jnp.zeros((5, coords.shape[1]), f32)], axis=0)
    row = lax.broadcasted_iota(i32, c.shape, 0)
    square = (-LOG2E / spread_sq) * jnp.sum(c * c, axis=0, keepdims=True)
    terms = jnp.where(row == 3, square, jnp.where(row == 4, 1.0, c * scale))
    return dot(selection, stacked(terms))


def work_list(idx, live, group, dummy):
    count, listed = idx.shape
    items = count * (listed // group)
    livei = live.astype(i32)
    rank = jnp.sum(
        livei[:, None, :] * (jnp.arange(listed)[None, None, :] < jnp.arange(listed)[None, :, None]),
        axis=2,
    )
    slot = jnp.arange(listed, dtype=i32)
    hit = live[:, :, None] & (rank[:, :, None] == slot[None, None, :])
    total = jnp.sum(livei, axis=1)
    packed = jnp.sum(jnp.where(hit, idx[:, :, None], 0), axis=1)
    packed = jnp.where(slot[None, :] < total[:, None], packed, dummy)
    need = (total + group - 1) // group
    upto = jnp.arange(count)
    start = jnp.sum(jnp.where(upto[None, :] < upto[:, None], need[None, :], 0), axis=1)
    end = start + need
    k = jnp.arange(items, dtype=i32)
    one_hot = (start[None, :] <= k[:, None]) & (k[:, None] < end[None, :])
    target = jnp.sum(jnp.where(one_hot, upto[None, :].astype(i32), 0), axis=1)
    within = jnp.sum(jnp.where(one_hot, k[:, None] - start[None, :], 0), axis=1)
    rows = jnp.einsum(
        "kt,tm->km", one_hot.astype(f32), packed.astype(f32), precision=lax.Precision.HIGHEST
    )
    rows = jnp.round(rows).astype(i32).reshape(items, listed // group, group)
    pick = within[:, None, None] == jnp.arange(listed // group)[None, :, None]
    sources = jnp.sum(jnp.where(pick, rows, 0), axis=1)
    used = jnp.sum(need)
    sources = jnp.where((k < used)[:, None], sources, dummy)
    steps = (used + UNROLL - 1) // UNROLL
    return jnp.concatenate([target, sources.T.reshape(-1), steps[None]]), items


def pair_sums(listing, items, coords, offset, sources, leaves, pts):
    rows = sources[0].shape[0]
    width = leaves * pts
    per = LANES // pts
    pieces = len(sources)
    held = pieces * leaves
    group = WIDE * per
    narrow = per > 2
    pick_source, pick_target = selections()
    eye = np.eye(LANES, dtype=np.float32)
    consts = [jnp.asarray(m, bf16) for m in (pick_source, pick_target, eye)]

    def body(list_ref, pick_s_ref, pick_t_ref, eye_ref, *refs):
        o_ref, tab, targets_tab, acc, coord_refs, x_refs, sems = refs[2 * pieces : 2 * pieces + 7]
        flat = refs[-1]
        own = pieces // 2
        order = [own] + [p for p in range(pieces) if p != own]
        copies = {}
        for p in order:
            copies[p] = [
                pltpu.make_async_copy(
                    refs[p].at[:, pl.ds(offset, width)], coord_refs.at[p], sems.at[2 * p]
                ),
                pltpu.make_async_copy(refs[pieces + p], x_refs.at[p], sems.at[2 * p + 1]),
            ]
            for copy in copies[p]:
                copy.start()
        lane = lax.broadcasted_iota(i32, (1, LANES), 1) // pts

        copies[own][0].wait()

        def fill_targets(first, n):
            here = span_of(first, n)
            feats = features(coord_refs[own, :, here], pick_t_ref[...], 2.0 * LOG2E / spread_sq).astype(bf16)
            outs = [
                dot(eye_ref[...], feats[:, j * LANES : (j + 1) * LANES], NT).astype(bf16)
                for j in range(n)
            ]
            for j, out in enumerate(outs):
                for g in range(per):
                    targets_tab[(first + j) * per + g] = out[g * pts : (g + 1) * pts]

        in_chunks(width // LANES, 32, fill_targets)

        def repeated(rec):
            turned = [rec] + [pltpu.roll(rec, pts * j, 1) for j in range(1, per)]
            outs = []
            for j in range(per):
                out = turned[(per - j) % per]
                for g in range(1, per):
                    out = jnp.where(lane == g, turned[(g - j) % per], out)
                outs.append(out.astype(bf16))
            return outs

        def fill_narrow(piece, first, n, feats):
            outs, upright = [], []
            for c in range(n):
                outs += repeated(feats[:, c * LANES : (c + 1) * LANES])
                x = stacked(x_refs[piece, :, at(first + c, LANES)])
                upright.append(dot(eye_ref[...], x, NT).astype(bf16))
            for j, out in enumerate(outs):
                tab[piece * leaves + first * per + j] = out
            for c, out in enumerate(upright):
                for j in range(per):
                    flat[piece * leaves + (first + c) * per + j] = out[j * pts : (j + 1) * pts]

        for piece in order:
            for copy in copies[piece][1 if piece == own else 0 :]:
                copy.wait()

            def fill(first, n):
                here = span_of(first, n)
                feats = features(coord_refs[piece, :, here], pick_s_ref[...], 1.0)
                if narrow:
                    fill_narrow(piece, first, n, feats)
                    return
                hi, lo = halves(x_refs[piece, :, here])
                whole_rec = jnp.concatenate([feats, hi, lo], axis=0)
                outs = []
                for c in range(n):
                    outs += repeated(whole_rec[:, c * LANES : (c + 1) * LANES])
                for j, out in enumerate(outs):
                    tab[piece * leaves + first * per + j] = out

            in_chunks(width // LANES, 64, fill)
        tab[held] = jnp.zeros(tab.shape[1:], bf16)
        if narrow:
            flat[held] = jnp.zeros(flat.shape[1:], bf16)

        def clear(first, n):
            for j in range(n):
                acc[first + j] = jnp.zeros(acc.shape[1:], f32)

        in_chunks(leaves, 32, clear)

        masks = [
            lax.broadcasted_iota(i32, (tab.shape[1], LANES), 1) >= g * pts
            for g in range(1, per)
        ]

        def step(n, carry):
            ks = [n * UNROLL + u for u in range(UNROLL)]
            targets = [list_ref[k] for k in ks]
            recs, values = [], []
            for k in ks:
                picks = [list_ref[(g + 1) * items + k] for g in range(group)]
                blocks = []
                for w in range(WIDE):
                    rec = tab[picks[w * per]]
                    for g in range(1, per):
                        rec = jnp.where(masks[g - 1], tab[picks[w * per + g]], rec)
                    blocks.append(rec)
                recs.append(jnp.concatenate(blocks, axis=1))
                if narrow:
                    values.append(jnp.concatenate([flat[pick] for pick in picks], axis=0))
                else:
                    values.append(recs[-1][FEATS:])
            logs = [dot(targets_tab[t], rec[:FEATS]) for t, rec in zip(targets, recs)]
            kernels = [jnp.exp2(e) for e in logs]
            his = [k.astype(bf16) for k in kernels]
            los = [(k - h.astype(f32)).astype(bf16) for k, h in zip(kernels, his)]
            outs = []
            for value, hi, lo in zip(values, his, los):
                both = jnp.concatenate([hi, lo], axis=0)
                if narrow:
                    out = dot(both, value, NN)
                    outs.append(out[:pts] + out[pts:])
                else:
                    out = dot(value, both, NT)
                    outs.append(out[:rows] + out[rows:])
            for t, out in zip(targets, outs):
                acc[t] += out
            return carry

        lax.fori_loop(0, list_ref[(group + 1) * items], step, 0)

        def lay(start, n):
            outs = []
            for c in range(n):
                first = (start + c) * per
                if narrow:
                    out = jnp.concatenate([acc[first + j] for j in range(per)], axis=0).T
                    outs.append(out[:rows] + out[rows:])
                else:
                    for j in range(per):
                        one = acc[first + j]
                        one = one + pltpu.roll(one, pts, 1)
                        out = one if j == 0 else jnp.where(lane == j, one, out)
                    outs.append(out)
            for c, out in enumerate(outs):
                o_ref[:, at(start + c, LANES)] = out

        in_chunks(width // LANES, 64, lay)

    scratch = [
        pltpu.VMEM((held + 1, FEATS + (0 if narrow else 2 * rows), LANES), bf16),
        pltpu.VMEM((leaves, pts, FEATS), bf16),
        pltpu.VMEM((leaves, pts, 2 * rows) if narrow else (leaves, rows, LANES), f32),
    ]
    scratch += [
        pltpu.VMEM((pieces, 3, width), f32),
        pltpu.VMEM((pieces, rows, width), f32),
        pltpu.SemaphoreType.DMA((2 * pieces,)),
    ]
    if narrow:
        scratch.append(pltpu.VMEM((held + 1, pts, 2 * rows), bf16))
    args = [listing, *consts, *coords, *sources]
    return call(
        body,
        jax.ShapeDtypeStruct((rows, width), f32),
        len(consts),
        scratch,
        nbytes=15 * 10**7,
        prefetch=True,
        n_any=2 * pieces,
    )(*args)


def local(rhs, points, basis, transfer, leaf_proxies, root_proxies, near_src, near_count, far_src):
    highest = lax.Precision.HIGHEST
    rows, width = rhs.shape
    leaves = near_src.shape[0]
    leaf_pts = width // leaves
    rank = basis.shape[0]
    near_max = near_src.shape[1]
    owner = lax.axis_index("leaf")
    size = lax.axis_size("leaf")
    up = [(i, (i + 1) % size) for i in range(size - 1)]
    down_pairs = [(j, i) for i, j in up]
    both_ways = lambda x: (lax.ppermute(x, "leaf", up), lax.ppermute(x, "leaf", down_pairs))

    coords = jnp.concatenate([points, leaf_proxies], axis=1)
    halo_coords = both_ways(coords)
    coef = leaf_coefs(rhs, basis, leaf_pts)

    anchor = (owner - 1) * leaves
    live = jnp.arange(near_max, dtype=i32)[None, :] < near_count[:, None]
    near_list = work_list(near_src - anchor, live, WIDE * LANES // leaf_pts, 3 * leaves)
    far_live = jnp.ones(far_src.shape, bool)
    far_list = work_list(far_src - anchor, far_live, WIDE * LANES // rank, 3 * leaves)

    root = tree_up(coef, transfer, leaves)
    halo_coords, root = lax.optimization_barrier((halo_coords, root))
    halo_coef = both_ways(coef)
    parts, origins = [], []
    for s in range(2, size):
        rise, fall = [(i, i + s) for i in range(size - s)], [(i + s, i) for i in range(size - s)]
        if 2 * s >= size:
            parts.append(lax.ppermute(root, "leaf", rise + fall))
            origins.append(jnp.where(owner >= s, owner - s, owner + s))
        else:
            parts += [lax.ppermute(root, "leaf", rise), lax.ppermute(root, "leaf", fall)]
            origins += [owner - s, owner + s]

    halo_coords, sent = lax.optimization_barrier((halo_coords, rhs))
    halo_rhs = both_ways(sent)
    coords = [halo_coords[0], coords, halo_coords[1]]
    couple = pair_sums(
        *far_list, coords, width, [halo_coef[0], coef, halo_coef[1]], leaves, rank
    )
    parts, couple = lax.optimization_barrier((parts, couple))
    own_proxy = lax.dynamic_slice_in_dim(root_proxies, owner * rank, rank, 1)
    top = jnp.zeros((rows, rank), f32)
    for part, origin in zip(parts, origins):
        there = (origin >= 0) & (origin < size)
        start = jnp.clip(origin, 0, size - 1) * rank
        proxy = lax.dynamic_slice_in_dim(root_proxies, start, rank, 1)
        dist = jnp.sum((own_proxy[:, :, None] - proxy[:, None, :]) ** 2, axis=0)
        kernel = jnp.where(there, jnp.exp(-dist / spread_sq), 0.0)
        top = top + jnp.einsum("aj,rj->ra", kernel, part, precision=highest)
    down = tree_down(top, transfer, leaves)
    halo_rhs, down = lax.optimization_barrier((halo_rhs, down))
    near = pair_sums(
        *near_list, coords, 0, [halo_rhs[0], rhs, halo_rhs[1]], leaves, leaf_pts
    )
    return leaf_product(down, couple, basis, near, leaf_pts)


def solution(mesh):
    in_specs = (
        P(("level", "sub"), ("groups", "leaf")),
        P(None, ("groups", "leaf")),
        P(None, ("groups", "leaf")),
        P(None, ("groups", "leaf")),
        P(None, ("groups", "leaf")),
        P(None, "groups"),
        P(("groups", "leaf"), None),
        P(("groups", "leaf")),
        P(("groups", "leaf"), None),
    )
    out_specs = P(("level", "sub"), ("groups", "leaf"))
    return jax.shard_map(local, mesh=mesh, in_specs=in_specs, out_specs=out_specs, check_vma=False)
```

```python
import functools
import math

import jax
import jax.numpy as jnp
import numpy as np
from jax import lax
from jax.experimental import pallas as pl
from jax.experimental.pallas import tpu as pltpu
from jax.sharding import PartitionSpec as P

spread_sq = 0.5
LANES = 128
FEATS = 16
UNROLL = 64
WIDE = 2
STEPS = 4
VMEM_LIMIT = 58 * 1024 * 1024
f32, bf16, i32 = jnp.float32, jnp.bfloat16, jnp.int32

NN = (((1,), (0,)), ((), ()))
NT = (((1,), (1,)), ((), ()))


def dot(a, b, dims=NN):
    return lax.dot_general(a, b, dims, preferred_element_type=f32)


def halves(x):
    hi = x.astype(bf16).astype(f32)
    return hi, x - hi


def stacked(x):
    hi, lo = halves(x)
    return jnp.concatenate([hi, lo], axis=0).astype(bf16)


def two_term(x, terms, dims):
    rows = x.shape[0]
    xs = stacked(x)
    high = dot(xs, terms[0], dims)
    low = dot(xs, terms[1], dims)
    return (high[:rows] + high[rows:]) + (low[:rows] + low[rows:])


def in_chunks(count, most, run):
    size = min(count, most)
    if count == size:
        run(0, size)
    else:

        def step(i, carry):
            run(i * size, size)
            return carry

        lax.fori_loop(0, count // size, step, 0)


def at(i, size):
    first = i * size
    return pl.ds(first if isinstance(first, int) else pl.multiple_of(first, size), size)


def span_of(first, n):
    start = first * LANES
    return pl.ds(start if isinstance(start, int) else pl.multiple_of(start, LANES), n * LANES)


def group_mask(shape, row_width, col_width):
    row = lax.broadcasted_iota(i32, shape, 0) // row_width
    col = lax.broadcasted_iota(i32, shape, 1) // col_width
    return row == col


def spread_rows(mat, copies, mask):
    zero = jnp.zeros((), bf16)
    parts = [part.astype(bf16) for part in halves(mat)]
    return [jnp.where(mask, jnp.concatenate([part] * copies, axis=0), zero) for part in parts]


def whole(n):
    return [pl.BlockSpec(memory_space=pltpu.VMEM)] * n


def call_blocks(body, out_shape, widths, rows, steps, nbytes):
    block = lambda r, w: pl.BlockSpec((r, w // steps), lambda i: (0, i))
    return pl.pallas_call(
        body,
        out_shape=out_shape,
        grid=(steps,),
        in_specs=[block(r, w) for r, w in zip(rows, widths)],
        out_specs=block(*out_shape.shape),
        compiler_params=pltpu.CompilerParams(vmem_limit_bytes=VMEM_LIMIT),
        cost_estimate=pl.CostEstimate(flops=0, bytes_accessed=nbytes, transcendentals=0),
    )


def call(body, out_shape, n_in, scratch=(), nbytes=0, prefetch=False, n_any=0):
    specs = ([pl.BlockSpec(memory_space=pltpu.SMEM)] if prefetch else []) + whole(n_in)
    specs += [pl.BlockSpec(memory_space=pl.ANY)] * n_any
    return pl.pallas_call(
        body,
        out_shape=out_shape,
        in_specs=specs,
        out_specs=pl.BlockSpec(memory_space=pltpu.VMEM),
        scratch_shapes=list(scratch),
        compiler_params=pltpu.CompilerParams(vmem_limit_bytes=VMEM_LIMIT),
        cost_estimate=pl.CostEstimate(flops=0, bytes_accessed=nbytes, transcendentals=0),
    )


def leaf_coefs(rhs, basis, leaf_pts):
    rows, width = rhs.shape
    rank = basis.shape[0]
    per = LANES // rank
    span = per * leaf_pts

    def body(x_ref, b_ref, o_ref):
        mask = group_mask((per * rank, span), rank, leaf_pts)

        def run(first, n):
            ids = [first + j for j in range(n)]
            ins = [(x_ref[:, at(i, span)], b_ref[:, at(i, span)]) for i in ids]
            outs = [two_term(x, spread_rows(m, per, mask), NT) for x, m in ins]
            for i, out in zip(ids, outs):
                o_ref[:, at(i, LANES)] = out

        in_chunks(width // span // STEPS, 32, run)

    out = jax.ShapeDtypeStruct((rows, width // leaf_pts * rank), f32)
    return call_blocks(body, out, (width, width), (rows, rank), STEPS, 4 * 10**7)(rhs, basis)


def tree_up(coef, transfer, leaves):
    rows, width = coef.shape
    rank = transfer.shape[0]
    levels = leaves.bit_length() - 1

    def body(c_ref, e_ref, o_ref, buf):
        for level in range(levels):
            here = leaves >> level
            offset = (2 * leaves - 2 * here) * rank
            share = 1 if level == 0 else 2
            out_span = min(LANES, here * rank)
            groups = out_span // rank * share
            span = groups * rank
            mask = group_mask((span, out_span), share * rank, rank)
            src = c_ref if level == 0 else buf.at[(level - 1) % 2]
            dst = buf.at[level % 2]

            def run(first, n):
                ids = [first + j for j in range(n)]
                base = offset // out_span
                ins = [(src[:, at(i, span)], e_ref[:, at(base + i, out_span)]) for i in ids]
                outs = [two_term(x, spread_rows(m, groups, mask), NN) for x, m in ins]
                for i, out in zip(ids, outs):
                    dst[:, at(i, out_span)] = out

            in_chunks(here * rank // out_span, 32, run)
        last = buf[(levels - 1) % 2, :, : 2 * rank]
        o_ref[...] = last[:, :rank] + last[:, rank:]

    return call(
        body,
        jax.ShapeDtypeStruct((rows, rank), f32),
        2,
        [pltpu.VMEM((2, rows, width), f32)],
        nbytes=4 * 10**7,
    )(coef, transfer)


def tree_down(root, transfer, leaves):
    rows = root.shape[0]
    rank = transfer.shape[0]
    levels = leaves.bit_length() - 1
    width = leaves * rank

    def body(r_ref, e_ref, o_ref, buf):
        top = r_ref[...]
        buf[levels % 2, :, : 2 * rank] = jnp.concatenate([top, top], axis=1)
        for level in reversed(range(levels)):
            here = leaves >> level
            offset = (2 * leaves - 2 * here) * rank
            share = 1 if level == 0 else 2
            in_span = min(LANES, here * rank)
            groups = in_span // rank * share
            span = groups * rank
            mask = group_mask((span, in_span), share * rank, rank)
            src = buf.at[(level + 1) % 2]
            dst = o_ref if level == 0 else buf.at[level % 2]

            def run(first, n):
                ids = [first + j for j in range(n)]
                base = offset // in_span
                ins = [(src[:, at(i, in_span)], e_ref[:, at(base + i, in_span)]) for i in ids]
                outs = [two_term(x, spread_rows(m, groups, mask), NT) for x, m in ins]
                for i, out in zip(ids, outs):
                    dst[:, at(i, span)] = out

            in_chunks(here * rank // in_span, 32, run)

    return call(
        body,
        jax.ShapeDtypeStruct((rows, width), f32),
        2,
        [pltpu.VMEM((2, rows, width), f32)],
        nbytes=4 * 10**7,
    )(root, transfer)


def full_list(idx, group):
    count, listed = idx.shape
    per = listed // group
    items = count * per
    target = jnp.arange(items, dtype=i32) // per
    sources = idx.reshape(items, group).T.reshape(-1)
    return jnp.concatenate([target, sources, jnp.full((1,), items // UNROLL, i32)]), items


LOG2E = math.log2(math.e)


def selections():
    source, target = np.zeros((FEATS, FEATS), np.float32), np.zeros((FEATS, FEATS), np.float32)
    for d in range(3):
        for row, (p, q) in enumerate(((0, 0), (0, 1), (1, 0), (1, 1))):
            target[3 * row + d, 8 * p + d] = 1.0
            source[3 * row + d, 8 * q + d] = 1.0
    for row, term in ((12, 3), (13, 11)):
        source[row, term] = 1.0
        target[row, 4] = 1.0
        target[row + 2, term] = 1.0
        source[row + 2, 4] = 1.0
    return source, target


def features(coords, selection, scale):
    c = jnp.concatenate([coords - 1.0, jnp.zeros((5, coords.shape[1]), f32)], axis=0)
    row = lax.broadcasted_iota(i32, c.shape, 0)
    square = (-LOG2E / spread_sq) * jnp.sum(c * c, axis=0, keepdims=True)
    terms = jnp.where(row == 3, square, jnp.where(row == 4, 1.0, c * scale))
    return dot(selection, stacked(terms))


def work_list(idx, live, group, dummy):
    count, listed = idx.shape
    items = count * (listed // group)
    livei = live.astype(i32)
    rank = jnp.sum(
        livei[:, None, :] * (jnp.arange(listed)[None, None, :] < jnp.arange(listed)[None, :, None]),
        axis=2,
    )
    slot = jnp.arange(listed, dtype=i32)
    hit = live[:, :, None] & (rank[:, :, None] == slot[None, None, :])
    total = jnp.sum(livei, axis=1)
    packed = jnp.sum(jnp.where(hit, idx[:, :, None], 0), axis=1)
    packed = jnp.where(slot[None, :] < total[:, None], packed, dummy)
    need = (total + group - 1) // group
    upto = jnp.arange(count)
    start = jnp.sum(jnp.where(upto[None, :] < upto[:, None], need[None, :], 0), axis=1)
    end = start + need
    k = jnp.arange(items, dtype=i32)
    one_hot = (start[None, :] <= k[:, None]) & (k[:, None] < end[None, :])
    target = jnp.sum(jnp.where(one_hot, upto[None, :].astype(i32), 0), axis=1)
    within = jnp.sum(jnp.where(one_hot, k[:, None] - start[None, :], 0), axis=1)
    rows = jnp.einsum(
        "kt,tm->km", one_hot.astype(f32), packed.astype(f32), precision=lax.Precision.HIGHEST
    )
    rows = jnp.round(rows).astype(i32).reshape(items, listed // group, group)
    pick = within[:, None, None] == jnp.arange(listed // group)[None, :, None]
    sources = jnp.sum(jnp.where(pick, rows, 0), axis=1)
    used = jnp.sum(need)
    sources = jnp.where((k < used)[:, None], sources, dummy)
    steps = (used + UNROLL - 1) // UNROLL
    return jnp.concatenate([target, sources.T.reshape(-1), steps[None]]), items


def pair_sums(listing, items, coords, offset, sources, leaves, pts, finish=()):
    rows = sources[0].shape[0]
    width = leaves * pts
    per = LANES // pts
    pieces = len(sources)
    held = pieces * leaves
    group = WIDE * per
    narrow = per > 2
    pick_source, pick_target = selections()
    eye = np.eye(LANES, dtype=np.float32)
    consts = [jnp.asarray(m, bf16) for m in (pick_source, pick_target, eye)]

    def body(list_ref, pick_s_ref, pick_t_ref, eye_ref, *refs):
        last = refs[2 * pieces : 2 * pieces + len(finish)]
        more = refs[2 * pieces + len(finish) :]
        o_ref, tab, targets_tab, acc, coord_refs, x_refs, sems = more[:7]
        flat, bufs = more[-1], more[7:]
        own = pieces // 2
        order = [own] + [p for p in range(pieces) if p != own]
        copies = {}
        for p in order:
            copies[p] = [
                pltpu.make_async_copy(
                    refs[p].at[:, pl.ds(offset, width)], coord_refs.at[p], sems.at[2 * p]
                ),
                pltpu.make_async_copy(refs[pieces + p], x_refs.at[p], sems.at[2 * p + 1]),
            ]
            for copy in copies[p]:
                copy.start()
        lane = lax.broadcasted_iota(i32, (1, LANES), 1) // pts

        late = [
            pltpu.make_async_copy(ref, buf, sems.at[2 * pieces + j])
            for j, (ref, buf) in enumerate(zip(last, bufs))
        ]
        for copy in late:
            copy.start()
        copies[own][0].wait()

        def fill_targets(first, n):
            here = span_of(first, n)
            feats = features(coord_refs[own, :, here], pick_t_ref[...], 2.0 * LOG2E / spread_sq).astype(bf16)
            outs = [
                dot(eye_ref[...], feats[:, j * LANES : (j + 1) * LANES], NT).astype(bf16)
                for j in range(n)
            ]
            for j, out in enumerate(outs):
                for g in range(per):
                    targets_tab[(first + j) * per + g] = out[g * pts : (g + 1) * pts]

        in_chunks(width // LANES, 32, fill_targets)

        def repeated(rec):
            turned = [rec] + [pltpu.roll(rec, pts * j, 1) for j in range(1, per)]
            outs = []
            for j in range(per):
                out = turned[(per - j) % per]
                for g in range(1, per):
                    out = jnp.where(lane == g, turned[(g - j) % per], out)
                outs.append(out.astype(bf16))
            return outs

        def fill_narrow(piece, first, n, feats):
            outs, upright = [], []
            for c in range(n):
                outs += repeated(feats[:, c * LANES : (c + 1) * LANES])
                x = stacked(x_refs[piece, :, at(first + c, LANES)])
                upright.append(dot(eye_ref[...], x, NT).astype(bf16))
            for j, out in enumerate(outs):
                tab[piece * leaves + first * per + j] = out
            for c, out in enumerate(upright):
                for j in range(per):
                    flat[piece * leaves + (first + c) * per + j] = out[j * pts : (j + 1) * pts]

        for piece in order:
            for copy in copies[piece][1 if piece == own else 0 :]:
                copy.wait()

            def fill(first, n):
                here = span_of(first, n)
                feats = features(coord_refs[piece, :, here], pick_s_ref[...], 1.0)
                if narrow:
                    fill_narrow(piece, first, n, feats)
                    return
                hi, lo = halves(x_refs[piece, :, here])
                whole_rec = jnp.concatenate([feats, hi, lo], axis=0)
                outs = []
                for c in range(n):
                    outs += repeated(whole_rec[:, c * LANES : (c + 1) * LANES])
                for j, out in enumerate(outs):
                    tab[piece * leaves + first * per + j] = out

            in_chunks(width // LANES, 64, fill)
        tab[held] = jnp.zeros(tab.shape[1:], bf16)
        if narrow:
            flat[held] = jnp.zeros(flat.shape[1:], bf16)

        def clear(first, n):
            for j in range(n):
                acc[first + j] = jnp.zeros(acc.shape[1:], f32)

        in_chunks(leaves, 32, clear)

        masks = [
            lax.broadcasted_iota(i32, (tab.shape[1], LANES), 1) >= g * pts
            for g in range(1, per)
        ]

        def step(n, carry):
            ks = [n * UNROLL + u for u in range(UNROLL)]
            targets = [list_ref[k] for k in ks]
            recs, values = [], []
            for k in ks:
                picks = [list_ref[(g + 1) * items + k] for g in range(group)]
                blocks = []
                for w in range(WIDE):
                    rec = tab[picks[w * per]]
                    for g in range(1, per):
                        rec = jnp.where(masks[g - 1], tab[picks[w * per + g]], rec)
                    blocks.append(rec)
                recs.append(jnp.concatenate(blocks, axis=1))
                if narrow:
                    values.append(jnp.concatenate([flat[pick] for pick in picks], axis=0))
                else:
                    values.append(recs[-1][FEATS:])
            logs = [dot(targets_tab[t], rec[:FEATS]) for t, rec in zip(targets, recs)]
            kernels = [jnp.exp2(e) for e in logs]
            his = [k.astype(bf16) for k in kernels]
            los = [(k - h.astype(f32)).astype(bf16) for k, h in zip(kernels, his)]
            outs = []
            for value, hi, lo in zip(values, his, los):
                both = jnp.concatenate([hi, lo], axis=0)
                if narrow:
                    out = dot(both, value, NN)
                    outs.append(out[:pts] + out[pts:])
                else:
                    out = dot(value, both, NT)
                    outs.append(out[:rows] + out[rows:])
            for t, out in zip(targets, outs):
                acc[t] += out
            return carry

        lax.fori_loop(0, list_ref[(group + 1) * items], step, 0)

        def block(i):
            if narrow:
                out = jnp.concatenate([acc[i * per + j] for j in range(per)], axis=0).T
                return out[:rows] + out[rows:]
            for j in range(per):
                one = acc[i * per + j]
                one = one + pltpu.roll(one, pts, 1)
                out = one if j == 0 else jnp.where(lane == j, one, out)
            return out

        if finish:
            for copy in late:
                copy.wait()
            d_ref, c_ref, b_ref = bufs[:3]
            rank = finish[2].shape[0]
            ranks = LANES // rank
            span = ranks * pts
            mask = group_mask((LANES, span), rank, pts)

            def lay(start, n):
                outs = []
                for i in range(n):
                    here = at(start + i, LANES)
                    first = (start + i) * (span // LANES)
                    near = jnp.concatenate([block(first + c) for c in range(span // LANES)], axis=1)
                    terms = spread_rows(b_ref[:, at(start + i, span)], ranks, mask)
                    outs.append(near + two_term(d_ref[:, here] + c_ref[:, here], terms, NN))
                for i, out in enumerate(outs):
                    o_ref[:, at(start + i, span)] = out

            in_chunks(width // span, 32, lay)
        else:

            def lay(start, n):
                outs = [block(start + c) for c in range(n)]
                for c, out in enumerate(outs):
                    o_ref[:, at(start + c, LANES)] = out

            in_chunks(width // LANES, 64, lay)

    scratch = [
        pltpu.VMEM((held + 1, FEATS + (0 if narrow else 2 * rows), LANES), bf16),
        pltpu.VMEM((leaves, pts, FEATS), bf16),
        pltpu.VMEM((leaves, pts, 2 * rows) if narrow else (leaves, rows, LANES), f32),
    ]
    scratch += [
        pltpu.VMEM((pieces, 3, width), f32),
        pltpu.VMEM((pieces, rows, width), f32),
        pltpu.SemaphoreType.DMA((2 * pieces + len(finish),)),
    ]
    scratch += [pltpu.VMEM(x.shape, f32) for x in finish]
    if narrow:
        scratch.append(pltpu.VMEM((held + 1, pts, 2 * rows), bf16))
    args = [listing, *consts, *coords, *sources, *finish]
    return call(
        body,
        jax.ShapeDtypeStruct((rows, width), f32),
        len(consts),
        scratch,
        nbytes=15 * 10**7,
        prefetch=True,
        n_any=2 * pieces + len(finish),
    )(*args)


def local(rhs, points, basis, transfer, leaf_proxies, root_proxies, near_src, near_count, far_src):
    highest = lax.Precision.HIGHEST
    rows, width = rhs.shape
    leaves = near_src.shape[0]
    leaf_pts = width // leaves
    rank = basis.shape[0]
    near_max = near_src.shape[1]
    owner = lax.axis_index("leaf")
    size = lax.axis_size("leaf")
    up = [(i, (i + 1) % size) for i in range(size - 1)]
    down_pairs = [(j, i) for i, j in up]
    both_ways = lambda x: (lax.ppermute(x, "leaf", up), lax.ppermute(x, "leaf", down_pairs))

    coords = jnp.concatenate([points, leaf_proxies], axis=1)
    halo_coords = both_ways(coords)
    coef = leaf_coefs(rhs, basis, leaf_pts)

    anchor = (owner - 1) * leaves
    live = jnp.arange(near_max, dtype=i32)[None, :] < near_count[:, None]
    near_list = work_list(near_src - anchor, live, WIDE * LANES // leaf_pts, 3 * leaves)
    far_list = full_list(far_src - anchor, WIDE * LANES // rank)

    root = tree_up(coef, transfer, leaves)
    halo_coords, root = lax.optimization_barrier((halo_coords, root))
    halo_coef = both_ways(coef)
    parts, origins = [], []
    for s in range(2, size):
        rise, fall = [(i, i + s) for i in range(size - s)], [(i + s, i) for i in range(size - s)]
        if 2 * s >= size:
            parts.append(lax.ppermute(root, "leaf", rise + fall))
            origins.append(jnp.where(owner >= s, owner - s, owner + s))
        else:
            parts += [lax.ppermute(root, "leaf", rise), lax.ppermute(root, "leaf", fall)]
            origins += [owner - s, owner + s]

    halo_coords, sent = lax.optimization_barrier((halo_coords, rhs))
    halo_rhs = both_ways(sent)
    coords = [halo_coords[0], coords, halo_coords[1]]
    couple = pair_sums(
        *far_list, coords, width, [halo_coef[0], coef, halo_coef[1]], leaves, rank
    )
    parts, couple = lax.optimization_barrier((parts, couple))
    own_proxy = lax.dynamic_slice_in_dim(root_proxies, owner * rank, rank, 1)
    top = jnp.zeros((rows, rank), f32)
    for part, origin in zip(parts, origins):
        there = (origin >= 0) & (origin < size)
        start = jnp.clip(origin, 0, size - 1) * rank
        proxy = lax.dynamic_slice_in_dim(root_proxies, start, rank, 1)
        dist = jnp.sum((own_proxy[:, :, None] - proxy[:, None, :]) ** 2, axis=0)
        kernel = jnp.where(there, jnp.exp(-dist / spread_sq), 0.0)
        top = top + jnp.einsum("aj,rj->ra", kernel, part, precision=highest)
    down = tree_down(top, transfer, leaves)
    halo_rhs, down = lax.optimization_barrier((halo_rhs, down))
    return pair_sums(
        *near_list,
        coords,
        0,
        [halo_rhs[0], rhs, halo_rhs[1]],
        leaves,
        leaf_pts,
        (down, couple, basis),
    )


def solution(mesh):
    in_specs = (
        P(("level", "sub"), ("groups", "leaf")),
        P(None, ("groups", "leaf")),
        P(None, ("groups", "leaf")),
        P(None, ("groups", "leaf")),
        P(None, ("groups", "leaf")),
        P(None, "groups"),
        P(("groups", "leaf"), None),
        P(("groups", "leaf")),
        P(("groups", "leaf"), None),
    )
    out_specs = P(("level", "sub"), ("groups", "leaf"))
    return jax.shard_map(local, mesh=mesh, in_specs=in_specs, out_specs=out_specs, check_vma=False)
```

```python
import functools
import math

import jax
import jax.numpy as jnp
import numpy as np
from jax import lax
from jax.experimental import pallas as pl
from jax.experimental.pallas import tpu as pltpu
from jax.sharding import PartitionSpec as P

spread_sq = 0.5
LANES = 128
FEATS = 16
UNROLL = 64
WIDE = 2
STEPS = 4
VMEM_LIMIT = 58 * 1024 * 1024
f32, bf16, i32 = jnp.float32, jnp.bfloat16, jnp.int32

NN = (((1,), (0,)), ((), ()))
NT = (((1,), (1,)), ((), ()))


def dot(a, b, dims=NN):
    return lax.dot_general(a, b, dims, preferred_element_type=f32)


def halves(x):
    hi = x.astype(bf16).astype(f32)
    return hi, x - hi


def stacked(x):
    hi, lo = halves(x)
    return jnp.concatenate([hi, lo], axis=0).astype(bf16)


def two_term(x, terms, dims):
    rows = x.shape[0]
    xs = stacked(x)
    high = dot(xs, terms[0], dims)
    low = dot(xs, terms[1], dims)
    return (high[:rows] + high[rows:]) + (low[:rows] + low[rows:])


def in_chunks(count, most, run):
    size = min(count, most)
    if count == size:
        run(0, size)
    else:

        def step(i, carry):
            run(i * size, size)
            return carry

        lax.fori_loop(0, count // size, step, 0)


def at(i, size):
    first = i * size
    return pl.ds(first if isinstance(first, int) else pl.multiple_of(first, size), size)


def span_of(first, n):
    start = first * LANES
    return pl.ds(start if isinstance(start, int) else pl.multiple_of(start, LANES), n * LANES)


def group_mask(shape, row_width, col_width):
    row = lax.broadcasted_iota(i32, shape, 0) // row_width
    col = lax.broadcasted_iota(i32, shape, 1) // col_width
    return row == col


def spread_rows(mat, copies, mask):
    zero = jnp.zeros((), bf16)
    parts = [part.astype(bf16) for part in halves(mat)]
    return [jnp.where(mask, jnp.concatenate([part] * copies, axis=0), zero) for part in parts]


def whole(n):
    return [pl.BlockSpec(memory_space=pltpu.VMEM)] * n


def call_blocks(body, out_shape, widths, rows, steps, nbytes):
    block = lambda r, w: pl.BlockSpec((r, w // steps), lambda i: (0, i))
    return pl.pallas_call(
        body,
        out_shape=out_shape,
        grid=(steps,),
        in_specs=[block(r, w) for r, w in zip(rows, widths)],
        out_specs=block(*out_shape.shape),
        compiler_params=pltpu.CompilerParams(vmem_limit_bytes=VMEM_LIMIT),
        cost_estimate=pl.CostEstimate(flops=0, bytes_accessed=nbytes, transcendentals=0),
    )


def call(body, out_shape, n_in, scratch=(), nbytes=0, prefetch=False, n_any=0):
    specs = ([pl.BlockSpec(memory_space=pltpu.SMEM)] if prefetch else []) + whole(n_in)
    specs += [pl.BlockSpec(memory_space=pl.ANY)] * n_any
    return pl.pallas_call(
        body,
        out_shape=out_shape,
        in_specs=specs,
        out_specs=pl.BlockSpec(memory_space=pltpu.VMEM),
        scratch_shapes=list(scratch),
        compiler_params=pltpu.CompilerParams(vmem_limit_bytes=VMEM_LIMIT),
        cost_estimate=pl.CostEstimate(flops=0, bytes_accessed=nbytes, transcendentals=0),
    )


def leaf_coefs(rhs, basis, leaf_pts):
    rows, width = rhs.shape
    rank = basis.shape[0]
    per = LANES // rank
    span = per * leaf_pts

    def body(x_ref, b_ref, o_ref):
        mask = group_mask((per * rank, span), rank, leaf_pts)

        def run(first, n):
            ids = [first + j for j in range(n)]
            ins = [(x_ref[:, at(i, span)], b_ref[:, at(i, span)]) for i in ids]
            outs = [two_term(x, spread_rows(m, per, mask), NT) for x, m in ins]
            for i, out in zip(ids, outs):
                o_ref[:, at(i, LANES)] = out

        in_chunks(width // span // STEPS, 32, run)

    out = jax.ShapeDtypeStruct((rows, width // leaf_pts * rank), f32)
    return call_blocks(body, out, (width, width), (rows, rank), STEPS, 4 * 10**7)(rhs, basis)


def tree_up(coef, transfer, leaves):
    rows, width = coef.shape
    rank = transfer.shape[0]
    levels = leaves.bit_length() - 1

    def body(c_ref, e_ref, o_ref, buf):
        for level in range(levels):
            here = leaves >> level
            offset = (2 * leaves - 2 * here) * rank
            share = 1 if level == 0 else 2
            out_span = min(LANES, here * rank)
            groups = out_span // rank * share
            span = groups * rank
            mask = group_mask((span, out_span), share * rank, rank)
            src = c_ref if level == 0 else buf.at[(level - 1) % 2]
            dst = buf.at[level % 2]

            def run(first, n):
                ids = [first + j for j in range(n)]
                base = offset // out_span
                ins = [(src[:, at(i, span)], e_ref[:, at(base + i, out_span)]) for i in ids]
                outs = [two_term(x, spread_rows(m, groups, mask), NN) for x, m in ins]
                for i, out in zip(ids, outs):
                    dst[:, at(i, out_span)] = out

            in_chunks(here * rank // out_span, 32, run)
        last = buf[(levels - 1) % 2, :, : 2 * rank]
        o_ref[...] = last[:, :rank] + last[:, rank:]

    return call(
        body,
        jax.ShapeDtypeStruct((rows, rank), f32),
        2,
        [pltpu.VMEM((2, rows, width), f32)],
        nbytes=4 * 10**7,
    )(coef, transfer)


def tree_down(root, transfer, leaves):
    rows = root.shape[0]
    rank = transfer.shape[0]
    levels = leaves.bit_length() - 1
    width = leaves * rank

    def body(r_ref, e_ref, o_ref, buf):
        top = r_ref[...]
        buf[levels % 2, :, : 2 * rank] = jnp.concatenate([top, top], axis=1)
        for level in reversed(range(levels)):
            here = leaves >> level
            offset = (2 * leaves - 2 * here) * rank
            share = 1 if level == 0 else 2
            in_span = min(LANES, here * rank)
            groups = in_span // rank * share
            span = groups * rank
            mask = group_mask((span, in_span), share * rank, rank)
            src = buf.at[(level + 1) % 2]
            dst = o_ref if level == 0 else buf.at[level % 2]

            def run(first, n):
                ids = [first + j for j in range(n)]
                base = offset // in_span
                ins = [(src[:, at(i, in_span)], e_ref[:, at(base + i, in_span)]) for i in ids]
                outs = [two_term(x, spread_rows(m, groups, mask), NT) for x, m in ins]
                for i, out in zip(ids, outs):
                    dst[:, at(i, span)] = out

            in_chunks(here * rank // in_span, 32, run)

    return call(
        body,
        jax.ShapeDtypeStruct((rows, width), f32),
        2,
        [pltpu.VMEM((2, rows, width), f32)],
        nbytes=4 * 10**7,
    )(root, transfer)


def full_list(idx, group):
    count, listed = idx.shape
    per = listed // group
    items = count * per
    target = jnp.arange(items, dtype=i32) // per
    sources = idx.reshape(items, group).T.reshape(-1)
    return jnp.concatenate([target, sources, jnp.full((1,), items // UNROLL, i32)]), items


LOG2E = math.log2(math.e)


def selections():
    source, target = np.zeros((FEATS, FEATS), np.float32), np.zeros((FEATS, FEATS), np.float32)
    for d in range(3):
        for row, (p, q) in enumerate(((0, 0), (0, 1), (1, 0), (1, 1))):
            target[3 * row + d, 8 * p + d] = 1.0
            source[3 * row + d, 8 * q + d] = 1.0
    for row, term in ((12, 3), (13, 11)):
        source[row, term] = 1.0
        target[row, 4] = 1.0
        target[row + 2, term] = 1.0
        source[row + 2, 4] = 1.0
    return source, target


def features(coords, selection, scale):
    c = jnp.concatenate([coords - 1.0, jnp.zeros((5, coords.shape[1]), f32)], axis=0)
    row = lax.broadcasted_iota(i32, c.shape, 0)
    square = (-LOG2E / spread_sq) * jnp.sum(c * c, axis=0, keepdims=True)
    terms = jnp.where(row == 3, square, jnp.where(row == 4, 1.0, c * scale))
    return dot(selection, stacked(terms))


def work_list(idx, live, group, dummy):
    count, listed = idx.shape
    items = count * (listed // group)
    livei = live.astype(i32)
    rank = jnp.sum(
        livei[:, None, :] * (jnp.arange(listed)[None, None, :] < jnp.arange(listed)[None, :, None]),
        axis=2,
    )
    slot = jnp.arange(listed, dtype=i32)
    hit = live[:, :, None] & (rank[:, :, None] == slot[None, None, :])
    total = jnp.sum(livei, axis=1)
    packed = jnp.sum(jnp.where(hit, idx[:, :, None], 0), axis=1)
    packed = jnp.where(slot[None, :] < total[:, None], packed, dummy)
    half = group // 2
    rest = total % group
    need = total // group + (rest > half).astype(i32)
    upto = jnp.arange(count)
    start = jnp.sum(jnp.where(upto[None, :] < upto[:, None], need[None, :], 0), axis=1)
    end = start + need
    k = jnp.arange(items, dtype=i32)
    one_hot = (start[None, :] <= k[:, None]) & (k[:, None] < end[None, :])
    target = jnp.sum(jnp.where(one_hot, upto[None, :].astype(i32), 0), axis=1)
    within = jnp.sum(jnp.where(one_hot, k[:, None] - start[None, :], 0), axis=1)
    rows = jnp.einsum(
        "kt,tm->km", one_hot.astype(f32), packed.astype(f32), precision=lax.Precision.HIGHEST
    )
    rows = jnp.round(rows).astype(i32).reshape(items, listed // group, group)
    pick = within[:, None, None] == jnp.arange(listed // group)[None, :, None]
    sources = jnp.sum(jnp.where(pick, rows, 0), axis=1)
    used = jnp.sum(need)
    sources = jnp.where((k < used)[:, None], sources, dummy)
    steps = (used + UNROLL - 1) // UNROLL
    short = ((rest > 0) & (rest <= half)).astype(i32)
    ahead = jnp.sum(jnp.where(upto[None, :] < upto[:, None], short[None, :], 0), axis=1)
    k = jnp.arange(count, dtype=i32)[:, None]
    chosen = (short[None, :] > 0) & (ahead[None, :] == k)
    parts = [jnp.sum(jnp.where(chosen, upto[None, :].astype(i32), 0), axis=1)]
    for g in range(half):
        mine = jnp.sum(jnp.where(slot[None, :] == group * need[:, None] + g, packed, 0), axis=1)
        source = jnp.sum(jnp.where(chosen, mine[None, :], 0), axis=1)
        parts.append(jnp.where(k[:, 0] < jnp.sum(short), source, dummy))
    short_steps = (jnp.sum(short) + UNROLL - 1) // UNROLL
    listing = [target, sources.T.reshape(-1), steps[None], *parts, short_steps[None]]
    return jnp.concatenate(listing), items


def pair_sums(listing, items, coords, offset, sources, leaves, pts, finish=()):
    rows = sources[0].shape[0]
    width = leaves * pts
    per = LANES // pts
    pieces = len(sources)
    held = pieces * leaves
    group = WIDE * per
    narrow = per > 2
    pick_source, pick_target = selections()
    eye = np.eye(LANES, dtype=np.float32)
    consts = [jnp.asarray(m, bf16) for m in (pick_source, pick_target, eye)]

    def body(list_ref, pick_s_ref, pick_t_ref, eye_ref, *refs):
        last = refs[2 * pieces : 2 * pieces + len(finish)]
        more = refs[2 * pieces + len(finish) :]
        o_ref, tab, targets_tab, acc, coord_refs, x_refs, sems = more[:7]
        flat, bufs = more[-1], more[7:]
        own = pieces // 2
        order = [own] + [p for p in range(pieces) if p != own]
        copies = {}
        for p in order:
            copies[p] = [
                pltpu.make_async_copy(
                    refs[p].at[:, pl.ds(offset, width)], coord_refs.at[p], sems.at[2 * p]
                ),
                pltpu.make_async_copy(refs[pieces + p], x_refs.at[p], sems.at[2 * p + 1]),
            ]
            for copy in copies[p]:
                copy.start()
        lane = lax.broadcasted_iota(i32, (1, LANES), 1) // pts

        late = [
            pltpu.make_async_copy(ref, buf, sems.at[2 * pieces + j])
            for j, (ref, buf) in enumerate(zip(last, bufs))
        ]
        for copy in late:
            copy.start()
        copies[own][0].wait()

        def fill_targets(first, n):
            here = span_of(first, n)
            feats = features(coord_refs[own, :, here], pick_t_ref[...], 2.0 * LOG2E / spread_sq).astype(bf16)
            outs = [
                dot(eye_ref[...], feats[:, j * LANES : (j + 1) * LANES], NT).astype(bf16)
                for j in range(n)
            ]
            for j, out in enumerate(outs):
                for g in range(per):
                    targets_tab[(first + j) * per + g] = out[g * pts : (g + 1) * pts]

        in_chunks(width // LANES, 32, fill_targets)

        def repeated(rec):
            turned = [rec] + [pltpu.roll(rec, pts * j, 1) for j in range(1, per)]
            outs = []
            for j in range(per):
                out = turned[(per - j) % per]
                for g in range(1, per):
                    out = jnp.where(lane == g, turned[(g - j) % per], out)
                outs.append(out.astype(bf16))
            return outs

        def fill_narrow(piece, first, n, feats):
            outs, upright = [], []
            for c in range(n):
                outs += repeated(feats[:, c * LANES : (c + 1) * LANES])
                x = stacked(x_refs[piece, :, at(first + c, LANES)])
                upright.append(dot(eye_ref[...], x, NT).astype(bf16))
            for j, out in enumerate(outs):
                tab[piece * leaves + first * per + j] = out
            for c, out in enumerate(upright):
                for j in range(per):
                    flat[piece * leaves + (first + c) * per + j] = out[j * pts : (j + 1) * pts]

        for piece in order:
            for copy in copies[piece][1 if piece == own else 0 :]:
                copy.wait()

            def fill(first, n):
                here = span_of(first, n)
                feats = features(coord_refs[piece, :, here], pick_s_ref[...], 1.0)
                if narrow:
                    fill_narrow(piece, first, n, feats)
                    return
                hi, lo = halves(x_refs[piece, :, here])
                whole_rec = jnp.concatenate([feats, hi, lo], axis=0)
                outs = []
                for c in range(n):
                    outs += repeated(whole_rec[:, c * LANES : (c + 1) * LANES])
                for j, out in enumerate(outs):
                    tab[piece * leaves + first * per + j] = out

            in_chunks(width // LANES, 64, fill)
        tab[held] = jnp.zeros(tab.shape[1:], bf16)
        if narrow:
            flat[held] = jnp.zeros(flat.shape[1:], bf16)

        def clear(first, n):
            for j in range(n):
                acc[first + j] = jnp.zeros(acc.shape[1:], f32)

        in_chunks(leaves, 32, clear)

        masks = [
            lax.broadcasted_iota(i32, (tab.shape[1], LANES), 1) >= g * pts
            for g in range(1, per)
        ]

        def step(n, carry, wide, base, items):
            ks = [base + n * UNROLL + u for u in range(UNROLL)]
            targets = [list_ref[k] for k in ks]
            recs, values = [], []
            for k in ks:
                picks = [list_ref[(g + 1) * items + k] for g in range(wide * per)]
                blocks = []
                for w in range(wide):
                    rec = tab[picks[w * per]]
                    for g in range(1, per):
                        rec = jnp.where(masks[g - 1], tab[picks[w * per + g]], rec)
                    blocks.append(rec)
                recs.append(blocks[0] if wide == 1 else jnp.concatenate(blocks, axis=1))
                if narrow:
                    values.append(jnp.concatenate([flat[pick] for pick in picks], axis=0))
                else:
                    values.append(recs[-1][FEATS:])
            logs = [dot(targets_tab[t], rec[:FEATS]) for t, rec in zip(targets, recs)]
            kernels = [jnp.exp2(e) for e in logs]
            his = [k.astype(bf16) for k in kernels]
            los = [(k - h.astype(f32)).astype(bf16) for k, h in zip(kernels, his)]
            outs = []
            for value, hi, lo in zip(values, his, los):
                both = jnp.concatenate([hi, lo], axis=0)
                if narrow:
                    out = dot(both, value, NN)
                    outs.append(out[:pts] + out[pts:])
                else:
                    out = dot(value, both, NT)
                    outs.append(out[:rows] + out[rows:])
            for t, out in zip(targets, outs):
                acc[t] += out
            return carry

        ends = (group + 1) * items
        run = functools.partial(step, wide=WIDE, base=0, items=items)
        lax.fori_loop(0, list_ref[ends], run, 0)
        if not narrow:
            run = functools.partial(step, wide=WIDE // 2, base=ends + 1, items=leaves)
            lax.fori_loop(0, list_ref[ends + 1 + (group // 2 + 1) * leaves], run, 0)

        def block(i):
            if narrow:
                out = jnp.concatenate([acc[i * per + j] for j in range(per)], axis=0).T
                return out[:rows] + out[rows:]
            for j in range(per):
                one = acc[i * per + j]
                one = one + pltpu.roll(one, pts, 1)
                out = one if j == 0 else jnp.where(lane == j, one, out)
            return out

        if finish:
            for copy in late:
                copy.wait()
            d_ref, c_ref, b_ref = bufs[:3]
            rank = finish[2].shape[0]
            ranks = LANES // rank
            span = ranks * pts
            mask = group_mask((LANES, span), rank, pts)

            def lay(start, n):
                outs = []
                for i in range(n):
                    here = at(start + i, LANES)
                    first = (start + i) * (span // LANES)
                    near = jnp.concatenate([block(first + c) for c in range(span // LANES)], axis=1)
                    terms = spread_rows(b_ref[:, at(start + i, span)], ranks, mask)
                    outs.append(near + two_term(d_ref[:, here] + c_ref[:, here], terms, NN))
                for i, out in enumerate(outs):
                    o_ref[:, at(start + i, span)] = out

            in_chunks(width // span, 32, lay)
        else:

            def lay(start, n):
                outs = [block(start + c) for c in range(n)]
                for c, out in enumerate(outs):
                    o_ref[:, at(start + c, LANES)] = out

            in_chunks(width // LANES, 64, lay)

    scratch = [
        pltpu.VMEM((held + 1, FEATS + (0 if narrow else 2 * rows), LANES), bf16),
        pltpu.VMEM((leaves, pts, FEATS), bf16),
        pltpu.VMEM((leaves, pts, 2 * rows) if narrow else (leaves, rows, LANES), f32),
    ]
    scratch += [
        pltpu.VMEM((pieces, 3, width), f32),
        pltpu.VMEM((pieces, rows, width), f32),
        pltpu.SemaphoreType.DMA((2 * pieces + len(finish),)),
    ]
    scratch += [pltpu.VMEM(x.shape, f32) for x in finish]
    if narrow:
        scratch.append(pltpu.VMEM((held + 1, pts, 2 * rows), bf16))
    args = [listing, *consts, *coords, *sources, *finish]
    return call(
        body,
        jax.ShapeDtypeStruct((rows, width), f32),
        len(consts),
        scratch,
        nbytes=15 * 10**7,
        prefetch=True,
        n_any=2 * pieces + len(finish),
    )(*args)


def local(rhs, points, basis, transfer, leaf_proxies, root_proxies, near_src, near_count, far_src):
    highest = lax.Precision.HIGHEST
    rows, width = rhs.shape
    leaves = near_src.shape[0]
    leaf_pts = width // leaves
    rank = basis.shape[0]
    near_max = near_src.shape[1]
    owner = lax.axis_index("leaf")
    size = lax.axis_size("leaf")
    up = [(i, (i + 1) % size) for i in range(size - 1)]
    down_pairs = [(j, i) for i, j in up]
    both_ways = lambda x: (lax.ppermute(x, "leaf", up), lax.ppermute(x, "leaf", down_pairs))

    coords = jnp.concatenate([points, leaf_proxies], axis=1)
    halo_coords = both_ways(coords)
    coef = leaf_coefs(rhs, basis, leaf_pts)

    anchor = (owner - 1) * leaves
    live = jnp.arange(near_max, dtype=i32)[None, :] < near_count[:, None]
    near_list = work_list(near_src - anchor, live, WIDE * LANES // leaf_pts, 3 * leaves)
    far_list = full_list(far_src - anchor, WIDE * LANES // rank)

    root = tree_up(coef, transfer, leaves)
    halo_coords, root = lax.optimization_barrier((halo_coords, root))
    halo_coef = both_ways(coef)
    parts, origins = [], []
    for s in range(2, size):
        rise, fall = [(i, i + s) for i in range(size - s)], [(i + s, i) for i in range(size - s)]
        if 2 * s >= size:
            parts.append(lax.ppermute(root, "leaf", rise + fall))
            origins.append(jnp.where(owner >= s, owner - s, owner + s))
        else:
            parts += [lax.ppermute(root, "leaf", rise), lax.ppermute(root, "leaf", fall)]
            origins += [owner - s, owner + s]

    halo_coords, sent = lax.optimization_barrier((halo_coords, rhs))
    halo_rhs = both_ways(sent)
    coords = [halo_coords[0], coords, halo_coords[1]]
    couple = pair_sums(
        *far_list, coords, width, [halo_coef[0], coef, halo_coef[1]], leaves, rank
    )
    parts, couple = lax.optimization_barrier((parts, couple))
    own_proxy = lax.dynamic_slice_in_dim(root_proxies, owner * rank, rank, 1)
    top = jnp.zeros((rows, rank), f32)
    for part, origin in zip(parts, origins):
        there = (origin >= 0) & (origin < size)
        start = jnp.clip(origin, 0, size - 1) * rank
        proxy = lax.dynamic_slice_in_dim(root_proxies, start, rank, 1)
        dist = jnp.sum((own_proxy[:, :, None] - proxy[:, None, :]) ** 2, axis=0)
        kernel = jnp.where(there, jnp.exp(-dist / spread_sq), 0.0)
        top = top + jnp.einsum("aj,rj->ra", kernel, part, precision=highest)
    down = tree_down(top, transfer, leaves)
    halo_rhs, down = lax.optimization_barrier((halo_rhs, down))
    return pair_sums(
        *near_list,
        coords,
        0,
        [halo_rhs[0], rhs, halo_rhs[1]],
        leaves,
        leaf_pts,
        (down, couple, basis),
    )


def solution(mesh):
    in_specs = (
        P(("level", "sub"), ("groups", "leaf")),
        P(None, ("groups", "leaf")),
        P(None, ("groups", "leaf")),
        P(None, ("groups", "leaf")),
        P(None, ("groups", "leaf")),
        P(None, "groups"),
        P(("groups", "leaf"), None),
        P(("groups", "leaf")),
        P(("groups", "leaf"), None),
    )
    out_specs = P(("level", "sub"), ("groups", "leaf"))
    return jax.shard_map(local, mesh=mesh, in_specs=in_specs, out_specs=out_specs, check_vma=False)
```

```python
import functools
import math

import jax
import jax.numpy as jnp
import numpy as np
from jax import lax
from jax.experimental import pallas as pl
from jax.experimental.pallas import tpu as pltpu
from jax.sharding import PartitionSpec as P

spread_sq = 0.5
LANES = 128
FEATS = 16
UNROLL = 64
WIDE = 2
STEPS = 4
VMEM_LIMIT = 58 * 1024 * 1024
f32, bf16, i32 = jnp.float32, jnp.bfloat16, jnp.int32

NN = (((1,), (0,)), ((), ()))
NT = (((1,), (1,)), ((), ()))


def dot(a, b, dims=NN):
    return lax.dot_general(a, b, dims, preferred_element_type=f32)


def halves(x):
    hi = x.astype(bf16).astype(f32)
    return hi, x - hi


def stacked(x):
    hi, lo = halves(x)
    return jnp.concatenate([hi, lo], axis=0).astype(bf16)


def two_term(x, terms, dims):
    rows = x.shape[0]
    xs = stacked(x)
    high = dot(xs, terms[0], dims)
    low = dot(xs, terms[1], dims)
    return (high[:rows] + high[rows:]) + (low[:rows] + low[rows:])


def in_chunks(count, most, run):
    size = min(count, most)
    if count == size:
        run(0, size)
    else:

        def step(i, carry):
            run(i * size, size)
            return carry

        lax.fori_loop(0, count // size, step, 0)


def at(i, size):
    first = i * size
    return pl.ds(first if isinstance(first, int) else pl.multiple_of(first, size), size)


def span_of(first, n):
    start = first * LANES
    return pl.ds(start if isinstance(start, int) else pl.multiple_of(start, LANES), n * LANES)


def group_mask(shape, row_width, col_width):
    row = lax.broadcasted_iota(i32, shape, 0) // row_width
    col = lax.broadcasted_iota(i32, shape, 1) // col_width
    return row == col


def spread_rows(mat, copies, mask):
    zero = jnp.zeros((), bf16)
    parts = [part.astype(bf16) for part in halves(mat)]
    return [jnp.where(mask, jnp.concatenate([part] * copies, axis=0), zero) for part in parts]


def whole(n):
    return [pl.BlockSpec(memory_space=pltpu.VMEM)] * n


def call_blocks(body, out_shape, widths, rows, steps, nbytes):
    block = lambda r, w: pl.BlockSpec((r, w // steps), lambda i: (0, i))
    return pl.pallas_call(
        body,
        out_shape=out_shape,
        grid=(steps,),
        in_specs=[block(r, w) for r, w in zip(rows, widths)],
        out_specs=block(*out_shape.shape),
        compiler_params=pltpu.CompilerParams(vmem_limit_bytes=VMEM_LIMIT),
        cost_estimate=pl.CostEstimate(flops=0, bytes_accessed=nbytes, transcendentals=0),
    )


def call(body, out_shape, n_in, scratch=(), nbytes=0, prefetch=False, n_any=0):
    specs = ([pl.BlockSpec(memory_space=pltpu.SMEM)] if prefetch else []) + whole(n_in)
    specs += [pl.BlockSpec(memory_space=pl.ANY)] * n_any
    return pl.pallas_call(
        body,
        out_shape=out_shape,
        in_specs=specs,
        out_specs=pl.BlockSpec(memory_space=pltpu.VMEM),
        scratch_shapes=list(scratch),
        compiler_params=pltpu.CompilerParams(vmem_limit_bytes=VMEM_LIMIT),
        cost_estimate=pl.CostEstimate(flops=0, bytes_accessed=nbytes, transcendentals=0),
    )


def leaf_coefs(rhs, basis, leaf_pts):
    rows, width = rhs.shape
    rank = basis.shape[0]
    per = LANES // rank
    span = per * leaf_pts

    def body(x_ref, b_ref, o_ref):
        mask = group_mask((per * rank, span), rank, leaf_pts)

        def run(first, n):
            ids = [first + j for j in range(n)]
            ins = [(x_ref[:, at(i, span)], b_ref[:, at(i, span)]) for i in ids]
            outs = [two_term(x, spread_rows(m, per, mask), NT) for x, m in ins]
            for i, out in zip(ids, outs):
                o_ref[:, at(i, LANES)] = out

        in_chunks(width // span // STEPS, 32, run)

    out = jax.ShapeDtypeStruct((rows, width // leaf_pts * rank), f32)
    return call_blocks(body, out, (width, width), (rows, rank), STEPS, 4 * 10**7)(rhs, basis)


def matrix_copies(hbm, held, sems, first):
    spans = (pl.ds(0, first), pl.ds(first, hbm.shape[1] - first))
    copies = [
        pltpu.make_async_copy(hbm.at[:, span], held.at[:, span], sems.at[j])
        for j, span in enumerate(spans)
    ]
    return copies


def tree_up(coef, transfer, leaves):
    rows, width = coef.shape
    rank = transfer.shape[0]
    levels = leaves.bit_length() - 1

    def body(c_ref, hbm_ref, o_ref, buf, e_ref, sems):
        low, high = matrix_copies(hbm_ref, e_ref, sems, leaves * rank)
        low.start()
        high.start()
        low.wait()
        for level in range(levels):
            if level == 1:
                high.wait()
            here = leaves >> level
            offset = (2 * leaves - 2 * here) * rank
            share = 1 if level == 0 else 2
            out_span = min(LANES, here * rank)
            groups = out_span // rank * share
            span = groups * rank
            mask = group_mask((span, out_span), share * rank, rank)
            src = c_ref if level == 0 else buf.at[(level - 1) % 2]
            dst = buf.at[level % 2]

            def run(first, n):
                ids = [first + j for j in range(n)]
                base = offset // out_span
                ins = [(src[:, at(i, span)], e_ref[:, at(base + i, out_span)]) for i in ids]
                outs = [two_term(x, spread_rows(m, groups, mask), NN) for x, m in ins]
                for i, out in zip(ids, outs):
                    dst[:, at(i, out_span)] = out

            in_chunks(here * rank // out_span, 64, run)
        last = buf[(levels - 1) % 2, :, : 2 * rank]
        o_ref[...] = last[:, :rank] + last[:, rank:]

    return call(
        body,
        jax.ShapeDtypeStruct((rows, rank), f32),
        1,
        [
            pltpu.VMEM((2, rows, width), f32),
            pltpu.VMEM(transfer.shape, f32),
            pltpu.SemaphoreType.DMA((2,)),
        ],
        nbytes=4 * 10**7,
        n_any=1,
    )(coef, transfer)


def tree_down(root, transfer, leaves):
    rows = root.shape[0]
    rank = transfer.shape[0]
    levels = leaves.bit_length() - 1
    width = leaves * rank

    def body(r_ref, hbm_ref, o_ref, buf, e_ref, sems):
        low, high = matrix_copies(hbm_ref, e_ref, sems, leaves * rank)
        high.start()
        low.start()
        high.wait()
        top = r_ref[...]
        buf[levels % 2, :, : 2 * rank] = jnp.concatenate([top, top], axis=1)
        for level in reversed(range(levels)):
            if level == 0:
                low.wait()
            here = leaves >> level
            offset = (2 * leaves - 2 * here) * rank
            share = 1 if level == 0 else 2
            in_span = min(LANES, here * rank)
            groups = in_span // rank * share
            span = groups * rank
            mask = group_mask((span, in_span), share * rank, rank)
            src = buf.at[(level + 1) % 2]
            dst = o_ref if level == 0 else buf.at[level % 2]

            def run(first, n):
                ids = [first + j for j in range(n)]
                base = offset // in_span
                ins = [(src[:, at(i, in_span)], e_ref[:, at(base + i, in_span)]) for i in ids]
                outs = [two_term(x, spread_rows(m, groups, mask), NT) for x, m in ins]
                for i, out in zip(ids, outs):
                    dst[:, at(i, span)] = out

            in_chunks(here * rank // in_span, 32, run)

    return call(
        body,
        jax.ShapeDtypeStruct((rows, width), f32),
        1,
        [
            pltpu.VMEM((2, rows, width), f32),
            pltpu.VMEM(transfer.shape, f32),
            pltpu.SemaphoreType.DMA((2,)),
        ],
        nbytes=4 * 10**7,
        n_any=1,
    )(root, transfer)


def full_list(idx, group):
    count, listed = idx.shape
    per = listed // group
    items = count * per
    target = jnp.arange(items, dtype=i32) // per
    sources = idx.reshape(items, group).T.reshape(-1)
    return jnp.concatenate([target, sources, jnp.full((1,), items // UNROLL, i32)]), items


LOG2E = math.log2(math.e)


def selections():
    source, target = np.zeros((FEATS, FEATS), np.float32), np.zeros((FEATS, FEATS), np.float32)
    for d in range(3):
        for row, (p, q) in enumerate(((0, 0), (0, 1), (1, 0), (1, 1))):
            target[3 * row + d, 8 * p + d] = 1.0
            source[3 * row + d, 8 * q + d] = 1.0
    for row, term in ((12, 3), (13, 11)):
        source[row, term] = 1.0
        target[row, 4] = 1.0
        target[row + 2, term] = 1.0
        source[row + 2, 4] = 1.0
    return source, target


def features(coords, selection, scale):
    c = jnp.concatenate([coords - 1.0, jnp.zeros((5, coords.shape[1]), f32)], axis=0)
    row = lax.broadcasted_iota(i32, c.shape, 0)
    square = (-LOG2E / spread_sq) * jnp.sum(c * c, axis=0, keepdims=True)
    terms = jnp.where(row == 3, square, jnp.where(row == 4, 1.0, c * scale))
    return dot(selection, stacked(terms))


def work_list(idx, live, group, dummy):
    count, listed = idx.shape
    items = count * (listed // group)
    livei = live.astype(i32)
    rank = jnp.sum(
        livei[:, None, :] * (jnp.arange(listed)[None, None, :] < jnp.arange(listed)[None, :, None]),
        axis=2,
    )
    slot = jnp.arange(listed, dtype=i32)
    hit = live[:, :, None] & (rank[:, :, None] == slot[None, None, :])
    total = jnp.sum(livei, axis=1)
    packed = jnp.sum(jnp.where(hit, idx[:, :, None], 0), axis=1)
    packed = jnp.where(slot[None, :] < total[:, None], packed, dummy)
    half = group // 2
    rest = total % group
    need = total // group + (rest > half).astype(i32)
    upto = jnp.arange(count)
    start = jnp.sum(jnp.where(upto[None, :] < upto[:, None], need[None, :], 0), axis=1)
    end = start + need
    k = jnp.arange(items, dtype=i32)
    one_hot = (start[None, :] <= k[:, None]) & (k[:, None] < end[None, :])
    target = jnp.sum(jnp.where(one_hot, upto[None, :].astype(i32), 0), axis=1)
    within = jnp.sum(jnp.where(one_hot, k[:, None] - start[None, :], 0), axis=1)
    rows = jnp.einsum(
        "kt,tm->km", one_hot.astype(f32), packed.astype(f32), precision=lax.Precision.HIGHEST
    )
    rows = jnp.round(rows).astype(i32).reshape(items, listed // group, group)
    pick = within[:, None, None] == jnp.arange(listed // group)[None, :, None]
    sources = jnp.sum(jnp.where(pick, rows, 0), axis=1)
    used = jnp.sum(need)
    sources = jnp.where((k < used)[:, None], sources, dummy)
    steps = (used + UNROLL - 1) // UNROLL
    short = ((rest > 0) & (rest <= half)).astype(i32)
    ahead = jnp.sum(jnp.where(upto[None, :] < upto[:, None], short[None, :], 0), axis=1)
    k = jnp.arange(count, dtype=i32)[:, None]
    chosen = (short[None, :] > 0) & (ahead[None, :] == k)
    parts = [jnp.sum(jnp.where(chosen, upto[None, :].astype(i32), 0), axis=1)]
    for g in range(half):
        mine = jnp.sum(jnp.where(slot[None, :] == group * need[:, None] + g, packed, 0), axis=1)
        source = jnp.sum(jnp.where(chosen, mine[None, :], 0), axis=1)
        parts.append(jnp.where(k[:, 0] < jnp.sum(short), source, dummy))
    short_steps = (jnp.sum(short) + UNROLL - 1) // UNROLL
    listing = [target, sources.T.reshape(-1), steps[None], *parts, short_steps[None]]
    return jnp.concatenate(listing), items


def pair_sums(listing, items, coords, offset, sources, leaves, pts, finish=()):
    rows = sources[0].shape[0]
    width = leaves * pts
    per = LANES // pts
    pieces = len(sources)
    held = pieces * leaves
    group = WIDE * per
    narrow = per > 2
    pick_source, pick_target = selections()
    eye = np.eye(LANES, dtype=np.float32)
    consts = [jnp.asarray(m, bf16) for m in (pick_source, pick_target, eye)]

    def body(list_ref, pick_s_ref, pick_t_ref, eye_ref, *refs):
        last = refs[2 * pieces : 2 * pieces + len(finish)]
        more = refs[2 * pieces + len(finish) :]
        o_ref, tab, targets_tab, acc, coord_refs, x_refs, sems = more[:7]
        flat, bufs = more[-1], more[7:]
        own = pieces // 2
        order = [own] + [p for p in range(pieces) if p != own]
        copies = {}
        for p in order:
            copies[p] = [
                pltpu.make_async_copy(
                    refs[p].at[:, pl.ds(offset, width)], coord_refs.at[p], sems.at[2 * p]
                ),
                pltpu.make_async_copy(refs[pieces + p], x_refs.at[p], sems.at[2 * p + 1]),
            ]
            for copy in copies[p]:
                copy.start()
        lane = lax.broadcasted_iota(i32, (1, LANES), 1) // pts

        late = [
            pltpu.make_async_copy(ref, buf, sems.at[2 * pieces + j])
            for j, (ref, buf) in enumerate(zip(last, bufs))
        ]
        for copy in late:
            copy.start()
        copies[own][0].wait()

        def fill_targets(first, n):
            here = span_of(first, n)
            feats = features(coord_refs[own, :, here], pick_t_ref[...], 2.0 * LOG2E / spread_sq).astype(bf16)
            outs = [
                dot(eye_ref[...], feats[:, j * LANES : (j + 1) * LANES], NT).astype(bf16)
                for j in range(n)
            ]
            for j, out in enumerate(outs):
                for g in range(per):
                    targets_tab[(first + j) * per + g] = out[g * pts : (g + 1) * pts]

        in_chunks(width // LANES, 32, fill_targets)

        def repeated(rec):
            turned = [rec] + [pltpu.roll(rec, pts * j, 1) for j in range(1, per)]
            outs = []
            for j in range(per):
                out = turned[(per - j) % per]
                for g in range(1, per):
                    out = jnp.where(lane == g, turned[(g - j) % per], out)
                outs.append(out.astype(bf16))
            return outs

        def fill_narrow(piece, first, n, feats):
            outs, upright = [], []
            for c in range(n):
                outs += repeated(feats[:, c * LANES : (c + 1) * LANES])
                x = stacked(x_refs[piece, :, at(first + c, LANES)])
                upright.append(dot(eye_ref[...], x, NT).astype(bf16))
            for j, out in enumerate(outs):
                tab[piece * leaves + first * per + j] = out
            for c, out in enumerate(upright):
                for j in range(per):
                    flat[piece * leaves + (first + c) * per + j] = out[j * pts : (j + 1) * pts]

        for piece in order:
            for copy in copies[piece][1 if piece == own else 0 :]:
                copy.wait()

            def fill(first, n):
                here = span_of(first, n)
                feats = features(coord_refs[piece, :, here], pick_s_ref[...], 1.0)
                if narrow:
                    fill_narrow(piece, first, n, feats)
                    return
                hi, lo = halves(x_refs[piece, :, here])
                whole_rec = jnp.concatenate([feats, hi, lo], axis=0)
                outs = []
                for c in range(n):
                    outs += repeated(whole_rec[:, c * LANES : (c + 1) * LANES])
                for j, out in enumerate(outs):
                    tab[piece * leaves + first * per + j] = out

            in_chunks(width // LANES, 64, fill)
        tab[held] = jnp.zeros(tab.shape[1:], bf16)
        if narrow:
            flat[held] = jnp.zeros(flat.shape[1:], bf16)

        def clear(first, n):
            for j in range(n):
                acc[first + j] = jnp.zeros(acc.shape[1:], f32)

        in_chunks(leaves, 32, clear)

        masks = [
            lax.broadcasted_iota(i32, (tab.shape[1], LANES), 1) >= g * pts
            for g in range(1, per)
        ]

        def step(n, carry, wide, base, items):
            ks = [base + n * UNROLL + u for u in range(UNROLL)]
            targets = [list_ref[k] for k in ks]
            recs, values = [], []
            for k in ks:
                picks = [list_ref[(g + 1) * items + k] for g in range(wide * per)]
                blocks = []
                for w in range(wide):
                    rec = tab[picks[w * per]]
                    for g in range(1, per):
                        rec = jnp.where(masks[g - 1], tab[picks[w * per + g]], rec)
                    blocks.append(rec)
                recs.append(blocks[0] if wide == 1 else jnp.concatenate(blocks, axis=1))
                if narrow:
                    values.append(jnp.concatenate([flat[pick] for pick in picks], axis=0))
                else:
                    values.append(recs[-1][FEATS:])
            logs = [dot(targets_tab[t], rec[:FEATS]) for t, rec in zip(targets, recs)]
            kernels = [jnp.exp2(e) for e in logs]
            his = [k.astype(bf16) for k in kernels]
            los = [(k - h.astype(f32)).astype(bf16) for k, h in zip(kernels, his)]
            outs = []
            for value, hi, lo in zip(values, his, los):
                both = jnp.concatenate([hi, lo], axis=0)
                if narrow:
                    out = dot(both, value, NN)
                    outs.append(out[:pts] + out[pts:])
                else:
                    out = dot(value, both, NT)
                    outs.append(out[:rows] + out[rows:])
            for t, out in zip(targets, outs):
                acc[t] += out
            return carry

        ends = (group + 1) * items
        run = functools.partial(step, wide=WIDE, base=0, items=items)
        lax.fori_loop(0, list_ref[ends], run, 0)
        if not narrow:
            run = functools.partial(step, wide=WIDE // 2, base=ends + 1, items=leaves)
            lax.fori_loop(0, list_ref[ends + 1 + (group // 2 + 1) * leaves], run, 0)

        def block(i):
            if narrow:
                out = jnp.concatenate([acc[i * per + j] for j in range(per)], axis=0).T
                return out[:rows] + out[rows:]
            for j in range(per):
                one = acc[i * per + j]
                one = one + pltpu.roll(one, pts, 1)
                out = one if j == 0 else jnp.where(lane == j, one, out)
            return out

        if finish:
            for copy in late:
                copy.wait()
            d_ref, c_ref, b_ref = bufs[:3]
            rank = finish[2].shape[0]
            ranks = LANES // rank
            span = ranks * pts
            mask = group_mask((LANES, span), rank, pts)

            def lay(start, n):
                outs = []
                for i in range(n):
                    here = at(start + i, LANES)
                    first = (start + i) * (span // LANES)
                    near = jnp.concatenate([block(first + c) for c in range(span // LANES)], axis=1)
                    terms = spread_rows(b_ref[:, at(start + i, span)], ranks, mask)
                    outs.append(near + two_term(d_ref[:, here] + c_ref[:, here], terms, NN))
                for i, out in enumerate(outs):
                    o_ref[:, at(start + i, span)] = out

            in_chunks(width // span, 32, lay)
        else:

            def lay(start, n):
                outs = [block(start + c) for c in range(n)]
                for c, out in enumerate(outs):
                    o_ref[:, at(start + c, LANES)] = out

            in_chunks(width // LANES, 64, lay)

    scratch = [
        pltpu.VMEM((held + 1, FEATS + (0 if narrow else 2 * rows), LANES), bf16),
        pltpu.VMEM((leaves, pts, FEATS), bf16),
        pltpu.VMEM((leaves, pts, 2 * rows) if narrow else (leaves, rows, LANES), f32),
    ]
    scratch += [
        pltpu.VMEM((pieces, 3, width), f32),
        pltpu.VMEM((pieces, rows, width), f32),
        pltpu.SemaphoreType.DMA((2 * pieces + len(finish),)),
    ]
    scratch += [pltpu.VMEM(x.shape, f32) for x in finish]
    if narrow:
        scratch.append(pltpu.VMEM((held + 1, pts, 2 * rows), bf16))
    args = [listing, *consts, *coords, *sources, *finish]
    return call(
        body,
        jax.ShapeDtypeStruct((rows, width), f32),
        len(consts),
        scratch,
        nbytes=15 * 10**7,
        prefetch=True,
        n_any=2 * pieces + len(finish),
    )(*args)


def local(rhs, points, basis, transfer, leaf_proxies, root_proxies, near_src, near_count, far_src):
    highest = lax.Precision.HIGHEST
    rows, width = rhs.shape
    leaves = near_src.shape[0]
    leaf_pts = width // leaves
    rank = basis.shape[0]
    near_max = near_src.shape[1]
    owner = lax.axis_index("leaf")
    size = lax.axis_size("leaf")
    up = [(i, (i + 1) % size) for i in range(size - 1)]
    down_pairs = [(j, i) for i, j in up]
    both_ways = lambda x: (lax.ppermute(x, "leaf", up), lax.ppermute(x, "leaf", down_pairs))

    coords = jnp.concatenate([points, leaf_proxies], axis=1)
    halo_coords = both_ways(coords)
    coef = leaf_coefs(rhs, basis, leaf_pts)

    anchor = (owner - 1) * leaves
    live = jnp.arange(near_max, dtype=i32)[None, :] < near_count[:, None]
    near_list = work_list(near_src - anchor, live, WIDE * LANES // leaf_pts, 3 * leaves)
    far_list = full_list(far_src - anchor, WIDE * LANES // rank)

    root = tree_up(coef, transfer, leaves)
    halo_coords, root = lax.optimization_barrier((halo_coords, root))
    halo_coef = both_ways(coef)
    parts, origins = [], []
    for s in range(2, size):
        rise, fall = [(i, i + s) for i in range(size - s)], [(i + s, i) for i in range(size - s)]
        if 2 * s >= size:
            parts.append(lax.ppermute(root, "leaf", rise + fall))
            origins.append(jnp.where(owner >= s, owner - s, owner + s))
        else:
            parts += [lax.ppermute(root, "leaf", rise), lax.ppermute(root, "leaf", fall)]
            origins += [owner - s, owner + s]

    halo_coords, sent = lax.optimization_barrier((halo_coords, rhs))
    halo_rhs = both_ways(sent)
    coords = [halo_coords[0], coords, halo_coords[1]]
    couple = pair_sums(
        *far_list, coords, width, [halo_coef[0], coef, halo_coef[1]], leaves, rank
    )
    parts, couple = lax.optimization_barrier((parts, couple))
    own_proxy = lax.dynamic_slice_in_dim(root_proxies, owner * rank, rank, 1)
    top = jnp.zeros((rows, rank), f32)
    for part, origin in zip(parts, origins):
        there = (origin >= 0) & (origin < size)
        start = jnp.clip(origin, 0, size - 1) * rank
        proxy = lax.dynamic_slice_in_dim(root_proxies, start, rank, 1)
        dist = jnp.sum((own_proxy[:, :, None] - proxy[:, None, :]) ** 2, axis=0)
        kernel = jnp.where(there, jnp.exp(-dist / spread_sq), 0.0)
        top = top + jnp.einsum("aj,rj->ra", kernel, part, precision=highest)
    down = tree_down(top, transfer, leaves)
    halo_rhs, down = lax.optimization_barrier((halo_rhs, down))
    return pair_sums(
        *near_list,
        coords,
        0,
        [halo_rhs[0], rhs, halo_rhs[1]],
        leaves,
        leaf_pts,
        (down, couple, basis),
    )


def solution(mesh):
    in_specs = (
        P(("level", "sub"), ("groups", "leaf")),
        P(None, ("groups", "leaf")),
        P(None, ("groups", "leaf")),
        P(None, ("groups", "leaf")),
        P(None, ("groups", "leaf")),
        P(None, "groups"),
        P(("groups", "leaf"), None),
        P(("groups", "leaf")),
        P(("groups", "leaf"), None),
    )
    out_specs = P(("level", "sub"), ("groups", "leaf"))
    return jax.shard_map(local, mesh=mesh, in_specs=in_specs, out_specs=out_specs, check_vma=False)
```
